32 devices in a mesh: dp: 2 (over core), expert: 16 (over z, y, x).
Axes of the slice: x: 2, y: 2, z: 4, core: 2. Of those that a mesh axis runs over, the one named last changes fastest.
Arguments:
- inputs: bfloat16 [32768, 512], P(('dp', 'expert')), may hold values from -6 to 6
- w_first: bfloat16 [16, 512, 256], P('expert'), may hold values from -0.25 to 0.25
- b_first: bfloat16 [16, 256], P('expert'), may hold values from -0.59765625 to 0.59765625
- w_second: bfloat16 [16, 256, 128], P('expert'), may hold values from -0.5 to 0.5
- b_second: bfloat16 [16, 128], P('expert'), may hold values from -0.59765625 to 0.59765625
- gate_weight: bfloat16 [2, 512, 16], replicated, may hold values from -0.125 to 0.125
- gate_bias: bfloat16 [2, 16], replicated, may hold values from -0.29882812 to 0.29882812
- tower_first_weight: bfloat16 [2, 128, 64], replicated, may hold values from -1 to 1
- tower_first_bias: bfloat16 [2, 64], replicated, may hold values from -0.59765625 to 0.59765625
- tower_last: bfloat16 [2, 64], replicated, may hold values from -1.5 to 1.5
- tower_out_bias: bfloat16 [2], replicated, may hold values from -2 to 2
- labels: int32 [2, 32768], P(None, ('dp', 'expert')), may hold values 0 or 1
- group_len: int32 [16], replicated, may hold values from 1 to 2048, as said below
- group_shard: int32 [16], replicated, may hold values from 0 to 1, as said below
Outputs:
- predictions: float32 [2, 32768], P(None, ('dp', 'expert'))
- input_grad: float32 [32768, 512], P(('dp', 'expert'))
- grad_w_first: float32 [16, 512, 256], P('expert')
- grad_b_first: float32 [16, 256], P('expert')
- grad_w_second: float32 [16, 256, 128], P('expert')
- grad_b_second: float32 [16, 128], P('expert')
- grad_gate: float32 [2, 512, 16], replicated
- grad_gate_bias: float32 [2, 16], replicated
- grad_tower_first: float32 [2, 128, 64], replicated
- grad_tower_bias: float32 [2, 64], replicated
- grad_tower_last: float32 [2, 64], replicated
- grad_tower_out_bias: float32 [2], replicated
The draws below stay inside these ranges and needn't reach their ends.
Inputs may be any that keep to these rules, and one draw needn't show every extreme that they name: `group_len`: the lengths of the groups of one batch shard sum to at most 16384, and in every draw some shard's groups fill exactly 16384 slots. `group_shard`: each shard number is taken by exactly 8 groups.
All inputs are finite; a program needn't handle non-finite values. No bound on the sum of `labels` on one device may be relied on, other than what follows from the above.
Results may differ from the reference program's by a relative error of at most 0.0083.
Values may be sent and summed in bfloat16 or wider, within the bound.
No kernel may reach another device: no remote copies, remote signals or barrier semaphores. Data moves between devices by JAX's collectives and lax.ppermute only.
A program may use at most 320 MiB of HBM per device.

```python
import jax
import jax.numpy as jnp
from jax import lax

D = 512
H1 = 256
H2 = 128
TH = 64
TASKS = 2
GRP_DP = 8
EXPERTS = 16
CAP = 16384
GROUPS = 16
ROWS = 32768
N_DP = 2


def deal_groups(key):
    longest = CAP // GRP_DP
    order = jax.random.permutation(jax.random.fold_in(key, 11), GROUPS)
    shard = (order % N_DP).astype(jnp.int32)
    limits = jax.random.randint(jax.random.fold_in(key, 12), (N_DP,), longest // 2, longest + 1)
    fullest = jax.random.randint(jax.random.fold_in(key, 13), (), 0, N_DP)
    limits = jnp.where(jnp.arange(N_DP) == fullest, longest, limits)
    limit_of = limits[shard]
    lowest = jnp.maximum(limit_of // 2, 1)
    raw = jax.random.randint(jax.random.fold_in(key, 14), (GROUPS,), 0, 1 << 20)
    sizes = lowest + raw % (limit_of - lowest + 1)
    sizes = jnp.where(shard == fullest, longest, sizes)
    return (sizes.astype(jnp.int32), shard)


def draw_group_len(key, part):
    return deal_groups(key)[0]


def draw_group_shard(key, part):
    return deal_groups(key)[1]


def place_ends(drawn, own_key, smallest, top_value):
    shape = drawn.shape
    spot = [jax.random.randint(jax.random.fold_in(own_key, axis), (), 0, shape[axis]) for axis in range(len(shape))]
    drawn = drawn.at[tuple(spot)].set(smallest)
    longest = shape.index(max(shape))
    spot[longest] = (spot[longest] + 1) % shape[longest]
    return drawn.at[tuple(spot)].set(top_value)


def shard_levels(rng, dims, pieces, low, largest):
    loudness, own = 1.0, jax.random.fold_in(rng, 6)
    for axis_at, blocks in pieces:
        heights = jnp.exp(jax.random.uniform(jax.random.fold_in(own, axis_at), (blocks,), jnp.float32, low / len(pieces), largest / len(pieces)))
        loudness = loudness * jnp.repeat(heights, dims[axis_at] // blocks).reshape([-1 if axis == axis_at else 1 for axis in range(len(dims))])
    return loudness


def noise(stream_key, extent, scale, limit, cuts=(), held_as=jnp.bfloat16):
    drawn = scale * jax.random.normal(stream_key, extent, jnp.float32)
    if cuts:
        drawn = drawn * shard_levels(stream_key, extent, cuts, -0.22, 0.18)
    return jnp.clip(drawn, -limit, limit).astype(held_as)


def setup_inputs(seed: int = 0) -> dict:
    arg_keys = jax.random.split(jax.random.key(seed), 15)
    inputs = noise(arg_keys[0], (ROWS, D), 1.0, 6.0, ((0, 32),))
    w_first = noise(arg_keys[1], (EXPERTS, D, H1), D ** -0.5, 0.25, ((0, 16),))
    b_first = noise(arg_keys[2], (EXPERTS, H1), 0.1, 0.59765625, ((0, 16),))
    w_second = noise(arg_keys[3], (EXPERTS, H1, H2), (H1 // 2) ** -0.5, 0.5, ((0, 16),))
    b_second = noise(arg_keys[4], (EXPERTS, H2), 0.1, 0.59765625, ((0, 16),))
    gate_weight = noise(arg_keys[5], (TASKS, D, EXPERTS), (4 * D) ** -0.5, 0.125)
    gate_bias = noise(arg_keys[6], (TASKS, EXPERTS), 0.05, 0.29882812)
    tower_first_weight = noise(arg_keys[7], (TASKS, H2, TH), (H2 // 4) ** -0.5, 1.0)
    tower_first_bias = noise(arg_keys[8], (TASKS, TH), 0.1, 0.59765625)
    tower_last = noise(arg_keys[9], (TASKS, TH), (TH // 4) ** -0.5, 1.5)
    tower_out_bias = noise(arg_keys[10], (TASKS,), 0.5, 2.0)
    labels = place_ends((jax.random.randint(arg_keys[11], (TASKS, ROWS), 0, 2) < 1).astype(jnp.int32), jax.random.fold_in(arg_keys[11], 1), 0, 1)
    group_len = draw_group_len(jax.random.fold_in(arg_keys[14], 71), 0)
    group_shard = draw_group_shard(jax.random.fold_in(arg_keys[14], 71), 0)
    return dict(inputs=inputs, w_first=w_first, b_first=b_first, w_second=w_second, b_second=b_second, gate_weight=gate_weight, gate_bias=gate_bias, tower_first_weight=tower_first_weight, tower_first_bias=tower_first_bias, tower_last=tower_last, tower_out_bias=tower_out_bias, labels=labels, group_len=group_len, group_shard=group_shard)


@jax.custom_vjp
def low_precision(v):
    return lax.optimization_barrier(v.astype(jnp.bfloat16)).astype(jnp.float32)

@jax.custom_vjp
def low_precision_backward(v):
    return v

def low_keep(v):
    return (low_precision(v), None)

def low_pass(kept, grad):
    return (grad,)

def back_keep(v):
    return (v, None)

def back_low(kept, grad):
    return (low_precision(grad),)
low_precision.defvjp(low_keep, low_pass)
low_precision_backward.defvjp(back_keep, back_low)

def row_weights(group_len, group_shard, shard, first, count):
    mine = group_shard == shard
    sizes = jnp.where(mine, group_len, 0).astype(jnp.int32)
    starts = (jnp.cumsum(sizes) - sizes).astype(jnp.int32)
    slots = (first + jnp.arange(count, dtype=jnp.int32))[:, None]
    inside = mine[None, :] & (slots >= starts[None, :]) & (slots < (starts + sizes)[None, :])
    recip = 1.0 / group_len.astype(jnp.float32)
    return lax.optimization_barrier(jnp.sum(jnp.where(inside, recip[None, :], jnp.float32(0.0)), axis=1))

def forward(inputs, w_first, b_first, w_second, b_second, gate_weight, gate_bias, tower_first_weight, tower_first_bias, tower_last, tower_out_bias, labels_f, weights):
    high_precision = lax.Precision.HIGHEST
    pre_one = low_precision_backward(jnp.einsum('rd,edh->erh', inputs, w_first, precision=high_precision) + b_first[:, None, :])
    hidden = low_precision(jax.nn.gelu(pre_one))
    pre_two = low_precision_backward(jnp.einsum('erh,ehf->erf', hidden, w_second, precision=high_precision) + b_second[:, None, :])
    expert_output = low_precision_backward(low_precision(jax.nn.gelu(pre_two)))
    gate_logits = low_precision_backward(jnp.einsum('rd,tde->tre', inputs, gate_weight, precision=high_precision) + gate_bias[:, None, :])
    gate_probabilities = low_precision(jax.nn.softmax(gate_logits, axis=-1))
    mixed_experts = low_precision(jnp.einsum('kvy,yvo->kvo', gate_probabilities, expert_output, precision=high_precision))
    tower_preactivation = low_precision_backward(jnp.einsum('wmn,wnl->wml', mixed_experts, tower_first_weight, precision=high_precision) + tower_first_bias[:, None, :])
    tower_act = jax.nn.gelu(tower_preactivation)
    score = jnp.einsum('trh,th->tr', tower_act, tower_last, precision=high_precision) + tower_out_bias[:, None]
    loss = jnp.sum(weights[None, :] * (jax.nn.softplus(score) - labels_f * score))
    return (loss, jax.nn.sigmoid(score))

def reference(inputs, w_first, b_first, w_second, b_second, gate_weight, gate_bias, tower_first_weight, tower_first_bias, tower_last, tower_out_bias, labels, group_len, group_shard):
    shards = jnp.arange(N_DP, dtype=jnp.int32)
    weights = jax.vmap(lambda shard: row_weights(group_len, group_shard, shard, 0, CAP))(shards).reshape(-1)
    labels_f = labels.astype(jnp.float32)
    params = tuple((a.astype(jnp.float32) for a in (inputs, w_first, b_first, w_second, b_second, gate_weight, gate_bias, tower_first_weight, tower_first_bias, tower_last, tower_out_bias)))

    def objective(*values):
        return forward(*values, labels_f, weights)
    loss, backward, predictions = jax.vjp(objective, *params, has_aux=True)
    grads = backward(jnp.float32(1.0))
    return (predictions, grads[0], grads[1], grads[2], grads[3], grads[4], grads[5], grads[6], grads[7], grads[8], grads[9], grads[10])
```

```python
import functools

import jax
import jax.numpy as jnp
from jax import lax
from jax.experimental import pallas as pl
from jax.experimental.pallas import tpu as pltpu
from jax.sharding import PartitionSpec as P

F32 = jnp.float32
BF16 = jnp.bfloat16
VMEM_BYTES = 56 * 2**20
CHUNK = 512
ROOT = 0.7978845608028654
CUBE = 0.044715
NN = (((1,), (0,)), ((), ()))
NT = (((1,), (1,)), ((), ()))
TN = (((0,), (0,)), ((), ()))
BIAS_ROWS = 16

def dot(a, b, dims):
    return lax.dot_general(a, b, dims, preferred_element_type=F32)

def gelu_pair(v):
    square = v * v
    upper = 0.5 + 0.5 * jnp.tanh(v * (ROOT + (ROOT * CUBE) * square))
    value = v * upper
    slope = upper + value * (1.0 - upper) * (2.0 * ROOT + (6.0 * ROOT * CUBE) * square)
    return value, slope

def row_weights(group_len, group_shard, shard, first, count):
    mine = group_shard == shard
    sizes = jnp.where(mine, group_len, 0)
    starts = jnp.cumsum(sizes) - sizes
    slots = (first + jnp.arange(count, dtype=jnp.int32))[:, None]
    inside = mine[None, :] & (slots >= starts[None, :]) & (slots < (starts + sizes)[None, :])
    recip = 1.0 / group_len.astype(F32)
    return jnp.sum(jnp.where(inside, recip[None, :], F32(0.0)), axis=1)

def params(flops, traffic):
    return dict(
        compiler_params=pltpu.CompilerParams(vmem_limit_bytes=VMEM_BYTES),
        cost_estimate=pl.CostEstimate(flops=flops, bytes_accessed=traffic, transcendentals=0),
    )

def whole(shape):
    return pl.BlockSpec(shape, lambda *_: (0,) * len(shape))


def gate_kernel(experts, half, slot_ref, x_ref, gw_ref, gb_ref, prob_ref, low_ref, scratch):
    logits = dot(gw_ref[...], x_ref[...], NT) + gb_ref[...]
    for t in range(2):
        part = logits[t * experts : (t + 1) * experts]
        top = jnp.max(part, axis=0, keepdims=True)
        e = jnp.exp(part - top)
        scratch[t * experts : (t + 1) * experts, :] = e / jnp.sum(e, axis=0, keepdims=True)
    for j in range(half):
        for t in range(2):
            row = scratch[pl.ds(t * experts + slot_ref[j], 1), :]
            prob_ref[j, t : t + 1, :] = row
            low_ref[j, t : t + 1, :] = row.astype(BF16).astype(F32)

def gate(slots, x, gw, gb):
    rows = x.shape[0]
    half = slots.shape[0]
    experts = 2 * half
    shape = jax.ShapeDtypeStruct((half, 2, rows), F32)

    return pl.pallas_call(
        functools.partial(gate_kernel, experts, half),
        in_specs=[
            pl.BlockSpec(memory_space=pltpu.SMEM),
            pl.BlockSpec(memory_space=pltpu.VMEM),
            pl.BlockSpec(memory_space=pltpu.VMEM),
            pl.BlockSpec(memory_space=pltpu.VMEM),
        ],
        out_specs=[pl.BlockSpec(memory_space=pltpu.VMEM)] * 2,
        out_shape=[shape, shape],
        scratch_shapes=[pltpu.VMEM((2 * experts, rows), F32)],
        **params(4 * rows * 512 * experts, rows * 1024),
    )(slots, x, gw, gb)


def bias_columns(pay):
    flipped = pay[-BIAS_ROWS:, :].astype(F32).T
    return flipped[:256, 0:1], flipped[256:384, 0:1]

def second_weight(pay):
    return jnp.concatenate([pay[256:320, :256], pay[256:320, 256:]], axis=0)

def forward_kernel(first, x_ref, pay_ref, low_ref, *refs):
    if first:
        h_ref, g1_ref, o_ref, g2_ref, mix_ref = refs
    else:
        mix_in, h_ref, g1_ref, o_ref, g2_ref, mix_ref = refs
    j = pl.program_id(0)

    @pl.when(j == 0)
    def _():
        mix_ref[...] = jnp.zeros_like(mix_ref) if first else mix_in[...]

    pay = pay_ref[0]
    w1 = pay[:256]
    w2 = second_weight(pay)
    b1, b2 = bias_columns(pay)
    rows = x_ref.shape[0]
    for k in range(0, rows, CHUNK):
        at = slice(k, k + CHUNK)
        value, slope = gelu_pair(dot(w1, x_ref[at, :], NT) + b1)
        hidden = value.astype(BF16)
        h_ref[0, :, at] = hidden
        g1_ref[0, :, at] = slope.astype(BF16)
        value, slope = gelu_pair(dot(w2, hidden, NN) + b2)
        out = value.astype(BF16)
        o_ref[0, :, at] = out
        g2_ref[0, :, at] = slope.astype(BF16)
        out = out.astype(F32)
        for t in range(2):
            mix_ref[t, :, at] += low_ref[0, t : t + 1, at] * out

def forward(x, pays, low, at, mixed):

    rows = x.shape[0]
    count = pays.shape[0]
    slot = lambda *shape: pl.BlockSpec((1,) + shape, lambda j: (j, 0, 0))
    mix_shape = (2, 128, rows)
    ins = [x, pays, low]
    specs = [whole(x.shape), slot(*pays.shape[1:]), pl.BlockSpec((1, 2, rows), lambda j: (at + j, 0, 0))]
    if mixed is not None:
        ins.append(mixed)
        specs.append(whole(mix_shape))
    return pl.pallas_call(
        functools.partial(forward_kernel, mixed is None),
        grid=(count,),
        in_specs=specs,
        out_specs=[slot(256, rows), slot(256, rows), slot(128, rows), slot(128, rows), whole(mix_shape)],
        out_shape=[
            jax.ShapeDtypeStruct((count, 256, rows), BF16),
            jax.ShapeDtypeStruct((count, 256, rows), BF16),
            jax.ShapeDtypeStruct((count, 128, rows), BF16),
            jax.ShapeDtypeStruct((count, 128, rows), BF16),
            jax.ShapeDtypeStruct(mix_shape, F32),
        ],
        **params(count * rows * (512 * 256 + 256 * 128) * 2, count * rows * 768 * 2),
    )(*ins)


def middle_kernel(
    experts,
    groups,
    slot_ref,
    x_ref,
    mix_ref,
    mix_other_ref,
    prob_ref,
    label_ref,
    weight_ref,
    tw_ref,
    tb_ref,
    tl_ref,
    to_ref,
    *refs,
):
    outs = refs[: len(groups)]
    pred_ref, dmix_ref, dgate_ref, shared_ref, mixed_low, d_tower, gates = refs[len(groups) :]
    rows = x_ref.shape[0]
    mine = rows // 2
    half = experts // 2
    gates[...] = jnp.zeros_like(gates)
    last = [jnp.zeros((64, 1), F32) for _ in range(2)]
    bias = [jnp.zeros((64, 1), F32) for _ in range(2)]
    out_bias = [jnp.zeros((1, 1), F32) for _ in range(2)]
    for k in range(0, rows, CHUNK):
        at = slice(k, k + CHUNK)
        other = slice((k + mine) % rows, (k + mine) % rows + CHUNK)
        d_mixed, centre = [], []
        for t in range(2):
            mixed = mix_ref[t, :, at] + mix_other_ref[t, :, other].astype(F32)
            low = mixed.astype(BF16)
            act, slope = gelu_pair(dot(tw_ref[t], low, NN) + tb_ref[t])
            score = jnp.sum(act * tl_ref[t], axis=0, keepdims=True) + to_ref[t]
            pred = 1.0 / (1.0 + jnp.exp(-score))
            pred_ref[t : t + 1, at] = pred
            d_score = weight_ref[:, at] * (pred - label_ref[t : t + 1, at].astype(F32))
            d_low = (d_score * tl_ref[t] * slope).astype(BF16)
            if k < mine:
                mixed_low[t, :, at] = low
                d_tower[t, :, at] = d_low
                last[t] = last[t] + jnp.sum(act * d_score, axis=1, keepdims=True)
                bias[t] = bias[t] + jnp.sum(d_low.astype(F32), axis=1, keepdims=True)
                out_bias[t] = out_bias[t] + jnp.sum(d_score, axis=1, keepdims=True)
            d_mixed.append(dot(tw_ref[t], d_low, TN))
            dmix_ref[t, :, at] = d_mixed[t]
            centre.append(jnp.sum(d_mixed[t] * mixed, axis=0, keepdims=True))
        j = 0
        for ref in outs:
            for i in range(ref.shape[0]):
                out = ref[i, :, at].astype(F32)
                for t in range(2):
                    d_prob = jnp.sum(d_mixed[t] * out, axis=0, keepdims=True)
                    d_gate = prob_ref[j, t : t + 1, at] * (d_prob - centre[t])
                    gates[pl.ds(t * experts + slot_ref[j], 1), at] = d_gate
                j += 1
    low = gates[...].astype(BF16)
    dgate_ref[...] = low
    for t in range(2):
        grad = dot(d_tower[t], mixed_low[t], NT)
        for k in range(4):
            shared_ref[16 * t : 16 * (t + 1), 128 * k : 128 * (k + 1)] = grad[16 * k : 16 * (k + 1)]
    shared_ref[32 : 32 + 2 * experts, :] = dot(low, x_ref[...], NN)
    tall = max(64, 2 * experts)
    pad = lambda col: jnp.concatenate([col, jnp.zeros((tall - col.shape[0], 1), F32)], axis=0) if col.shape[0] < tall else col
    columns = [
        pad(last[0]),
        pad(last[1]),
        pad(bias[0]),
        pad(bias[1]),
        jnp.broadcast_to(out_bias[0], (tall, 1)),
        jnp.broadcast_to(out_bias[1], (tall, 1)),
        pad(jnp.sum(low.astype(F32), axis=1, keepdims=True)),
    ]
    lane = lax.broadcasted_iota(jnp.int32, (tall, 128), 1)
    small = jnp.zeros((tall, 128), F32)
    for n, col in enumerate(columns):
        small = jnp.where(lane == n, jnp.broadcast_to(col, (tall, 128)), small)
    base = 32 + 2 * experts
    deep = tall // 4
    for k in range(4):
        shared_ref[base : base + deep, 128 * k : 128 * (k + 1)] = small[deep * k : deep * (k + 1)]

def middle(slots, x, mixed, mixed_other, prob, labels, weights, tw, tb, tl, to, outs):

    rows = x.shape[0]
    experts = 2 * slots.shape[0]
    shared_rows = 32 + 2 * experts + max(64, 2 * experts) // 4
    vmem = pl.BlockSpec(memory_space=pltpu.VMEM)
    smem = pl.BlockSpec(memory_space=pltpu.SMEM)
    return pl.pallas_call(
        functools.partial(middle_kernel, experts, tuple(o.shape[0] for o in outs)),
        in_specs=[smem] + [vmem] * 9 + [smem] + [vmem] * len(outs),
        out_specs=[vmem] * 4,
        out_shape=[
            jax.ShapeDtypeStruct((2, rows), F32),
            jax.ShapeDtypeStruct((2, 128, rows), F32),
            jax.ShapeDtypeStruct((2 * experts, rows), BF16),
            jax.ShapeDtypeStruct((shared_rows, 512), F32),
        ],
        scratch_shapes=[
            pltpu.VMEM((2, 128, rows // 2), BF16),
            pltpu.VMEM((2, 64, rows // 2), BF16),
            pltpu.VMEM((2 * experts, rows), F32),
        ],
        **params(rows * 128 * 64 * 12, rows * 128 * 2 * (experts // 2 + 8)),
    )(slots, x, mixed, mixed_other, prob, labels, weights, tw, tb, tl, to, *outs)


def backward_kernel(x_ref, pay_ref, low_ref, dmix_ref, h_ref, g1_ref, g2_ref, grad_ref, done_ref, d_two):
    w2 = second_weight(pay_ref[0])
    rows = x_ref.shape[0]
    sum_one = jnp.zeros((256, 128), F32)
    sum_two = jnp.zeros((128, 128), F32)
    for k in range(0, rows, CHUNK):
        at = slice(k, k + CHUNK)
        d_out = low_ref[0, 0:1, at] * dmix_ref[0, :, at] + low_ref[0, 1:2, at] * dmix_ref[1, :, at]
        two = d_out.astype(BF16).astype(F32) * g2_ref[0, :, at].astype(F32)
        two_low = two.astype(BF16)
        d_two[:, at] = two_low
        one = dot(w2, two_low, TN) * g1_ref[0, :, at].astype(F32)
        one_low = one.astype(BF16)
        done_ref[0, :, at] = one_low
        for n in range(0, CHUNK, 128):
            sum_one = sum_one + one[:, n : n + 128]
            sum_two = sum_two + two[:, n : n + 128]
    grad_ref[0, :256, :] = dot(done_ref[0], x_ref[...], NN).astype(BF16)
    second = dot(d_two[...], h_ref[0], NT).astype(BF16)
    grad_ref[0, 256:320, :256] = second[:64]
    grad_ref[0, 256:320, 256:] = second[64:]
    row = jnp.concatenate(
        [
            jnp.sum(sum_one.T, axis=0, keepdims=True),
            jnp.sum(sum_two.T, axis=0, keepdims=True),
            jnp.zeros((1, 128), F32),
        ],
        axis=1,
    )
    high = row.astype(BF16).astype(F32)
    index = lax.broadcasted_iota(jnp.int32, (BIAS_ROWS, 512), 0)
    both = jnp.where(index == 0, high, jnp.where(index == 1, row - high, 0.0))
    grad_ref[0, 320:, :] = both.astype(BF16)

def backward(x, pays, low, dmix, saved, at, first, count):
    h, g1, _, g2 = saved
    rows = x.shape[0]
    slot = lambda *shape: pl.BlockSpec((1,) + shape, lambda j: (first + j, 0, 0))
    out_slot = lambda *shape: pl.BlockSpec((1,) + shape, lambda j: (j, 0, 0))
    return pl.pallas_call(
        backward_kernel,
        grid=(count,),
        in_specs=[
            whole(x.shape),
            slot(*pays.shape[1:]),
            pl.BlockSpec((1, 2, rows), lambda j: (at + j, 0, 0)),
            whole(dmix.shape),
            slot(256, rows),
            slot(256, rows),
            slot(128, rows),
        ],
        out_specs=[out_slot(*pays.shape[1:]), out_slot(256, rows)],
        out_shape=[
            jax.ShapeDtypeStruct((count,) + pays.shape[1:], BF16),
            jax.ShapeDtypeStruct((count, 256, rows), BF16),
        ],
        scratch_shapes=[pltpu.VMEM((128, rows), BF16)],
        **params(count * rows * (512 * 256 + 2 * 256 * 128) * 2, count * rows * 900 * 2),
    )(x, pays, low, dmix, h, g1, g2)


def input_kernel(counts, add, dgate_ref, gw_ref, *refs):
    n = len(counts)
    total = dot(dgate_ref[...], gw_ref[...], TN)
    for ones, pays, count in zip(refs[:n], refs[n : 2 * n], counts):
        for j in range(count):
            total = total + dot(ones[j], pays[j, :256, :], TN)
    if add:
        total = total + refs[2 * n][...].astype(F32)
    refs[-1][...] = total.astype(refs[-1].dtype)

def input_gradient(dgate, gw, ones, pays, first, rows, added, dtype):

    block = 512
    start = first // block
    specs = [pl.BlockSpec((dgate.shape[0], block), lambda i: (0, start + i)), whole(gw.shape)]
    specs += [pl.BlockSpec((o.shape[0], 256, block), lambda i: (0, 0, start + i)) for o in ones]
    specs += [whole(p.shape) for p in pays]
    args = [dgate, gw, *ones, *pays]
    if added is not None:
        args.append(added)
        specs.append(pl.BlockSpec((block, 512), lambda i: (i, 0)))
    experts = sum(o.shape[0] for o in ones)
    return pl.pallas_call(
        functools.partial(input_kernel, tuple(o.shape[0] for o in ones), added is not None),
        grid=(rows // block,),
        in_specs=specs,
        out_specs=pl.BlockSpec((block, 512), lambda i: (i, 0)),
        out_shape=jax.ShapeDtypeStruct((rows, 512), dtype),
        **params(experts * rows * 512 * 256 * 2, experts * rows * 256 * 2),
    )(*args)


def per_device(
    inputs,
    w_first,
    b_first,
    w_second,
    b_second,
    gate_weight,
    gate_bias,
    tower_first_weight,
    tower_first_bias,
    tower_last,
    tower_out_bias,
    labels,
    group_len,
    group_shard,
):
    rows = inputs.shape[0]
    experts = lax.axis_size("expert")
    half = experts // 2
    bits = experts.bit_length() - 1
    core = lax.axis_index("dp")
    place = lax.axis_index("expert")
    owner = core == place // half

    order = [[bits - 2 - s for s in range(bits - 1)] for _ in range(2)]
    order[1][-2:] = order[1][-2:][::-1]

    def pairs(bit_of_core, want=None):
        return [
            (c * experts + q, c * experts + (q ^ (1 << bit_of_core[c])))
            for c in range(2)
            for q in range(experts)
            if want is None or (c == q // half) == want
        ]

    def send(value, bit_of_core, want=None):
        return lax.ppermute(value, ("dp", "expert"), pairs(bit_of_core, want))

    def swap(value):
        return lax.ppermute(value, "dp", [(0, 1), (1, 0)])

    masks = [
        [sum(((j >> s) & 1) << order[c][s] for s in range(bits - 1)) for j in range(half)]
        for c in range(2)
    ]
    mask = jnp.where(core == 0, jnp.array(masks[0], jnp.int32), jnp.array(masks[1], jnp.int32))
    slots = core * half + ((place % half) ^ mask)

    first_t = w_first[0].T
    second_t = w_second[0].T
    bias_row = jnp.concatenate([b_first[0], b_second[0], jnp.zeros((128,), BF16)])
    pay = jnp.concatenate(
        [
            first_t,
            jnp.concatenate([second_t[:64], second_t[64:]], axis=1),
            jnp.broadcast_to(bias_row[None], (BIAS_ROWS, 512)),
        ],
        axis=0,
    )
    top = [bits - 1] * 2
    low_bit = [order[0][0], order[1][0]]
    from_far = send(pay, top, True)
    from_near = send(pay, low_bit, True)
    x = jnp.concatenate([inputs, swap(inputs)], axis=0)
    label_pair = jnp.concatenate([labels, swap(labels)], axis=1)
    slot_zero = jnp.where(owner, pay, from_far)
    slot_one = from_near + send(slot_zero, low_bit, False)
    groups = [jnp.stack([slot_zero, slot_one])]
    for s in range(1, bits - 1):
        held = groups[0] if len(groups) == 1 else jnp.concatenate(groups, axis=0)
        groups.append(send(held, [order[0][s], order[1][s]]))
    starts = [0] + [1 << s for s in range(1, bits - 1)]

    gw = jnp.transpose(gate_weight, (0, 2, 1)).reshape(2 * experts, 512)
    gb = gate_bias.astype(F32).reshape(2 * experts, 1)
    prob, low = gate(slots, x, gw, gb)
    weights = jnp.concatenate(
        [
            row_weights(group_len, group_shard, core, place * rows, rows),
            row_weights(group_len, group_shard, 1 - core, place * rows, rows),
        ]
    )[None, :]

    mixed = None
    saved = []
    for at, group in zip(starts, groups):
        *kept, mixed = forward(x, group, low, at, mixed)
        saved.append(kept)

    mixed_other = swap(mixed.astype(BF16))
    predictions, dmix, dgate, shared = middle(
        slots,
        x,
        mixed,
        mixed_other,
        prob,
        label_pair,
        weights,
        jnp.transpose(tower_first_weight, (0, 2, 1)),
        tower_first_bias.astype(F32)[:, :, None],
        tower_last.astype(F32)[:, :, None],
        tower_out_bias.astype(F32),
        [kept[2] for kept in saved],
    )

    shared = shared + swap(shared)
    for b in reversed(range(bits)):
        shared = shared + send(shared, [b, b])

    grads = [None] * len(groups)
    ones = [None] * len(groups)
    coming = None
    for s in reversed(range(bits - 1)):
        g = max(s, 0)
        grads[g], ones[g] = backward(x, groups[g], low, dmix, saved[g], starts[g], 0, groups[g].shape[0])
        if s == 0:
            break
        total = grads[g]
        if coming is not None:
            size = total.shape[0]
            total = (total.astype(F32) + coming[size : 2 * size].astype(F32)).astype(BF16)
            coming = coming[:size]
        arrived = send(total, [order[0][s], order[1][s]])
        coming = arrived if coming is None else (coming.astype(F32) + arrived.astype(F32)).astype(BF16)
    total = grads[0].astype(F32) + coming.astype(F32)
    slot_zero, slot_one = total[0], total[1].astype(BF16)
    passed = slot_zero + send(slot_one, low_bit, False).astype(F32)
    far = send(passed.astype(BF16), top, False)
    near = send(slot_one, low_bit, True)
    final = slot_zero + far.astype(F32) + near.astype(F32)
    final = jnp.where(owner, final, swap(final))

    over = input_gradient(dgate, gw, ones, groups, rows, rows, None, BF16)
    input_grad = input_gradient(dgate, gw, ones, groups, 0, rows, swap(over), F32)

    grad_w_first = final[:256].T
    grad_w_second = jnp.concatenate([final[256:320, :256], final[256:320, 256:]], axis=0).T
    bias = final[320] + final[321]
    base = 32 + 2 * experts
    tall = max(64, 2 * experts)
    unfold = lambda block: jnp.concatenate([block[:, 128 * k : 128 * (k + 1)] for k in range(4)], axis=0)
    small = unfold(shared[base : base + tall // 4])
    tower_first = jnp.stack([unfold(shared[16 * t : 16 * (t + 1)]).T for t in range(2)])
    return (
        predictions[:, :rows],
        input_grad,
        grad_w_first[None],
        bias[None, :256],
        grad_w_second[None],
        bias[None, 256:384],
        jnp.transpose(shared[32:base].reshape(2, experts, 512), (0, 2, 1)),
        small[: 2 * experts, 6].reshape(2, experts),
        tower_first,
        small[:64, 2:4].T,
        small[:64, 0:2].T,
        small[0, 4:6],
    )

def solution(mesh):
    in_specs = (
        P(("dp", "expert"), None),
        P("expert", None, None),
        P("expert", None),
        P("expert", None, None),
        P("expert", None),
        P(),
        P(),
        P(),
        P(),
        P(),
        P(),
        P(None, ("dp", "expert")),
        P(),
        P(),
    )
    out_specs = (
        P(None, ("dp", "expert")),
        P(("dp", "expert"), None),
        P("expert", None, None),
        P("expert", None),
        P("expert", None, None),
        P("expert", None),
        P(),
        P(),
        P(),
        P(),
        P(),
        P(),
    )
    return jax.shard_map(
        per_device, mesh=mesh, in_specs=in_specs, out_specs=out_specs, check_vma=False
    )
```

```python
import functools

import jax
import jax.numpy as jnp
from jax import lax
from jax.experimental import pallas as pl
from jax.experimental.pallas import tpu as pltpu
from jax.sharding import PartitionSpec as P

F32 = jnp.float32
BF16 = jnp.bfloat16
ROOT = 0.7978845608028654
CUBE = 0.044715
NN = (((1,), (0,)), ((), ()))
NT = (((1,), (1,)), ((), ()))
TN = (((0,), (0,)), ((), ()))
TT = (((0,), (1,)), ((), ()))
BIAS_ROWS = 16
PAY_ROWS = 320 + BIAS_ROWS
VMEM = pl.BlockSpec(memory_space=pltpu.VMEM)
SMEM = pl.BlockSpec(memory_space=pltpu.SMEM)


def dot(a, b, dims):
    return lax.dot_general(a, b, dims, preferred_element_type=F32)


def gelu_pair(v):
    square = v * v
    upper = 0.5 + 0.5 * jnp.tanh(v * (ROOT + (ROOT * CUBE) * square))
    value = v * upper
    slope = upper + value * (1.0 - upper) * (2.0 * ROOT + (6.0 * ROOT * CUBE) * square)
    return value, slope


def call(kernel, ins, outs, pin, micros, scratch=(), scalars=0, limit=8):
    limit = limit if pin is not None else 60
    pinned = lambda a: pltpu.with_memory_space_constraint(a, pltpu.VMEM) if pin else a
    args = [a if n < scalars else pinned(a) for n, a in enumerate(ins)]
    kept = pltpu.VMEM if pin else jax.ShapeDtypeStruct
    shapes = [(kept if stay else jax.ShapeDtypeStruct)(shape, dtype) for shape, dtype, stay in outs]
    return pl.pallas_call(
        kernel,
        in_specs=[SMEM] * scalars + [VMEM] * (len(ins) - scalars),
        out_specs=[VMEM] * len(outs),
        out_shape=shapes,
        scratch_shapes=list(scratch),
        compiler_params=pltpu.CompilerParams(vmem_limit_bytes=limit * 2**20),
        cost_estimate=pl.CostEstimate(flops=int(micros * 1e9), bytes_accessed=0, transcendentals=0),
    )(*args)


def to_column(row):
    n = row.shape[1]
    same = lax.broadcasted_iota(jnp.int32, (n, n), 0) == lax.broadcasted_iota(jnp.int32, (n, n), 1)
    return jnp.sum(jnp.where(same, jnp.broadcast_to(row, (n, n)), 0.0), axis=1, keepdims=True)


def side_by_side(columns, tall):
    lane = lax.broadcasted_iota(jnp.int32, (tall, 128), 1)
    small = jnp.zeros((tall, 128), F32)
    for n, col in enumerate(columns):
        small = jnp.where(lane == n, jnp.broadcast_to(col, (tall, 128)), small)
    return small


def fold(ref, base, block):
    deep = block.shape[0] // 4
    for k in range(4):
        ref[base : base + deep, 128 * k : 128 * (k + 1)] = block[deep * k : deep * (k + 1)]


def unfold(ref, base, deep):
    return jnp.concatenate(
        [ref[base : base + deep, 128 * k : 128 * (k + 1)] for k in range(4)], axis=0
    )


def pack_kernel(w1_ref, w2_ref, b1_ref, b2_ref, pay_ref):
    pay_ref[0, :256, :] = w1_ref[0].astype(F32).T.astype(BF16)
    second = w2_ref[0].astype(F32).T.astype(BF16)
    pay_ref[0, 256:320, :256] = second[:64]
    pay_ref[0, 256:320, 256:] = second[64:]
    row = jnp.concatenate(
        [b1_ref[...].astype(F32), b2_ref[...].astype(F32), jnp.zeros((1, 128), F32)], axis=1
    )
    pay_ref[0, 320:, :] = jnp.broadcast_to(row, (BIAS_ROWS, 512)).astype(BF16)


def biases(pay):
    flipped = pay[320:, :].astype(F32).T
    return flipped[:256, 0:1], flipped[256:384, 0:1]


def second_weight(pay):
    return jnp.concatenate([pay[256:320, :256], pay[256:320, 256:]], axis=0)


def gate_kernel(experts, groups, slot_ref, len_ref, shard_ref, where_ref, tob_ref, mine_ref, other_ref, gw_ref, gb_ref, *refs):
    prob_ref, low_ref, weight_ref, tob_out, scratch = refs
    for t in range(2):
        tob_out[t : t + 1, :] = jnp.full((1, 128), tob_ref[t], F32)
    rows = mine_ref.shape[0]
    for side, x_ref in enumerate((mine_ref, other_ref)):
        at = slice(side * rows, (side + 1) * rows)
        for t in range(2):
            part = dot(gw_ref[t], x_ref[...], NT) + to_column(gb_ref[t : t + 1, :].astype(F32))
            top = jnp.max(part, axis=0, keepdims=True)
            e = jnp.exp(part - top)
            scratch[t * experts : (t + 1) * experts, at] = e / jnp.sum(e, axis=0, keepdims=True)
        shard = where_ref[0] if side == 0 else 1 - where_ref[0]
        index = where_ref[1] * rows + lax.broadcasted_iota(jnp.int32, (1, rows), 1)
        start = jnp.int32(0)
        weight = jnp.zeros((1, rows), F32)
        for g in range(groups):
            size = jnp.where(shard_ref[g] == shard, len_ref[g], 0)
            inside = (index >= start) & (index < start + size)
            recip = 1.0 / jnp.full((1, rows), len_ref[g], jnp.int32).astype(F32)
            weight = weight + jnp.where(inside, recip, 0.0)
            start = start + size
        weight_ref[:, at] = weight
    for j in range(experts // 2):
        for t in range(2):
            row = scratch[pl.ds(t * experts + slot_ref[j], 1), :]
            prob_ref[j, t : t + 1, :] = row
            low_ref[j, t : t + 1, :] = row.astype(BF16).astype(F32)


def forward_kernel(bundles, first, chunk, mine_ref, other_ref, pay_a, pay_b, low_ref, *refs):
    if not first:
        mix_in, *refs = refs
    kept, mix_ref = (refs[:4], refs[4:8]), refs[8]
    rows = mine_ref.shape[0]
    depth = pay_a.shape[0]
    weights = {}
    for k in range(depth):
        for n, pay_ref in enumerate((pay_a, pay_b)):
            pay = pay_ref[k]
            weights[k, n] = (pay[:256], second_weight(pay), *biases(pay))
    work = [(c, k, n) for c in range(0, 2 * rows, chunk) for k in range(depth) for n in range(2)]
    totals = [None, None]

    def layer_one(c, k, n):
        ref, c = (mine_ref, c) if c < rows else (other_ref, c - rows)
        return dot(weights[k, n][0], ref[c : c + chunk, :], NT)

    def after_one(pre, c, k, n):
        value, slope = gelu_pair(pre + weights[k, n][2])
        hidden = value.astype(BF16)
        kept[n][0][k, :, c : c + chunk] = hidden
        kept[n][1][k, :, c : c + chunk] = slope.astype(kept[n][1].dtype)
        return hidden

    def after_two(pre, c, k, n):
        at = slice(c, c + chunk)
        value, slope = gelu_pair(pre + weights[k, n][3])
        out = value.astype(BF16)
        kept[n][2][k, :, at] = out
        kept[n][3][k, :, at] = slope.astype(kept[n][3].dtype)
        out = out.astype(F32)
        for t in range(2):
            term = low_ref[bundles[n] * depth + k, t : t + 1, at] * out
            if k == 0 and n == 0:
                totals[t] = term if first else mix_in[t, :, at] + term
            else:
                totals[t] = totals[t] + term
            if k == depth - 1 and n == 1:
                mix_ref[t, :, at] = totals[t].astype(mix_ref.dtype)

    ones, twos = {0: layer_one(*work[0])}, {}
    for i in range(len(work) + 1):
        if i + 1 < len(work):
            ones[i + 1] = layer_one(*work[i + 1])
        if i < len(work):
            hidden = after_one(ones.pop(i), *work[i])
        if i >= 1:
            after_two(twos.pop(i - 1), *work[i - 1])
        if i < len(work):
            twos[i] = dot(weights[work[i][1:]][1], hidden, NN)


def tower_kernel(
    chunk, mix_ref, come_ref, mine_ref, other_ref, weight_ref, tob_ref, tw_ref, tb_ref, tl_ref,
    pred_ref, dmix_ref, centre_ref, shared_ref,
):
    rows = mine_ref.shape[1]
    first = [jnp.zeros((64, 128), F32) for _ in range(2)]
    sums = [[jnp.zeros((64, 1), F32) for _ in range(3)] for _ in range(2)]
    tb = [to_column(tb_ref[t : t + 1, :].astype(F32)) for t in range(2)]
    tl = [to_column(tl_ref[t : t + 1, :].astype(F32)) for t in range(2)]
    for c in range(0, 2 * rows, chunk):
        at = slice(c, c + chunk)
        there = slice((c + rows) % (2 * rows), (c + rows) % (2 * rows) + chunk)
        ref, lo = (mine_ref, c) if c < rows else (other_ref, c - rows)
        for t in range(2):
            mixed = mix_ref[t, :, at].astype(F32) + come_ref[t, :, there].astype(F32)
            low = mixed.astype(BF16)
            act, slope = gelu_pair(dot(tw_ref[t], low, NN) + tb[t])
            score = jnp.sum(act * tl[t], axis=0, keepdims=True) + tob_ref[t : t + 1, 0:1]
            pred = 1.0 / (1.0 + jnp.exp(-score))
            d_score = weight_ref[:, at] * (pred - ref[t : t + 1, lo : lo + chunk].astype(F32))
            d_low = (d_score * tl[t] * slope).astype(BF16)
            d_mixed = dot(tw_ref[t], d_low, TN)
            dmix_ref[t, :, at] = d_mixed
            centre_ref[t : t + 1, at] = jnp.sum(d_mixed * mixed, axis=0, keepdims=True)
            if c < rows:
                pred_ref[t : t + 1, at] = pred
                first[t] = first[t] + dot(d_low, low, NT)
                sums[t][0] = sums[t][0] + jnp.sum(act * d_score, axis=1, keepdims=True)
                sums[t][1] = sums[t][1] + jnp.sum(d_low.astype(F32), axis=1, keepdims=True)
                total = jnp.sum(d_score, axis=1, keepdims=True)
                sums[t][2] = sums[t][2] + jnp.broadcast_to(total, (64, 1))
    for t in range(2):
        fold(shared_ref, 16 * t, first[t])
    fold(shared_ref, 32, side_by_side([sums[t][n] for n in range(3) for t in range(2)], 64))


def shared_rows(experts):
    return -(-(48 + 2 * experts + experts // 2) // 16) * 16


def gate_back_kernel(experts, chunk, slot_ref, spot_ref, mine_ref, other_ref, dmix_ref, centre_ref, prob_ref, tower_ref, *refs):
    outs = refs[:8]
    dgate_ref, keep_ref, give_ref, gates, shared_ref = refs[8:]
    rows = mine_ref.shape[0]
    depth = outs[0].shape[0]
    gates[...] = jnp.zeros_like(gates)
    for c in range(0, 2 * rows, chunk):
        at = slice(c, c + chunk)
        for j in range(8 * depth):
            out = outs[j // depth][j % depth, :, at].astype(F32)
            for t in range(2):
                d_prob = jnp.sum(dmix_ref[t, :, at] * out, axis=0, keepdims=True)
                d_gate = prob_ref[j, t : t + 1, at] * (d_prob - centre_ref[t : t + 1, at])
                gates[pl.ds(t * experts + slot_ref[j], 1), at] = d_gate
    low = gates[...].astype(BF16)
    dgate_ref[...] = low
    shared_ref[...] = jnp.zeros_like(shared_ref)
    shared_ref[:48, :] = tower_ref[...]
    grad = dot(low[:, :rows], mine_ref[...], NN) + dot(low[:, rows:], other_ref[...], NN)
    shared_ref[48 : 48 + 2 * experts, :] = grad
    bias = jnp.sum(low.astype(F32), axis=1, keepdims=True)
    fold(shared_ref, 48 + 2 * experts, side_by_side([bias], 2 * experts))
    deep = keep_ref.shape[0]
    keep_ref[...] = shared_ref[pl.ds(pl.multiple_of(spot_ref[0] * deep, 8), deep), :]
    give_ref[...] = shared_ref[pl.ds(pl.multiple_of((1 - spot_ref[0]) * deep, 8), deep), :]


def backward_kernel(bundles, add, chunk, mine_ref, other_ref, pay_a, pay_b, low_ref, dmix_ref, *refs):
    kept, refs = (refs[:3], refs[3:6]), refs[6:]
    if add:
        come, refs = refs[:2], refs[2:]
    grads, dones, d_two = refs[:2], refs[2:4], refs[4]
    rows = mine_ref.shape[0]
    depth = pay_a.shape[0]
    for k in range(depth):
        for n in range(2):
            h_ref, g1_ref, g2_ref = kept[n]
            j = bundles[n] * depth + k
            w2 = second_weight((pay_a, pay_b)[n][k])
            sum_one = jnp.zeros((256, 128), F32)
            sum_two = jnp.zeros((128, 128), F32)
            for c in range(0, 2 * rows, chunk):
                at = slice(c, c + chunk)
                d_out = low_ref[j, 0:1, at] * dmix_ref[0, :, at] + low_ref[j, 1:2, at] * dmix_ref[1, :, at]
                two = d_out.astype(BF16).astype(F32) * g2_ref[k, :, at].astype(F32)
                two_low = two.astype(BF16)
                d_two[n, :, at] = two_low
                one = dot(w2, two_low, TN) * g1_ref[k, :, at].astype(F32)
                dones[n][k, :, at] = one.astype(BF16)
                for m in range(0, chunk, 128):
                    sum_one = sum_one + one[:, m : m + 128]
                    sum_two = sum_two + two[:, m : m + 128]
            first = dot(dones[n][k, :, :rows], mine_ref[...], NN)
            first = first + dot(dones[n][k, :, rows:], other_ref[...], NN)
            second = dot(d_two[n], h_ref[k], NT)
            second = jnp.concatenate([second[:64], second[64:]], axis=1)
            row = jnp.concatenate(
                [
                    jnp.sum(sum_one.T, axis=0, keepdims=True),
                    jnp.sum(sum_two.T, axis=0, keepdims=True),
                    jnp.zeros((1, 128), F32),
                ],
                axis=1,
            )
            high = row.astype(BF16).astype(F32)
            index = lax.broadcasted_iota(jnp.int32, (BIAS_ROWS, 512), 0)
            both = jnp.where(index == 0, high, jnp.where(index == 1, row - high, 0.0))
            if add:
                first = first + come[n][k, :256, :].astype(F32)
                second = second + come[n][k, 256:320, :].astype(F32)
                both = both + come[n][k, 320:, :].astype(F32)
            grads[n][k, :256, :] = first.astype(grads[n].dtype)
            grads[n][k, 256:320, :] = second.astype(grads[n].dtype)
            grads[n][k, 320:, :] = both.astype(grads[n].dtype)


def input_kernel(side, add, dgate_ref, gw_ref, *refs):
    ones, pays, out_ref = refs[:8], refs[8:16], refs[-1]
    rows = out_ref.shape[0]
    depth = ones[0].shape[0]
    experts = gw_ref.shape[1]
    chunk = 256
    for c in range(0, rows, chunk):
        at = slice(side * rows + c, side * rows + c + chunk)
        total = dot(dgate_ref[:experts, at], gw_ref[0], TN) + dot(dgate_ref[experts:, at], gw_ref[1], TN)
        for one, pay in zip(ones, pays):
            for k in range(depth):
                total = total + dot(one[k, :, at], pay[k, :256, :], TN)
        if add:
            total = total + refs[16][c : c + chunk, :].astype(F32)
        out_ref[c : c + chunk, :] = total.astype(out_ref.dtype)


def add_kernel(count, *refs):
    total = refs[0][...].astype(F32)
    for ref in refs[1:count]:
        total = total + ref[...].astype(F32)
    for ref in refs[count:]:
        ref[...] = total.astype(ref.dtype)


def finish_kernel(owner_ref, mine_ref, come_ref, w1_ref, b1_ref, w2_ref, b2_ref):
    owner = owner_ref[2] == 1
    mine_ref, come_ref = mine_ref.at[0], come_ref.at[0]
    w1_ref[0] = jnp.where(owner, mine_ref[:256, :], come_ref[:256, :]).T
    second = jnp.where(owner, mine_ref[256:320, :], come_ref[256:320, :])
    w2_ref[0] = jnp.concatenate([second[:, :256], second[:, 256:]], axis=0).T
    bias = jnp.where(owner, mine_ref[320:328, :], come_ref[320:328, :])
    bias = bias[0:1] + bias[1:2]
    b1_ref[...] = bias[:, :256]
    b2_ref[...] = bias[:, 256:384]


def finish_shared_kernel(experts, spot_ref, keep_ref, give_ref, gate_ref, gate_bias_ref, first_ref, tb_ref, tl_ref, tob_ref, shared_ref):
    base = 48 + 2 * experts
    deep = keep_ref.shape[0]
    shared_ref[pl.ds(pl.multiple_of(spot_ref[0] * deep, 8), deep), :] = keep_ref[...]
    shared_ref[pl.ds(pl.multiple_of((1 - spot_ref[0]) * deep, 8), deep), :] = give_ref[...]
    for t in range(2):
        gate_ref[t] = shared_ref[48 + t * experts : 48 + (t + 1) * experts, :]
        first_ref[t] = unfold(shared_ref, 16 * t, 16)
    small = unfold(shared_ref, 32, 16).T
    tl_ref[...] = small[0:2, :]
    tb_ref[...] = small[2:4, :]
    tob_ref[...] = small[4:6, :]
    bias = unfold(shared_ref, base, experts // 2).T
    gate_bias_ref[0:1, :] = bias[0:1, :experts]
    gate_bias_ref[1:2, :] = bias[0:1, experts:]


def per_device(
    inputs,
    w_first,
    b_first,
    w_second,
    b_second,
    gate_weight,
    gate_bias,
    tower_first_weight,
    tower_first_bias,
    tower_last,
    tower_out_bias,
    labels,
    group_len,
    group_shard,
):
    rows = inputs.shape[0]
    experts = lax.axis_size("expert")
    half = experts // 2
    bits = experts.bit_length() - 1
    depth = half // 8
    pin = True if depth == 1 else None
    chunk = 256 if pin else 512
    core = lax.axis_index("dp")
    place = lax.axis_index("expert")
    owner = core == place // half
    near_bit, mid_bit, end_bit = (2, 2), (1, 0), (0, 1)
    extra = [(b, b) for b in range(bits - 2, 2, -1)]

    def pairs(bit_of_core, want=None):
        return [
            (c * experts + q, c * experts + (q ^ (1 << bit_of_core[c])))
            for c in range(2)
            for q in range(experts)
            if want is None or (c == q // half) == want
        ]

    def send(value, bit_of_core, want=None):
        return lax.ppermute(value, ("dp", "expert"), pairs(bit_of_core, want))

    def swap(value):
        return lax.ppermute(value, "dp", [(0, 1), (1, 0)])

    def deal(value):
        route = []
        for c in range(2):
            for q in range(experts):
                target = c * experts + (q ^ half) if c == q // half else (1 - c) * experts + q
                route.append((c * experts + q, target))
        return lax.ppermute(value, ("dp", "expert"), route)

    def expert_mask(c, j):
        bundle, inner = j // depth, j % depth
        found = sum(1 << extra[e][c] for e in range(len(extra)) if (inner >> e) & 1)
        for n, at in enumerate((near_bit, mid_bit, end_bit)):
            found |= ((bundle >> n) & 1) << at[c]
        return found

    masks = [jnp.array([expert_mask(c, j) for j in range(half)], jnp.int32) for c in range(2)]
    spot = jnp.stack([core, place, owner.astype(jnp.int32)]).astype(jnp.int32)
    slots = core * half + ((place % half) ^ jnp.where(core == 0, masks[0], masks[1]))

    (pay,) = call(
        pack_kernel, [w_first, w_second, b_first, b_second], [((1, PAY_ROWS, 512), BF16, False)], pin, 1.5
    )
    zero = deal(pay)
    for at in extra:
        zero = jnp.concatenate([zero, send(zero, at)], axis=0)
    pays = [zero] + [None] * 7
    pays[1] = send(pays[0], near_bit)
    pays[2] = send(pays[0], mid_bit)
    pays[4] = send(pays[0], end_bit)
    pays[3] = send(pays[1], mid_bit)
    pays[5] = send(pays[1], end_bit)
    pays[6] = send(pays[2], end_bit)
    pays[7] = send(pays[3], end_bit)

    x = [inputs, swap(inputs)]
    other_labels = swap(labels)
    gate_rows = jnp.transpose(gate_weight, (0, 2, 1))
    prob, low, weights, tob = call(
        functools.partial(gate_kernel, experts, group_len.shape[0]),
        [slots, group_len, group_shard, spot, tower_out_bias.astype(F32), *x, gate_rows, gate_bias],
        [((half, 2, 2 * rows), F32, True)] * 2 + [((1, 2 * rows), F32, True), ((2, 128), F32, True)],
        pin,
        4,
        [pltpu.VMEM((2 * experts, 2 * rows), F32)],
        5,
    )

    mixed = None
    saved = [None] * 8
    slope_type = F32 if pin else BF16
    for a, b in ((0, 1), (2, 4), (3, 5), (6, 7)):
        shape = lambda deep, dtype: ((depth, deep, 2 * rows), dtype, True)
        *kept, mixed = call(
            functools.partial(forward_kernel, (a, b), mixed is None, chunk),
            [*x, pays[a], pays[b], low] + ([] if mixed is None else [mixed]),
            [shape(256, BF16), shape(256, BF16), shape(128, BF16), shape(128, slope_type)] * 2
            + [((2, 128, 2 * rows), BF16 if a == 6 else F32, True)],
            pin,
            4.5 * depth,
        )
        saved[a], saved[b] = kept[:4], kept[4:]

    predictions, dmix, centre, tower_sums = call(
        functools.partial(tower_kernel, 512),
        [mixed, swap(mixed), labels, other_labels, weights, tob]
        + [jnp.transpose(tower_first_weight, (0, 2, 1)), tower_first_bias, tower_last],
        [
            ((2, rows), F32, False),
            ((2, 128, 2 * rows), F32, True),
            ((2, 2 * rows), F32, True),
            ((48, 512), F32, True),
        ],
        pin,
        4,
    )

    def back(a, b, come, dtype):
        grad = ((depth, PAY_ROWS, 512), dtype, False)
        done = ((depth, 256, 2 * rows), BF16, True)
        return call(
            functools.partial(backward_kernel, (a, b), come is not None, chunk),
            [*x, pays[a], pays[b], low, dmix]
            + [saved[n][m] for n in (a, b) for m in (0, 1, 3)]
            + list(come or ()),
            [grad, grad, done, done],
            pin,
            5 * depth,
            [pltpu.VMEM((2, 128, 2 * rows), BF16)],
        )

    ones = [None] * 8
    grad_six, grad_seven, ones[6], ones[7] = back(6, 7, None, BF16)
    six, seven = send(grad_six, end_bit), send(grad_seven, end_bit)
    grad_four, grad_five, ones[4], ones[5] = back(4, 5, None, BF16)
    five, four = send(grad_five, end_bit), send(grad_four, end_bit)
    deep = shared_rows(experts) // 2
    dgate, keep, give = call(
        functools.partial(gate_back_kernel, experts, 512),
        [slots, spot, *x, dmix, centre, prob, tower_sums] + [kept[2] for kept in saved],
        [((2 * experts, 2 * rows), BF16, True)] + [((deep, 512), F32, True)] * 2,
        pin,
        5,
        [pltpu.VMEM((2 * experts, 2 * rows), F32), pltpu.VMEM((2 * deep, 512), F32)],
        2,
    )
    grad_two, grad_three, ones[2], ones[3] = back(2, 3, (six, seven), BF16)
    three, two = send(grad_three, mid_bit), send(grad_two, mid_bit)
    grad_zero, grad_one, ones[0], ones[1] = back(0, 1, None, F32)

    def add(values, dtypes):
        shape = values[0].shape
        return call(functools.partial(add_kernel, len(values)), values, [(shape, dtype, True) for dtype in dtypes], pin, 0.5)

    (keep,) = add([keep, swap(give)], [F32])
    for b in reversed(range(bits)):
        (keep,) = add([keep, send(keep, (b, b))], [F32])
    give = swap(keep)

    def input_gradient(side, added, dtype):
        (out,) = call(
            functools.partial(input_kernel, side, added is not None),
            [dgate, gate_rows, *ones, *pays] + ([] if added is None else [added]),
            [((rows, 512), dtype, False)],
            pin,
            5 * depth,
        )
        return out

    over = input_gradient(1, None, F32)

    (one,) = add([grad_one, five, three], [BF16])
    near = send(one, near_bit, True)
    zero, low_zero = add([grad_zero, four, two, send(one, near_bit, False)], [F32, BF16])
    if extra:
        (zero,) = add([zero, near], [F32])
        for at in reversed(extra):
            count = zero.shape[0] // 2
            zero = zero[:count] + send(zero[count:].astype(BF16), at).astype(F32)
        low_zero = zero.astype(BF16)
        near = jnp.zeros_like(low_zero)
    (final,) = add([zero, near, send(low_zero, (bits - 1, bits - 1), False)], [F32])

    input_grad = input_gradient(0, swap(over), F32)

    grad_w_first, grad_b_first, grad_w_second, grad_b_second = call(
        finish_kernel,
        [spot, final, swap(final)],
        [
            ((1, 512, 256), F32, False),
            ((1, 256), F32, False),
            ((1, 256, 128), F32, False),
            ((1, 128), F32, False),
        ],
        pin,
        2,
        scalars=1,
    )
    grad_gate, grad_gate_bias, tower_first, tower_bias, last, out_bias = call(
        functools.partial(finish_shared_kernel, experts),
        [spot, keep, give],
        [
            ((2, experts, 512), F32, False),
            ((2, experts), F32, False),
            ((2, 64, 128), F32, False),
            ((2, 64), F32, False),
            ((2, 64), F32, False),
            ((2, 64), F32, False),
        ],
        pin,
        1,
        [pltpu.VMEM((2 * deep, 512), F32)],
        1,
    )
    return (
        predictions,
        input_grad,
        grad_w_first,
        grad_b_first,
        grad_w_second,
        grad_b_second,
        jnp.transpose(grad_gate, (0, 2, 1)),
        grad_gate_bias,
        jnp.transpose(tower_first, (0, 2, 1)),
        tower_bias,
        last,
        out_bias[:, 0],
    )


def solution(mesh):
    in_specs = (
        P(("dp", "expert"), None),
        P("expert", None, None),
        P("expert", None),
        P("expert", None, None),
        P("expert", None),
        P(),
        P(),
        P(),
        P(),
        P(),
        P(),
        P(None, ("dp", "expert")),
        P(),
        P(),
    )
    out_specs = (
        P(None, ("dp", "expert")),
        P(("dp", "expert"), None),
        P("expert", None, None),
        P("expert", None),
        P("expert", None, None),
        P("expert", None),
        P(),
        P(),
        P(),
        P(),
        P(),
        P(),
    )
    return jax.shard_map(
        per_device, mesh=mesh, in_specs=in_specs, out_specs=out_specs, check_vma=False
    )
```

```python
import functools

import jax
import jax.numpy as jnp
from jax import lax
from jax.experimental import pallas as pl
from jax.experimental.pallas import tpu as pltpu
from jax.sharding import PartitionSpec as P

F32 = jnp.float32
BF16 = jnp.bfloat16
ROOT = 0.7978845608028654
CUBE = 0.044715
NN = (((1,), (0,)), ((), ()))
NT = (((1,), (1,)), ((), ()))
TN = (((0,), (0,)), ((), ()))
TT = (((0,), (1,)), ((), ()))
BIAS_ROWS = 16
SCALE = 1e9
EARLY = 2
TAIL = 10
PAIRS = ((0, 4), (1, 2), (5, 6), (3, 7))
PAY_ROWS = 320 + BIAS_ROWS
VMEM = pl.BlockSpec(memory_space=pltpu.VMEM)
SMEM = pl.BlockSpec(memory_space=pltpu.SMEM)
ANY = pl.BlockSpec(memory_space=pl.ANY)


def dot(a, b, dims):
    return lax.dot_general(a, b, dims, preferred_element_type=F32)


def gelu_pair(v):
    square = v * v
    upper = 0.5 + 0.5 * jnp.tanh(v * (ROOT + (ROOT * CUBE) * square))
    value = v * upper
    slope = upper + value * (1.0 - upper) * (2.0 * ROOT + (6.0 * ROOT * CUBE) * square)
    return value, slope


def call(name, kernel, ins, outs, pin, micros, scratch=(), scalars=0, limit=8, after=()):
    limit = limit if pin is not None else 60
    pinned = lambda a: pltpu.with_memory_space_constraint(a, pltpu.VMEM) if pin else a
    args = [a if n < scalars else pinned(a) for n, a in enumerate(ins)] + list(after)
    count = len(ins)
    body = kernel
    if after:

        def body(*refs):
            return kernel(*refs[:count], *refs[count + len(after) :])

    kept = pltpu.VMEM if pin else jax.ShapeDtypeStruct
    shapes = [(kept if stay else jax.ShapeDtypeStruct)(shape, dtype) for shape, dtype, stay in outs]
    return pl.pallas_call(
        body,
        name=name,
        in_specs=[SMEM] * scalars + [VMEM] * (count - scalars) + [ANY] * len(after),
        out_specs=[VMEM] * len(outs),
        out_shape=shapes,
        scratch_shapes=list(scratch),
        compiler_params=pltpu.CompilerParams(vmem_limit_bytes=limit * 2**20),
        cost_estimate=pl.CostEstimate(flops=int(micros * SCALE), bytes_accessed=0, transcendentals=0),
    )(*args)


def hold(value, after):
    count = len(after)
    return pl.pallas_call(
        lambda *refs: None,
        name="hold",
        in_specs=[ANY] * (1 + count),
        out_specs=ANY,
        out_shape=jax.ShapeDtypeStruct(value.shape, value.dtype),
        input_output_aliases={0: 0},
        compiler_params=pltpu.CompilerParams(vmem_limit_bytes=2**20),
        cost_estimate=pl.CostEstimate(flops=0, bytes_accessed=0, transcendentals=0),
    )(value, *after)


def to_column(row):
    n = row.shape[1]
    same = lax.broadcasted_iota(jnp.int32, (n, n), 0) == lax.broadcasted_iota(jnp.int32, (n, n), 1)
    return jnp.sum(jnp.where(same, jnp.broadcast_to(row, (n, n)), 0.0), axis=1, keepdims=True)


def side_by_side(columns, tall):
    lane = lax.broadcasted_iota(jnp.int32, (tall, 128), 1)
    small = jnp.zeros((tall, 128), F32)
    for n, col in enumerate(columns):
        small = jnp.where(lane == n, jnp.broadcast_to(col, (tall, 128)), small)
    return small


def fold(ref, base, block):
    deep = block.shape[0] // 4
    for k in range(4):
        ref[base : base + deep, 128 * k : 128 * (k + 1)] = block[deep * k : deep * (k + 1)]


def unfold(ref, base, deep):
    return jnp.concatenate(
        [ref[base : base + deep, 128 * k : 128 * (k + 1)] for k in range(4)], axis=0
    )


def pack_kernel(w1_ref, w2_ref, b1_ref, b2_ref, pay_ref):
    pay_ref[0, :256, :] = w1_ref[0].astype(F32).T.astype(BF16)
    second = w2_ref[0].astype(F32).T.astype(BF16)
    pay_ref[0, 256:320, :256] = second[:64]
    pay_ref[0, 256:320, 256:] = second[64:]
    row = jnp.concatenate(
        [b1_ref[...].astype(F32), b2_ref[...].astype(F32), jnp.zeros((1, 128), F32)], axis=1
    )
    pay_ref[0, 320:, :] = jnp.broadcast_to(row, (BIAS_ROWS, 512)).astype(BF16)


def biases(pay):
    flipped = pay[320:, :].astype(F32).T
    return flipped[:256, 0:1], flipped[256:384, 0:1]


def second_weight(pay):
    return jnp.concatenate([pay[256:320, :256], pay[256:320, 256:]], axis=0)


def gate_kernel(experts, groups, slot_ref, len_ref, shard_ref, where_ref, tob_ref, mine_ref, other_ref, gw_ref, gb_ref, *refs):
    prob_ref, low_ref, weight_ref, tob_out, scratch = refs
    for t in range(2):
        tob_out[t : t + 1, :] = jnp.full((1, 128), tob_ref[t], F32)
    rows = mine_ref.shape[0]
    for side, x_ref in enumerate((mine_ref, other_ref)):
        at = slice(side * rows, (side + 1) * rows)
        for t in range(2):
            part = dot(gw_ref[t], x_ref[...], NT) + to_column(gb_ref[t : t + 1, :].astype(F32))
            top = jnp.max(part, axis=0, keepdims=True)
            e = jnp.exp(part - top)
            scratch[t * experts : (t + 1) * experts, at] = e / jnp.sum(e, axis=0, keepdims=True)
        shard = where_ref[0] if side == 0 else 1 - where_ref[0]
        index = where_ref[1] * rows + lax.broadcasted_iota(jnp.int32, (1, rows), 1)
        start = jnp.int32(0)
        weight = jnp.zeros((1, rows), F32)
        for g in range(groups):
            size = jnp.where(shard_ref[g] == shard, len_ref[g], 0)
            inside = (index >= start) & (index < start + size)
            recip = 1.0 / jnp.full((1, rows), len_ref[g], jnp.int32).astype(F32)
            weight = weight + jnp.where(inside, recip, 0.0)
            start = start + size
        weight_ref[:, at] = weight
    for j in range(experts // 2):
        for t in range(2):
            row = scratch[pl.ds(t * experts + slot_ref[j], 1), :]
            prob_ref[j, t : t + 1, :] = row
            low_ref[j, t : t + 1, :] = row.astype(BF16).astype(F32)


def forward_kernel(bundles, first, chunk, mine_ref, other_ref, pay_a, pay_b, low_ref, *refs):
    if not first:
        mix_in, *refs = refs
    kept, mix_ref = (refs[:4], refs[4:8]), refs[8]
    rows = mine_ref.shape[0]
    depth = pay_a.shape[0]
    weights = {}
    for k in range(depth):
        for n, pay_ref in enumerate((pay_a, pay_b)):
            pay = pay_ref[k]
            weights[k, n] = (pay[:256], second_weight(pay), *biases(pay))
    work = [(c, k, n) for c in range(0, 2 * rows, chunk) for k in range(depth) for n in range(2)]
    totals = [None, None]

    def layer_one(c, k, n):
        ref, c = (mine_ref, c) if c < rows else (other_ref, c - rows)
        return dot(weights[k, n][0], ref[c : c + chunk, :], NT)

    def after_one(pre, c, k, n):
        value, slope = gelu_pair(pre + weights[k, n][2])
        hidden = value.astype(BF16)
        kept[n][0][k, :, c : c + chunk] = hidden
        kept[n][1][k, :, c : c + chunk] = slope.astype(kept[n][1].dtype)
        return hidden

    def after_two(pre, c, k, n):
        at = slice(c, c + chunk)
        value, slope = gelu_pair(pre + weights[k, n][3])
        out = value.astype(BF16)
        kept[n][2][k, :, at] = out
        kept[n][3][k, :, at] = slope.astype(kept[n][3].dtype)
        out = out.astype(F32)
        for t in range(2):
            term = low_ref[bundles[n] * depth + k, t : t + 1, at] * out
            if k == 0 and n == 0:
                totals[t] = term if first else mix_in[t, :, at] + term
            else:
                totals[t] = totals[t] + term
            if k == depth - 1 and n == 1:
                mix_ref[t, :, at] = totals[t].astype(mix_ref.dtype)

    ones, twos = {0: layer_one(*work[0])}, {}
    for i in range(len(work) + 1):
        if i + 1 < len(work):
            ones[i + 1] = layer_one(*work[i + 1])
        if i < len(work):
            hidden = after_one(ones.pop(i), *work[i])
        if i >= 1:
            after_two(twos.pop(i - 1), *work[i - 1])
        if i < len(work):
            twos[i] = dot(weights[work[i][1:]][1], hidden, NN)


def tower_kernel(
    chunk, mix_ref, come_ref, mine_ref, other_ref, weight_ref, tob_ref, tw_ref, tb_ref, tl_ref,
    pred_ref, dmix_ref, centre_ref, shared_ref,
):
    rows = mine_ref.shape[1]
    first = [jnp.zeros((64, 128), F32) for _ in range(2)]
    sums = [[jnp.zeros((64, 1), F32) for _ in range(3)] for _ in range(2)]
    tb = [to_column(tb_ref[t : t + 1, :].astype(F32)) for t in range(2)]
    tl = [to_column(tl_ref[t : t + 1, :].astype(F32)) for t in range(2)]
    for c in range(0, 2 * rows, chunk):
        at = slice(c, c + chunk)
        there = slice((c + rows) % (2 * rows), (c + rows) % (2 * rows) + chunk)
        ref, lo = (mine_ref, c) if c < rows else (other_ref, c - rows)
        for t in range(2):
            mixed = mix_ref[t, :, at].astype(F32) + come_ref[t, :, there].astype(F32)
            low = mixed.astype(BF16)
            act, slope = gelu_pair(dot(tw_ref[t], low, NN) + tb[t])
            score = jnp.sum(act * tl[t], axis=0, keepdims=True) + tob_ref[t : t + 1, 0:1]
            pred = 1.0 / (1.0 + jnp.exp(-score))
            d_score = weight_ref[:, at] * (pred - ref[t : t + 1, lo : lo + chunk].astype(F32))
            d_low = (d_score * tl[t] * slope).astype(BF16)
            d_mixed = dot(tw_ref[t], d_low, TN)
            dmix_ref[t, :, at] = d_mixed
            centre_ref[t : t + 1, at] = jnp.sum(d_mixed * mixed, axis=0, keepdims=True)
            if c < rows:
                pred_ref[t : t + 1, at] = pred
                first[t] = first[t] + dot(d_low, low, NT)
                sums[t][0] = sums[t][0] + jnp.sum(act * d_score, axis=1, keepdims=True)
                sums[t][1] = sums[t][1] + jnp.sum(d_low.astype(F32), axis=1, keepdims=True)
                total = jnp.sum(d_score, axis=1, keepdims=True)
                sums[t][2] = sums[t][2] + jnp.broadcast_to(total, (64, 1))
    for t in range(2):
        fold(shared_ref, 16 * t, first[t])
    fold(shared_ref, 32, side_by_side([sums[t][n] for n in range(3) for t in range(2)], 64))


def shared_rows(experts):
    return -(-(48 + 2 * experts + experts // 2) // 16) * 16


def gate_back_kernel(experts, chunk, slot_ref, spot_ref, mine_ref, other_ref, dmix_ref, centre_ref, prob_ref, tower_ref, *refs):
    outs = refs[:8]
    dgate_ref, keep_ref, give_ref, gates, shared_ref = refs[8:]
    rows = mine_ref.shape[0]
    depth = outs[0].shape[0]
    gates[...] = jnp.zeros_like(gates)
    for c in range(0, 2 * rows, chunk):
        at = slice(c, c + chunk)
        for j in range(8 * depth):
            out = outs[j // depth][j % depth, :, at].astype(F32)
            for t in range(2):
                d_prob = jnp.sum(dmix_ref[t, :, at] * out, axis=0, keepdims=True)
                d_gate = prob_ref[j, t : t + 1, at] * (d_prob - centre_ref[t : t + 1, at])
                gates[pl.ds(t * experts + slot_ref[j], 1), at] = d_gate
    low = gates[...].astype(BF16)
    dgate_ref[...] = low
    shared_ref[...] = jnp.zeros_like(shared_ref)
    shared_ref[:48, :] = tower_ref[...]
    grad = dot(low[:, :rows], mine_ref[...], NN) + dot(low[:, rows:], other_ref[...], NN)
    shared_ref[48 : 48 + 2 * experts, :] = grad
    bias = jnp.sum(low.astype(F32), axis=1, keepdims=True)
    fold(shared_ref, 48 + 2 * experts, side_by_side([bias], 2 * experts))
    deep = keep_ref.shape[0]
    keep_ref[...] = shared_ref[pl.ds(pl.multiple_of(spot_ref[0] * deep, 8), deep), :]
    give_ref[...] = shared_ref[pl.ds(pl.multiple_of((1 - spot_ref[0]) * deep, 8), deep), :]


def backward_kernel(bundles, add, chunk, mine_ref, other_ref, pay_a, pay_b, low_ref, dmix_ref, *refs):
    kept, refs = (refs[:3], refs[3:6]), refs[6:]
    if add:
        come, refs = refs[:2], refs[2:]
    grads, dones, d_two = refs[:2], refs[2:4], refs[4]
    rows = mine_ref.shape[0]
    depth = pay_a.shape[0]
    for k in range(depth):
        for n in range(2):
            h_ref, g1_ref, g2_ref = kept[n]
            j = bundles[n] * depth + k
            w2 = second_weight((pay_a, pay_b)[n][k])
            sum_one = jnp.zeros((256, 128), F32)
            sum_two = jnp.zeros((128, 128), F32)
            for c in range(0, 2 * rows, chunk):
                at = slice(c, c + chunk)
                d_out = low_ref[j, 0:1, at] * dmix_ref[0, :, at] + low_ref[j, 1:2, at] * dmix_ref[1, :, at]
                two = d_out.astype(BF16).astype(F32) * g2_ref[k, :, at].astype(F32)
                two_low = two.astype(BF16)
                d_two[n, :, at] = two_low
                one = dot(w2, two_low, TN) * g1_ref[k, :, at].astype(F32)
                dones[n][k, :, at] = one.astype(BF16)
                for m in range(0, chunk, 128):
                    sum_one = sum_one + one[:, m : m + 128]
                    sum_two = sum_two + two[:, m : m + 128]
            first = dot(dones[n][k, :, :rows], mine_ref[...], NN)
            first = first + dot(dones[n][k, :, rows:], other_ref[...], NN)
            second = dot(d_two[n], h_ref[k], NT)
            second = jnp.concatenate([second[:64], second[64:]], axis=1)
            row = jnp.concatenate(
                [
                    jnp.sum(sum_one.T, axis=0, keepdims=True),
                    jnp.sum(sum_two.T, axis=0, keepdims=True),
                    jnp.zeros((1, 128), F32),
                ],
                axis=1,
            )
            high = row.astype(BF16).astype(F32)
            index = lax.broadcasted_iota(jnp.int32, (BIAS_ROWS, 512), 0)
            both = jnp.where(index == 0, high, jnp.where(index == 1, row - high, 0.0))
            if add:
                first = first + come[n][k, :256, :].astype(F32)
                second = second + come[n][k, 256:320, :].astype(F32)
                both = both + come[n][k, 320:, :].astype(F32)
            grads[n][k, :256, :] = first.astype(grads[n].dtype)
            grads[n][k, 256:320, :] = second.astype(grads[n].dtype)
            grads[n][k, 320:, :] = both.astype(grads[n].dtype)


def input_kernel(bundles, chunk, dgate_ref, gw_ref, *refs):
    experts = gw_ref.shape[1]
    count = len(bundles)
    ones, pays, outs = refs[:count], refs[count : 2 * count], refs[2 * count :]
    for side, out_ref in enumerate(outs):
        rows = out_ref.shape[0]
        for c in range(0, rows, chunk):
            at = slice(side * rows + c, side * rows + c + chunk)
            total = dot(dgate_ref[:experts, at], gw_ref[0], TN) + dot(dgate_ref[experts:, at], gw_ref[1], TN)
            for one, pay in zip(ones, pays):
                for k in range(one.shape[0]):
                    total = total + dot(one[k, :, at], pay[k, :256, :], TN)
            out_ref[c : c + chunk, :] = total


def input_rest_kernel(bundles, chunk, *refs):
    count = len(bundles)
    ones, pays, befores, outs = refs[:count], refs[count : 2 * count], refs[2 * count : 2 * count + 2], refs[-2:]
    for side, (before, out_ref) in enumerate(zip(befores, outs)):
        rows = out_ref.shape[0]
        for c in range(0, rows, chunk):
            at = slice(side * rows + c, side * rows + c + chunk)
            total = before[c : c + chunk, :]
            for one, pay in zip(ones, pays):
                for k in range(one.shape[0]):
                    total = total + dot(one[k, :, at], pay[k, :256, :], TN)
            out_ref[c : c + chunk, :] = total


def add_kernel(count, *refs):
    total = refs[0][...].astype(F32)
    for ref in refs[1:count]:
        total = total + ref[...].astype(F32)
    for ref in refs[count:]:
        ref[...] = total.astype(ref.dtype)


def finish_kernel(owner_ref, mine_ref, come_ref, w1_ref, b1_ref, w2_ref, b2_ref):
    owner = owner_ref[2] == 1
    mine_ref, come_ref = mine_ref.at[0], come_ref.at[0]
    w1_ref[0] = jnp.where(owner, mine_ref[:256, :], come_ref[:256, :]).T
    second = jnp.where(owner, mine_ref[256:320, :], come_ref[256:320, :])
    w2_ref[0] = jnp.concatenate([second[:, :256], second[:, 256:]], axis=0).T
    bias = jnp.where(owner, mine_ref[320:328, :], come_ref[320:328, :])
    bias = bias[0:1] + bias[1:2]
    b1_ref[...] = bias[:, :256]
    b2_ref[...] = bias[:, 256:384]


def finish_shared_kernel(experts, spot_ref, keep_ref, give_ref, gate_ref, gate_bias_ref, first_ref, tb_ref, tl_ref, tob_ref, shared_ref):
    base = 48 + 2 * experts
    deep = keep_ref.shape[0]
    shared_ref[pl.ds(pl.multiple_of(spot_ref[0] * deep, 8), deep), :] = keep_ref[...]
    shared_ref[pl.ds(pl.multiple_of((1 - spot_ref[0]) * deep, 8), deep), :] = give_ref[...]
    for t in range(2):
        gate_ref[t] = shared_ref[48 + t * experts : 48 + (t + 1) * experts, :]
        first_ref[t] = unfold(shared_ref, 16 * t, 16)
    small = unfold(shared_ref, 32, 16).T
    tl_ref[...] = small[0:2, :]
    tb_ref[...] = small[2:4, :]
    tob_ref[...] = small[4:6, :]
    bias = unfold(shared_ref, base, experts // 2).T
    gate_bias_ref[0:1, :] = bias[0:1, :experts]
    gate_bias_ref[1:2, :] = bias[0:1, experts:]


def per_device(
    inputs,
    w_first,
    b_first,
    w_second,
    b_second,
    gate_weight,
    gate_bias,
    tower_first_weight,
    tower_first_bias,
    tower_last,
    tower_out_bias,
    labels,
    group_len,
    group_shard,
):
    rows = inputs.shape[0]
    experts = lax.axis_size("expert")
    half = experts // 2
    bits = experts.bit_length() - 1
    depth = half // 8
    pin = True if depth == 1 else None
    chunk = 256 if pin else 512
    core = lax.axis_index("dp")
    place = lax.axis_index("expert")
    owner = core == place // half
    near_bit, mid_bit, end_bit = (2, 2), (1, 0), (0, 1)
    extra = [(b, b) for b in range(bits - 2, 2, -1)]

    def pairs(bit_of_core, want=None):
        return [
            (c * experts + q, c * experts + (q ^ (1 << bit_of_core[c])))
            for c in range(2)
            for q in range(experts)
            if want is None or (c == q // half) == want
        ]

    def send(name, value, bit_of_core, want=None):
        with jax.named_scope(name):
            return lax.ppermute(value, ("dp", "expert"), pairs(bit_of_core, want))

    def swap(name, value):
        with jax.named_scope(name):
            return lax.ppermute(value, "dp", [(0, 1), (1, 0)])

    def deal(value):
        route = []
        for c in range(2):
            for q in range(experts):
                target = c * experts + (q ^ half) if c == q // half else (1 - c) * experts + q
                route.append((c * experts + q, target))
        with jax.named_scope("deal"):
            return lax.ppermute(value, ("dp", "expert"), route)

    def expert_mask(c, j):
        bundle, inner = j // depth, j % depth
        found = sum(1 << extra[e][c] for e in range(len(extra)) if (inner >> e) & 1)
        for n, at in enumerate((near_bit, mid_bit, end_bit)):
            found |= ((bundle >> n) & 1) << at[c]
        return found

    masks = [jnp.array([expert_mask(c, j) for j in range(half)], jnp.int32) for c in range(2)]
    spot = jnp.stack([core, place, owner.astype(jnp.int32)]).astype(jnp.int32)
    slots = core * half + ((place % half) ^ jnp.where(core == 0, masks[0], masks[1]))

    (pay,) = call(
        "pack", pack_kernel, [w_first, w_second, b_first, b_second], [((1, PAY_ROWS, 512), BF16, False)], pin, 1.5
    )
    zero = deal(pay)
    for at in extra:
        zero = jnp.concatenate([zero, send("pay_extra", zero, at)], axis=0)
    x = [inputs, swap("inputs", inputs)]
    other_labels = swap("labels", labels)
    gate_rows = jnp.transpose(gate_weight, (0, 2, 1))
    prob, low, weights, tob = call(
        "gate",
        functools.partial(gate_kernel, experts, group_len.shape[0]),
        [slots, group_len, group_shard, spot, tower_out_bias.astype(F32), *x, gate_rows, gate_bias],
        [((half, 2, 2 * rows), F32, True)] * 2 + [((1, 2 * rows), F32, True), ((2, 128), F32, True)],
        pin,
        4,
        [pltpu.VMEM((2 * experts, 2 * rows), F32)],
        5,
    )

    pays = [hold(zero, [low])] + [None] * 7
    pays[1] = send("pay_1", pays[0], near_bit)
    pays[2] = send("pay_2", pays[0], mid_bit)
    pays[4] = send("pay_4", pays[0], end_bit)
    held = hold(pays[1], [pays[2], pays[4]])
    pays[3] = send("pay_3", held, mid_bit)
    pays[5] = send("pay_5", held, end_bit)
    pays[6] = send("pay_6", pays[2], end_bit)
    pays[7] = send("pay_7", pays[3], end_bit)

    mixed = None
    saved = [None] * 8
    slope_type = F32 if pin else BF16
    for a, b in PAIRS:
        shape = lambda deep, dtype: ((depth, deep, 2 * rows), dtype, True)
        *kept, mixed = call(
            f"forward_{a}{b}",
            functools.partial(forward_kernel, (a, b), mixed is None, chunk),
            [*x, pays[a], pays[b], low] + ([] if mixed is None else [mixed]),
            [shape(256, BF16), shape(256, BF16), shape(128, BF16), shape(128, slope_type)] * 2
            + [((2, 128, 2 * rows), BF16 if (a, b) == PAIRS[-1] else F32, True)],
            pin,
            4.5 * depth,
        )
        saved[a], saved[b] = kept[:4], kept[4:]

    predictions, dmix, centre, tower_sums = call(
        "tower",
        functools.partial(tower_kernel, 512),
        [mixed, swap("mixed", mixed), labels, other_labels, weights, tob]
        + [jnp.transpose(tower_first_weight, (0, 2, 1)), tower_first_bias, tower_last],
        [
            ((2, rows), F32, False),
            ((2, 128, 2 * rows), F32, True),
            ((2, 2 * rows), F32, True),
            ((48, 512), F32, True),
        ],
        pin,
        4,
    )

    def back(a, b, come, dtype, cost, after=()):
        grad = ((depth, PAY_ROWS, 512), dtype, False)
        done = ((depth, 256, 2 * rows), BF16, True)
        return call(
            f"backward_{a}{b}",
            functools.partial(backward_kernel, (a, b), come is not None, chunk),
            [*x, pays[a], pays[b], low, dmix]
            + [saved[n][m] for n in (a, b) for m in (0, 1, 3)]
            + list(come or ()),
            [grad, grad, done, done],
            pin,
            cost,
            [pltpu.VMEM((2, 128, 2 * rows), BF16)],
            after=after,
        )

    ones = [None] * 8
    grad_six, grad_seven, ones[6], ones[7] = back(6, 7, None, BF16, 5)
    six, seven = send("grad_six", grad_six, end_bit), send("grad_seven", grad_seven, end_bit)
    grad_four, grad_five, ones[4], ones[5] = back(4, 5, None, BF16, 1, [ones[7]])
    five, four = send("grad_five", grad_five, end_bit), send("grad_four", grad_four, end_bit)
    deep = shared_rows(experts) // 2
    dgate, keep, give = call(
        "gate_back",
        functools.partial(gate_back_kernel, experts, 512),
        [slots, spot, *x, dmix, centre, prob, tower_sums] + [kept[2] for kept in saved],
        [((2 * experts, 2 * rows), BF16, True)] + [((deep, 512), F32, True)] * 2,
        pin,
        1,
        [pltpu.VMEM((2 * experts, 2 * rows), F32), pltpu.VMEM((2 * deep, 512), F32)],
        2,
        after=[ones[5]],
    )
    grad_two, grad_three, ones[2], ones[3] = back(2, 3, (six, seven), BF16, 1, [dgate])
    three, two = send("grad_three", grad_three, mid_bit), send("grad_two", grad_two, mid_bit)
    def add(values, dtypes, after=()):
        shape = values[0].shape
        outs = [(shape, dtype, True) for dtype in dtypes]
        return call("add", functools.partial(add_kernel, len(values)), values, outs, pin, 0, after=after)

    (keep,) = add([keep, swap("give", give)], [F32], [ones[3]])
    stages = []
    for b in reversed(range(bits)):
        (keep,) = add([keep, send(f"shared_{b}", keep, (b, b))], [F32])
        stages.append(keep)
    give = swap("keep", keep)

    halves = [((rows, 512), F32, True)] * 2
    early, late = (2, 3, 4, 5, 6, 7), (0, 1)
    parts = call(
        "input_early",
        functools.partial(input_kernel, early, chunk),
        [dgate, gate_rows] + [ones[n] for n in early] + [pays[n] for n in early],
        halves,
        pin,
        EARLY * depth,
    )
    grad_zero, grad_one, ones[0], ones[1] = back(0, 1, (four, five), F32, 5, [parts[0], stages[0]])
    own, over = call(
        "input_late",
        functools.partial(input_rest_kernel, late, chunk),
        [ones[n] for n in late] + [pays[n] for n in late] + list(parts),
        halves,
        pin,
        2.5 * depth,
        after=[stages[1]],
    )

    (one,) = add([grad_one, three], [BF16], [over])
    near = send("near", one, near_bit, True)
    zero, low_zero = add([grad_zero, two, send("pass", one, near_bit, False)], [F32, BF16], [stages[2]])
    if extra:
        (zero,) = add([zero, near], [F32])
        for at in reversed(extra):
            count = zero.shape[0] // 2
            zero = zero[:count] + send("extra", zero[count:].astype(BF16), at).astype(F32)
        low_zero = zero.astype(BF16)
        near = jnp.zeros_like(low_zero)
    (final,) = add([zero, near, send("far", low_zero, (bits - 1, bits - 1), False)], [F32], [stages[3]])

    come = swap("over", over)
    (input_grad,) = call(
        "input_sum", functools.partial(add_kernel, 2), [own, come], [((rows, 512), F32, False)], pin, 1.5
    )

    grad_w_first, grad_b_first, grad_w_second, grad_b_second = call(
        "finish",
        finish_kernel,
        [spot, final, swap("final", final)],
        [
            ((1, 512, 256), F32, False),
            ((1, 256), F32, False),
            ((1, 256, 128), F32, False),
            ((1, 128), F32, False),
        ],
        pin,
        TAIL,
        scalars=1,
    )
    grad_gate, grad_gate_bias, tower_first, tower_bias, last, out_bias = call(
        "finish_shared",
        functools.partial(finish_shared_kernel, experts),
        [spot, keep, give],
        [
            ((2, experts, 512), F32, False),
            ((2, experts), F32, False),
            ((2, 64, 128), F32, False),
            ((2, 64), F32, False),
            ((2, 64), F32, False),
            ((2, 64), F32, False),
        ],
        pin,
        1,
        [pltpu.VMEM((2 * deep, 512), F32)],
        1,
    )
    return (
        predictions,
        input_grad,
        grad_w_first,
        grad_b_first,
        grad_w_second,
        grad_b_second,
        jnp.transpose(grad_gate, (0, 2, 1)),
        grad_gate_bias,
        jnp.transpose(tower_first, (0, 2, 1)),
        tower_bias,
        last,
        out_bias[:, 0],
    )


def solution(mesh):
    in_specs = (
        P(("dp", "expert"), None),
        P("expert", None, None),
        P("expert", None),
        P("expert", None, None),
        P("expert", None),
        P(),
        P(),
        P(),
        P(),
        P(),
        P(),
        P(None, ("dp", "expert")),
        P(),
        P(),
    )
    out_specs = (
        P(None, ("dp", "expert")),
        P(("dp", "expert"), None),
        P("expert", None, None),
        P("expert", None),
        P("expert", None, None),
        P("expert", None),
        P(),
        P(),
        P(),
        P(),
        P(),
        P(),
    )
    return jax.shard_map(
        per_device, mesh=mesh, in_specs=in_specs, out_specs=out_specs, check_vma=False
    )
```

```python
import functools

import jax
import jax.numpy as jnp
from jax import lax
from jax.experimental import pallas as pl
from jax.experimental.pallas import tpu as pltpu
from jax.sharding import PartitionSpec as P

F32 = jnp.float32
BF16 = jnp.bfloat16
ROOT = 0.7978845608028654
CUBE = 0.044715
NN = (((1,), (0,)), ((), ()))
NT = (((1,), (1,)), ((), ()))
TN = (((0,), (0,)), ((), ()))
TT = (((0,), (1,)), ((), ()))
BIAS_ROWS = 16
SCALE = 3e8
EARLY = 6
BACK_CHUNK = 2048
TAIL = 10
PAIRS = ((0, 4), (1, 2), (5, 6), (3, 7))
PAY_ROWS = 320 + BIAS_ROWS
VMEM = pl.BlockSpec(memory_space=pltpu.VMEM)
SMEM = pl.BlockSpec(memory_space=pltpu.SMEM)
ANY = pl.BlockSpec(memory_space=pl.ANY)


def dot(a, b, dims):
    return lax.dot_general(a, b, dims, preferred_element_type=F32)


def gelu_pair(v):
    square = v * v
    upper = 0.5 + 0.5 * jnp.tanh(v * (ROOT + (ROOT * CUBE) * square))
    value = v * upper
    slope = upper + value * (1.0 - upper) * (2.0 * ROOT + (6.0 * ROOT * CUBE) * square)
    return value, slope


def call(name, kernel, ins, outs, pin, micros, scratch=(), scalars=0, limit=8, after=()):
    limit = limit if pin is not None else 60
    pinned = lambda a: pltpu.with_memory_space_constraint(a, pltpu.VMEM) if pin else a
    args = [a if n < scalars else pinned(a) for n, a in enumerate(ins)] + list(after)
    count = len(ins)
    body = kernel
    if after:

        def body(*refs):
            return kernel(*refs[:count], *refs[count + len(after) :])

    kept = pltpu.VMEM if pin else jax.ShapeDtypeStruct
    shapes = [(kept if stay else jax.ShapeDtypeStruct)(shape, dtype) for shape, dtype, stay in outs]
    return pl.pallas_call(
        body,
        name=name,
        in_specs=[SMEM] * scalars + [VMEM] * (count - scalars) + [ANY] * len(after),
        out_specs=[VMEM] * len(outs),
        out_shape=shapes,
        scratch_shapes=list(scratch),
        compiler_params=pltpu.CompilerParams(vmem_limit_bytes=limit * 2**20),
        cost_estimate=pl.CostEstimate(flops=int(micros * SCALE), bytes_accessed=0, transcendentals=0),
    )(*args)


def hold(value, after):
    count = len(after)
    return pl.pallas_call(
        lambda *refs: None,
        name="hold",
        in_specs=[ANY] * (1 + count),
        out_specs=ANY,
        out_shape=jax.ShapeDtypeStruct(value.shape, value.dtype),
        input_output_aliases={0: 0},
        compiler_params=pltpu.CompilerParams(vmem_limit_bytes=2**20),
        cost_estimate=pl.CostEstimate(flops=0, bytes_accessed=0, transcendentals=0),
    )(value, *after)


def slot_of(masks, int_ref, j):
    half = len(masks[0])
    mask = jnp.where(int_ref[0] == 0, masks[0][j], masks[1][j])
    return int_ref[0] * half + ((int_ref[1] & (half - 1)) ^ mask)


def to_column(row):
    n = row.shape[1]
    same = lax.broadcasted_iota(jnp.int32, (n, n), 0) == lax.broadcasted_iota(jnp.int32, (n, n), 1)
    return jnp.sum(jnp.where(same, jnp.broadcast_to(row, (n, n)), 0.0), axis=1, keepdims=True)


def side_by_side(columns, tall):
    lane = lax.broadcasted_iota(jnp.int32, (tall, 128), 1)
    small = jnp.zeros((tall, 128), F32)
    for n, col in enumerate(columns):
        small = jnp.where(lane == n, jnp.broadcast_to(col, (tall, 128)), small)
    return small


def fold(ref, base, block):
    deep = block.shape[0] // 4
    for k in range(4):
        ref[base : base + deep, 128 * k : 128 * (k + 1)] = block[deep * k : deep * (k + 1)]


def unfold(ref, base, deep):
    return jnp.concatenate(
        [ref[base : base + deep, 128 * k : 128 * (k + 1)] for k in range(4)], axis=0
    )


def pack_kernel(w1_ref, w2_ref, b1_ref, b2_ref, pay_ref, w1, w2, b1, b2, sems):
    copies = [
        pltpu.make_async_copy(src, dst, sems.at[n])
        for n, (src, dst) in enumerate(((w1_ref, w1), (w2_ref, w2), (b1_ref, b1), (b2_ref, b2)))
    ]
    for copy in copies:
        copy.start()
    for copy in copies[1:]:
        copy.wait()
    second = w2[0].astype(F32).T.astype(BF16)
    pay_ref[0, 256:320, :256] = second[:64]
    pay_ref[0, 256:320, 256:] = second[64:]
    row = jnp.concatenate([b1[...].astype(F32), b2[...].astype(F32), jnp.zeros((1, 128), F32)], axis=1)
    pay_ref[0, 320:, :] = jnp.broadcast_to(row, (BIAS_ROWS, 512)).astype(BF16)
    copies[0].wait()
    pay_ref[0, :256, :] = w1[0].astype(F32).T.astype(BF16)


def pack(w1, w2, b1, b2):
    arrays = (w1, w2, b1, b2)
    return pl.pallas_call(
        pack_kernel,
        name="pack",
        in_specs=[pl.BlockSpec(memory_space=pltpu.HBM)] * 4,
        out_specs=VMEM,
        out_shape=jax.ShapeDtypeStruct((1, PAY_ROWS, 512), BF16),
        scratch_shapes=[pltpu.VMEM(a.shape, a.dtype) for a in arrays] + [pltpu.SemaphoreType.DMA((4,))],
        compiler_params=pltpu.CompilerParams(vmem_limit_bytes=8 * 2**20),
        cost_estimate=pl.CostEstimate(flops=0, bytes_accessed=0, transcendentals=0),
    )(*[pltpu.with_memory_space_constraint(a, pltpu.HBM) for a in arrays])


def biases(pay):
    flipped = pay[320:, :].astype(F32).T
    return flipped[:256, 0:1], flipped[256:384, 0:1]


def second_weight(pay):
    return jnp.concatenate([pay[256:320, :256], pay[256:320, 256:]], axis=0)


def gate_kernel(masks, groups, int_ref, label_ref, there_ref, gw_ref, gb_ref, mine_ref, other_ref, *refs):
    prob_ref, low_ref, weight_ref, x_out, label_out, scratch, sems = refs
    rows = mine_ref.shape[0]
    experts = 2 * len(masks[0])
    copies = [
        pltpu.make_async_copy(src, x_out.at[pl.ds(n * rows, rows), :], sems.at[n])
        for n, src in enumerate((mine_ref, other_ref))
    ]
    for copy in copies:
        copy.start()
    for side in range(2):
        at = slice(side * rows, (side + 1) * rows)
        label_out[:, at] = (label_ref, there_ref)[side][...].astype(F32)
        copies[side].wait()
        for t in range(2):
            part = dot(gw_ref[t], x_out[at, :], NT) + to_column(gb_ref[t : t + 1, :].astype(F32))
            top = jnp.max(part, axis=0, keepdims=True)
            e = jnp.exp(part - top)
            scratch[t * experts : (t + 1) * experts, at] = e / jnp.sum(e, axis=0, keepdims=True)
        shard = int_ref[0] if side == 0 else 1 - int_ref[0]
        index = int_ref[1] * rows + lax.broadcasted_iota(jnp.int32, (1, rows), 1)
        start = jnp.int32(0)
        weight = jnp.zeros((1, rows), F32)
        for g in range(groups):
            length = int_ref[3 + groups + g]
            size = jnp.where(int_ref[3 + g] == shard, length, 0)
            inside = (index >= start) & (index < start + size)
            recip = 1.0 / jnp.full((1, rows), length, jnp.int32).astype(F32)
            weight = weight + jnp.where(inside, recip, 0.0)
            start = start + size
        weight_ref[:, at] = weight
    for j in range(experts // 2):
        slot = slot_of(masks, int_ref, j)
        for t in range(2):
            row = scratch[pl.ds(t * experts + slot, 1), :]
            prob_ref[j, t : t + 1, :] = row
            low_ref[j, t : t + 1, :] = row.astype(BF16).astype(F32)


def forward_kernel(bundles, first, block, chunk, x_ref, pay_a, pay_b, low_ref, *refs):
    if not first:
        mix_in, *refs = refs
    kept, mix_ref = (refs[:4], refs[4:8]), refs[8]
    depth = pay_a.shape[0]
    weights = {}
    for k in range(depth):
        for n, pay_ref in enumerate((pay_a, pay_b)):
            pay = pay_ref[k]
            weights[k, n] = (pay[:256], second_weight(pay), *biases(pay))
    work = [(c, k, n) for c in range(0, block, chunk) for k in range(depth) for n in range(2)]

    def step(i, _):
        base = pl.multiple_of(i * block, block)
        totals = [None, None]

        def layer_one(c, k, n):
            return dot(weights[k, n][0], x_ref[pl.ds(base + c, chunk), :], NT)

        def after_one(pre, c, k, n):
            value, slope = gelu_pair(pre + weights[k, n][2])
            hidden = value.astype(BF16)
            kept[n][0][k, :, pl.ds(base + c, chunk)] = hidden
            kept[n][1][k, :, pl.ds(base + c, chunk)] = slope.astype(kept[n][1].dtype)
            return hidden

        def after_two(pre, c, k, n):
            at = pl.ds(base + c, chunk)
            value, slope = gelu_pair(pre + weights[k, n][3])
            out = value.astype(BF16)
            kept[n][2][k, :, at] = out
            kept[n][3][k, :, at] = slope.astype(kept[n][3].dtype)
            out = out.astype(F32)
            for t in range(2):
                term = low_ref[bundles[n] * depth + k, t : t + 1, at] * out
                if k == 0 and n == 0:
                    totals[t] = term if first else mix_in[t, :, at] + term
                else:
                    totals[t] = totals[t] + term
                if k == depth - 1 and n == 1:
                    mix_ref[t, :, at] = totals[t].astype(mix_ref.dtype)

        ones, twos = {0: layer_one(*work[0])}, {}
        for i in range(len(work) + 1):
            if i + 1 < len(work):
                ones[i + 1] = layer_one(*work[i + 1])
            if i < len(work):
                hidden = after_one(ones.pop(i), *work[i])
            if i >= 1:
                after_two(twos.pop(i - 1), *work[i - 1])
            if i < len(work):
                twos[i] = dot(weights[work[i][1:]][1], hidden, NN)
        return 0

    lax.fori_loop(0, x_ref.shape[0] // block, step, 0)


def tower_kernel(
    chunk, mix_ref, come_ref, label_ref, weight_ref, tob_ref, tw_ref, tb_ref, tl_ref,
    pred_ref, dmix_ref, centre_ref, shared_ref, first, sums,
):
    rows = pred_ref.shape[1]
    first[...] = jnp.zeros_like(first)
    sums[...] = jnp.zeros_like(sums)
    tb = [to_column(tb_ref[t : t + 1, :].astype(F32)) for t in range(2)]
    tl = [to_column(tl_ref[t : t + 1, :].astype(F32)) for t in range(2)]

    def step(side, i, _):
        at = pl.ds(pl.multiple_of(side * rows + i * chunk, chunk), chunk)
        there = pl.ds(pl.multiple_of((1 - side) * rows + i * chunk, chunk), chunk)
        cols = []
        for t in range(2):
            mixed = mix_ref[t, :, at].astype(F32) + come_ref[t, :, there].astype(F32)
            low = mixed.astype(BF16)
            act, slope = gelu_pair(dot(tw_ref[t], low, NN) + tb[t])
            score = jnp.sum(act * tl[t], axis=0, keepdims=True) + tob_ref[0:1, t : t + 1].astype(F32)
            pred = 1.0 / (1.0 + jnp.exp(-score))
            d_score = weight_ref[:, at] * (pred - label_ref[t : t + 1, at])
            d_low = (d_score * tl[t] * slope).astype(BF16)
            d_mixed = dot(tw_ref[t], d_low, TN)
            dmix_ref[t, :, at] = d_mixed
            centre_ref[t : t + 1, at] = jnp.sum(d_mixed * mixed, axis=0, keepdims=True)
            if side == 0:
                pred_ref[t : t + 1, at] = pred
                first[t] += dot(d_low, low, NT)
                cols.append(jnp.sum(act * d_score, axis=1, keepdims=True))
                cols.append(jnp.sum(d_low.astype(F32), axis=1, keepdims=True))
                total = jnp.sum(d_score, axis=1, keepdims=True)
                cols.append(jnp.broadcast_to(total, (64, 1)))
        if side == 0:
            sums[...] += side_by_side([cols[3 * t + n] for n in range(3) for t in range(2)], 64)
        return 0

    lax.fori_loop(0, rows // chunk, functools.partial(step, 0), 0)
    lax.fori_loop(0, rows // chunk, functools.partial(step, 1), 0)
    for t in range(2):
        fold(shared_ref, 16 * t, first[t])
    fold(shared_ref, 32, sums[...])


def shared_rows(experts):
    return -(-(48 + 2 * experts + experts // 2) // 16) * 16


def gate_back_kernel(masks, chunk, spot_ref, x_ref, dmix_ref, centre_ref, prob_ref, tower_ref, *refs):
    outs = refs[:8]
    dgate_ref, keep_ref, give_ref, gates, shared_ref = refs[8:]
    depth = outs[0].shape[0]
    experts = 2 * len(masks[0])
    gates[...] = jnp.zeros_like(gates)

    def step(i, _):
        at = pl.ds(pl.multiple_of(i * chunk, chunk), chunk)
        for j in range(8 * depth):
            out = outs[j // depth][j % depth, :, at].astype(F32)
            slot = slot_of(masks, spot_ref, j)
            for t in range(2):
                d_prob = jnp.sum(dmix_ref[t, :, at] * out, axis=0, keepdims=True)
                d_gate = prob_ref[j, t : t + 1, at] * (d_prob - centre_ref[t : t + 1, at])
                gates[pl.ds(t * experts + slot, 1), at] = d_gate
        return 0

    lax.fori_loop(0, x_ref.shape[0] // chunk, step, 0)
    low = gates[...].astype(BF16)
    dgate_ref[...] = low
    shared_ref[...] = jnp.zeros_like(shared_ref)
    shared_ref[:48, :] = tower_ref[...]
    shared_ref[48 : 48 + 2 * experts, :] = dot(low, x_ref[...], NN)
    bias = jnp.sum(low.astype(F32), axis=1, keepdims=True)
    fold(shared_ref, 48 + 2 * experts, side_by_side([bias], 2 * experts))
    deep = keep_ref.shape[0]
    keep_ref[...] = shared_ref[pl.ds(pl.multiple_of(spot_ref[0] * deep, 8), deep), :]
    give_ref[...] = shared_ref[pl.ds(pl.multiple_of((1 - spot_ref[0]) * deep, 8), deep), :]


def backward_kernel(bundles, add, block, x_ref, pay_a, pay_b, low_ref, dmix_ref, *refs):
    kept, refs = (refs[:3], refs[3:6]), refs[6:]
    if add:
        come, refs = refs[:2], refs[2:]
    grads, dones, d_two, sums = refs[:2], refs[2:4], refs[4], refs[5]
    depth = pay_a.shape[0]
    for k in range(depth):
        weights = [second_weight(pay[k]) for pay in (pay_a, pay_b)]
        sums[...] = jnp.zeros_like(sums)

        def step(i, _, k=k, weights=weights):
            at = pl.ds(pl.multiple_of(i * block, block), block)
            for n in range(2):
                _, g1_ref, g2_ref = kept[n]
                j = bundles[n] * depth + k
                d_out = low_ref[j, 0:1, at] * dmix_ref[0, :, at] + low_ref[j, 1:2, at] * dmix_ref[1, :, at]
                two = d_out.astype(BF16).astype(F32) * g2_ref[k, :, at].astype(F32)
                two_low = two.astype(BF16)
                d_two[n, :, at] = two_low
                one = dot(weights[n], two_low, TN) * g1_ref[k, :, at].astype(F32)
                dones[n][k, :, at] = one.astype(BF16)
                add_one, add_two = one[:, :128], two[:, :128]
                for m in range(128, block, 128):
                    add_one = add_one + one[:, m : m + 128]
                    add_two = add_two + two[:, m : m + 128]
                sums[n, :256] += add_one
                sums[n, 256:] += add_two
            return 0

        lax.fori_loop(0, x_ref.shape[0] // block, step, 0)
        for n in range(2):
            h_ref = kept[n][0]
            first = dot(dones[n][k], x_ref[...], NN)
            second = dot(d_two[n], h_ref[k], NT)
            second = jnp.concatenate([second[:64], second[64:]], axis=1)
            row = jnp.concatenate(
                [
                    jnp.sum(sums[n].T, axis=0, keepdims=True),
                    jnp.zeros((1, 128), F32),
                ],
                axis=1,
            )
            high = row.astype(BF16).astype(F32)
            index = lax.broadcasted_iota(jnp.int32, (BIAS_ROWS, 512), 0)
            both = jnp.where(index == 0, high, jnp.where(index == 1, row - high, 0.0))
            if add:
                first = first + come[n][k, :256, :].astype(F32)
                second = second + come[n][k, 256:320, :].astype(F32)
                both = both + come[n][k, 320:, :].astype(F32)
            grads[n][k, :256, :] = first.astype(grads[n].dtype)
            grads[n][k, 256:320, :] = second.astype(grads[n].dtype)
            grads[n][k, 320:, :] = both.astype(grads[n].dtype)


def input_kernel(bundles, chunk, dgate_ref, gw_ref, *refs):
    experts = gw_ref.shape[1]
    count = len(bundles)
    ones, pays, outs = refs[:count], refs[count : 2 * count], refs[2 * count :]
    for side, out_ref in enumerate(outs):
        rows = out_ref.shape[0]

        def step(i, _, side=side, rows=rows, out_ref=out_ref):
            at = pl.ds(pl.multiple_of(side * rows + i * chunk, chunk), chunk)
            total = dot(dgate_ref[:experts, at], gw_ref[0], TN) + dot(dgate_ref[experts:, at], gw_ref[1], TN)
            for one, pay in zip(ones, pays):
                for k in range(one.shape[0]):
                    total = total + dot(one[k, :, at], pay[k, :256, :], TN)
            out_ref[pl.ds(pl.multiple_of(i * chunk, chunk), chunk), :] = total
            return 0

        lax.fori_loop(0, rows // chunk, step, 0)


def input_rest_kernel(bundles, chunk, *refs):
    count = len(bundles)
    ones, pays, befores, outs = refs[:count], refs[count : 2 * count], refs[2 * count : 2 * count + 2], refs[-2:]
    for side, (before, out_ref) in enumerate(zip(befores, outs)):
        rows = out_ref.shape[0]

        def step(i, _, side=side, rows=rows, before=before, out_ref=out_ref):
            at = pl.ds(pl.multiple_of(side * rows + i * chunk, chunk), chunk)
            here = pl.ds(pl.multiple_of(i * chunk, chunk), chunk)
            total = before[here, :]
            for one, pay in zip(ones, pays):
                for k in range(one.shape[0]):
                    total = total + dot(one[k, :, at], pay[k, :256, :], TN)
            out_ref[here, :] = total.astype(out_ref.dtype)
            return 0

        lax.fori_loop(0, rows // chunk, step, 0)


def add_kernel(count, *refs):
    total = refs[0][...].astype(F32)
    for ref in refs[1:count]:
        total = total + ref[...].astype(F32)
    for ref in refs[count:]:
        ref[...] = total.astype(ref.dtype)


def finish_kernel(owner_ref, mine_ref, come_ref, w1_ref, b1_ref, w2_ref, b2_ref):
    owner = owner_ref[2] == 1
    mine_ref, come_ref = mine_ref.at[0], come_ref.at[0]
    w1_ref[0] = jnp.where(owner, mine_ref[:256, :], come_ref[:256, :]).T
    second = jnp.where(owner, mine_ref[256:320, :], come_ref[256:320, :])
    w2_ref[0] = jnp.concatenate([second[:, :256], second[:, 256:]], axis=0).T
    bias = jnp.where(owner, mine_ref[320:328, :], come_ref[320:328, :])
    bias = bias[0:1] + bias[1:2]
    b1_ref[...] = bias[:, :256]
    b2_ref[...] = bias[:, 256:384]


def close_kernel(
    experts, spot_ref, keep_ref, give_ref,
    gate_ref, gate_bias_ref, first_ref, tb_ref, tl_ref, tob_ref, done_ref, shared_ref,
):

    base = 48 + 2 * experts
    deep = keep_ref.shape[0]
    shared_ref[pl.ds(pl.multiple_of(spot_ref[0] * deep, 8), deep), :] = keep_ref[...]
    shared_ref[pl.ds(pl.multiple_of((1 - spot_ref[0]) * deep, 8), deep), :] = give_ref[...]
    for t in range(2):
        gate_ref[t] = shared_ref[48 + t * experts : 48 + (t + 1) * experts, :]
        first_ref[t] = unfold(shared_ref, 16 * t, 16)
    small = unfold(shared_ref, 32, 16).T
    tl_ref[...] = small[0:2, :]
    tb_ref[...] = small[2:4, :]
    tob_ref[:, 0:1] = small[4:5, 0:1]
    tob_ref[:, 1:2] = small[5:6, 0:1]
    bias = unfold(shared_ref, base, experts // 2).T
    gate_bias_ref[0:1, :] = bias[0:1, :experts]
    gate_bias_ref[1:2, :] = bias[0:1, experts:]
    done_ref[...] = jnp.zeros_like(done_ref)


def per_device(
    inputs,
    w_first,
    b_first,
    w_second,
    b_second,
    gate_weight,
    gate_bias,
    tower_first_weight,
    tower_first_bias,
    tower_last,
    tower_out_bias,
    labels,
    group_len,
    group_shard,
):
    rows = inputs.shape[0]
    experts = lax.axis_size("expert")
    half = experts // 2
    bits = experts.bit_length() - 1
    depth = half // 8
    pin = True if depth == 1 else None
    chunk = 256 if pin else 512
    core = lax.axis_index("dp")
    place = lax.axis_index("expert")
    owner = core == place // half
    near_bit, mid_bit, end_bit = (2, 2), (1, 0), (0, 1)
    extra = [(b, b) for b in range(bits - 2, 2, -1)]

    def pairs(bit_of_core, want=None, also=0):
        return [
            (c * experts + q, c * experts + (q ^ (1 << bit_of_core[c]) ^ also))
            for c in range(2)
            for q in range(experts)
            if want is None or (c == q // half) == want
        ]

    def send(name, value, bit_of_core, want=None, also=0):
        with jax.named_scope(name):
            return lax.ppermute(value, ("dp", "expert"), pairs(bit_of_core, want, also))

    def swap(name, value):
        with jax.named_scope(name):
            return lax.ppermute(value, "dp", [(0, 1), (1, 0)])

    def deal(value):
        route = []
        for c in range(2):
            for q in range(experts):
                target = c * experts + (q ^ half) if c == q // half else (1 - c) * experts + q
                route.append((c * experts + q, target))
        with jax.named_scope("deal"):
            return lax.ppermute(value, ("dp", "expert"), route)

    def expert_mask(c, j):
        bundle, inner = j // depth, j % depth
        found = sum(1 << extra[e][c] for e in range(len(extra)) if (inner >> e) & 1)
        for n, at in enumerate((near_bit, mid_bit, end_bit)):
            found |= ((bundle >> n) & 1) << at[c]
        return found

    masks = [[expert_mask(c, j) for j in range(half)] for c in range(2)]
    spot = jnp.stack([core, place, owner.astype(jnp.int32)]).astype(jnp.int32)

    pay = pack(w_first, w_second, b_first, b_second)
    zero = deal(pay)
    for at in extra:
        zero = jnp.concatenate([zero, send("pay_extra", zero, at)], axis=0)
    labels_there = swap("labels", labels)
    inputs_there = swap("inputs", inputs)
    gate_rows = jnp.transpose(gate_weight, (0, 2, 1))
    ints = jnp.concatenate([spot, group_shard, group_len])
    outs = [((half, 2, 2 * rows), F32)] * 2 + [((1, 2 * rows), F32), ((2 * rows, 512), BF16), ((2, 2 * rows), F32)]
    kept = pltpu.VMEM if pin else jax.ShapeDtypeStruct
    prob, low, weights, x, both_labels = pl.pallas_call(
        functools.partial(gate_kernel, masks, group_len.shape[0]),
        name="gate",
        in_specs=[SMEM] + [VMEM] * 4 + [ANY] * 2,
        out_specs=[VMEM] * 5,
        out_shape=[kept(shape, dtype) for shape, dtype in outs],
        scratch_shapes=[pltpu.VMEM((2 * experts, 2 * rows), F32), pltpu.SemaphoreType.DMA((2,))],
        compiler_params=pltpu.CompilerParams(vmem_limit_bytes=(8 if pin else 60) * 2**20),
        cost_estimate=pl.CostEstimate(flops=0, bytes_accessed=0, transcendentals=0),
    )(ints, labels, labels_there, gate_rows, gate_bias, inputs, inputs_there)

    pays = [hold(zero, [low])] + [None] * 7
    pays[1] = send("pay_1", pays[0], near_bit)
    pays[2] = send("pay_2", pays[0], mid_bit)
    pays[4] = send("pay_4", pays[0], end_bit)
    held = hold(pays[1], [pays[2], pays[4]])
    pays[3] = send("pay_3", held, mid_bit)
    pays[5] = send("pay_5", held, end_bit)
    pays[6] = send("pay_6", pays[2], end_bit)

    mixed = None
    saved = [None] * 8
    slope_type = F32 if pin else BF16
    for a, b in PAIRS:
        shape = lambda deep, dtype: ((depth, deep, 2 * rows), dtype, True)
        *kept, mixed = call(
            f"forward_{a}{b}",
            functools.partial(forward_kernel, (a, b), mixed is None, 4 * chunk, chunk),
            [x, pays[a], pays[b], low] + ([] if mixed is None else [mixed]),
            [shape(256, BF16), shape(256, BF16), shape(128, BF16), shape(128, slope_type)] * 2
            + [((2, 128, 2 * rows), BF16 if (a, b) == PAIRS[-1] else F32, True)],
            pin,
            4.5 * depth,
        )
        saved[a], saved[b] = kept[:4], kept[4:]
        if pays[7] is None:
            pays[7] = send("pay_7", hold(pays[3], [mixed]), end_bit)

    predictions, dmix, centre, tower_sums = call(
        "tower",
        functools.partial(tower_kernel, 512),
        [mixed, swap("mixed", mixed), both_labels, weights, tower_out_bias[None]]
        + [jnp.transpose(tower_first_weight, (0, 2, 1)), tower_first_bias, tower_last],
        [
            ((2, rows), F32, False),
            ((2, 128, 2 * rows), F32, True),
            ((2, 2 * rows), F32, True),
            ((48, 512), F32, True),
        ],
        pin,
        4,
        [pltpu.VMEM((2, 64, 128), F32), pltpu.VMEM((64, 128), F32)],
    )

    def back(a, b, come, dtype, cost, after=()):
        grad = ((depth, PAY_ROWS, 512), dtype, False)
        done = ((depth, 256, 2 * rows), BF16, True)
        return call(
            f"backward_{a}{b}",
            functools.partial(backward_kernel, (a, b), come is not None, BACK_CHUNK),
            [x, pays[a], pays[b], low, dmix]
            + [saved[n][m] for n in (a, b) for m in (0, 1, 3)]
            + list(come or ()),
            [grad, grad, done, done],
            pin,
            cost,
            [pltpu.VMEM((2, 128, 2 * rows), BF16), pltpu.VMEM((2, 384, 128), F32)],
            after=after,
        )

    ones = [None] * 8
    grad_six, grad_seven, ones[6], ones[7] = back(6, 7, None, BF16, 5)
    six, seven = send("grad_six", grad_six, end_bit), send("grad_seven", grad_seven, end_bit)
    grad_four, grad_five, ones[4], ones[5] = back(4, 5, None, BF16, 1, [ones[7]])
    five, four = send("grad_five", grad_five, end_bit), send("grad_four", grad_four, end_bit)
    deep = shared_rows(experts) // 2
    dgate, keep, give = call(
        "gate_back",
        functools.partial(gate_back_kernel, masks, 512),
        [ints, x, dmix, centre, prob, tower_sums] + [kept[2] for kept in saved],
        [((2 * experts, 2 * rows), BF16, True)] + [((deep, 512), F32, True)] * 2,
        pin,
        1,
        [pltpu.VMEM((2 * experts, 2 * rows), F32), pltpu.VMEM((2 * deep, 512), F32)],
        1,
        after=[ones[5]],
    )
    grad_two, grad_three, ones[2], ones[3] = back(2, 3, (six, seven), BF16, 1, [dgate])
    three, two = send("grad_three", grad_three, mid_bit), send("grad_two", grad_two, mid_bit)
    halves = [((rows, 512), F32, True)] * 2
    early, late = (2, 3, 4, 5, 6, 7), (0, 1)
    parts = call(
        "input_early",
        functools.partial(input_kernel, early, 512),
        [dgate, gate_rows] + [ones[n] for n in early] + [pays[n] for n in early],
        halves,
        pin,
        EARLY * depth,
    )
    def add(values, dtypes, after=()):
        shape = values[0].shape
        outs = [(shape, dtype, True) for dtype in dtypes]
        return call("add", functools.partial(add_kernel, len(values)), values, outs, pin, 0, after=after)

    (keep,) = add([keep, swap("give", give)], [F32], [ones[3]])
    stages = []
    for b in range(2, bits):
        (keep,) = add([keep, send(f"shared_{b}", keep, (b, b))], [F32])
        stages.append(keep)

    grad_zero, grad_one, ones[0], ones[1] = back(0, 1, (four, five), F32, 5, [parts[0], stages[0]])
    own, over = call(
        "input_late",
        functools.partial(input_rest_kernel, late, 512),
        [ones[n] for n in late] + [pays[n] for n in late] + list(parts),
        [((rows, 512), F32, True), ((rows, 512), BF16, True)],
        pin,
        2.5 * depth,
        after=[stages[0]],
    )

    top = bits - 1
    (one,) = add([grad_one, three], [BF16])
    if extra:
        (zero,) = add([grad_zero, two, send("near", one, near_bit)], [F32])
        for at in reversed(extra):
            count = zero.shape[0] // 2
            zero = zero[:count] + send("extra", zero[count:].astype(BF16), at).astype(F32)
        low_zero = zero.astype(BF16)
        pieces = []
    else:
        pieces = [send("cross", one, (top, top), False, 1 << near_bit[0]), send("near", one, near_bit, True)]
        zero, low_zero = add([grad_zero, two], [F32, BF16], [own])
    pieces = [zero, *pieces, send("far", low_zero, (top, top), False)]
    (keep,) = add([keep, send("shared_1", keep, (1, 1))], [F32], [low_zero])
    (keep,) = add([keep, send("shared_0", keep, (0, 0))], [F32])
    give = swap("keep", keep)
    grad_gate, grad_gate_bias, tower_first, tower_bias, last, out_bias, done = call(
        "close",
        functools.partial(close_kernel, experts),
        [ints, keep, give],
        [
            ((2, experts, 512), F32, False),
            ((2, experts), F32, False),
            ((2, 64, 128), F32, False),
            ((2, 64), F32, False),
            ((2, 64), F32, False),
            ((1, 2), F32, False),
            ((8, 128), F32, True),
        ],
        pin,
        1,
        [pltpu.VMEM((2 * deep, 512), F32)],
        1,
    )
    (final,) = add(pieces, [F32], [done])

    (input_grad,) = call(
        "input_sum",
        functools.partial(add_kernel, 2),
        [own, swap("over", over)],
        [((rows, 512), F32, False)],
        pin,
        1.5,
        after=[final],
    )
    grad_w_first, grad_b_first, grad_w_second, grad_b_second = call(
        "finish",
        finish_kernel,
        [ints, final, swap("final", final)],
        [
            ((1, 512, 256), F32, False),
            ((1, 256), F32, False),
            ((1, 256, 128), F32, False),
            ((1, 128), F32, False),
        ],
        pin,
        TAIL,
        scalars=1,
    )
    return (
        predictions,
        input_grad,
        grad_w_first,
        grad_b_first,
        grad_w_second,
        grad_b_second,
        jnp.transpose(grad_gate, (0, 2, 1)),
        grad_gate_bias,
        jnp.transpose(tower_first, (0, 2, 1)),
        tower_bias,
        last,
        out_bias[0],
    )


def solution(mesh):
    in_specs = (
        P(("dp", "expert"), None),
        P("expert", None, None),
        P("expert", None),
        P("expert", None, None),
        P("expert", None),
        P(),
        P(),
        P(),
        P(),
        P(),
        P(),
        P(None, ("dp", "expert")),
        P(),
        P(),
    )
    out_specs = (
        P(None, ("dp", "expert")),
        P(("dp", "expert"), None),
        P("expert", None, None),
        P("expert", None),
        P("expert", None, None),
        P("expert", None),
        P(),
        P(),
        P(),
        P(),
        P(),
        P(),
    )
    return jax.shard_map(
        per_device, mesh=mesh, in_specs=in_specs, out_specs=out_specs, check_vma=False
    )
```

```python
import functools

import jax
import jax.numpy as jnp
from jax import lax
from jax.experimental import pallas as pl
from jax.experimental.pallas import tpu as pltpu
from jax.sharding import PartitionSpec as P

F32 = jnp.float32
BF16 = jnp.bfloat16
ROOT = 0.7978845608028654
CUBE = 0.044715
NN = (((1,), (0,)), ((), ()))
NT = (((1,), (1,)), ((), ()))
TN = (((0,), (0,)), ((), ()))
TT = (((0,), (1,)), ((), ()))
BIAS_ROWS = 16
SCALE = 3e8
EARLY = 6
BACK_CHUNK = 2048
TAIL = 10
GROUPS = ((0,), (1, 4), (2,), (3, 5), (6, 7))
LAST_ASK = 2
PAY_ROWS = 320 + BIAS_ROWS
VMEM = pl.BlockSpec(memory_space=pltpu.VMEM)
SMEM = pl.BlockSpec(memory_space=pltpu.SMEM)
ANY = pl.BlockSpec(memory_space=pl.ANY)


def dot(a, b, dims):
    return lax.dot_general(a, b, dims, preferred_element_type=F32)


def gelu_pair(v):
    square = v * v
    upper = 0.5 + 0.5 * jnp.tanh(v * (ROOT + (ROOT * CUBE) * square))
    value = v * upper
    slope = upper + value * (1.0 - upper) * (2.0 * ROOT + (6.0 * ROOT * CUBE) * square)
    return value, slope


def call(name, kernel, ins, outs, pin, micros, scratch=(), scalars=0, limit=8, after=()):
    limit = limit if pin is not None else 60
    pinned = lambda a: pltpu.with_memory_space_constraint(a, pltpu.VMEM) if pin else a
    args = [a if n < scalars else pinned(a) for n, a in enumerate(ins)] + list(after)
    count = len(ins)
    body = kernel
    if after:

        def body(*refs):
            return kernel(*refs[:count], *refs[count + len(after) :])

    kept = pltpu.VMEM if pin else jax.ShapeDtypeStruct
    shapes = [(kept if stay else jax.ShapeDtypeStruct)(shape, dtype) for shape, dtype, stay in outs]
    return pl.pallas_call(
        body,
        name=name,
        in_specs=[SMEM] * scalars + [VMEM] * (count - scalars) + [ANY] * len(after),
        out_specs=[VMEM] * len(outs),
        out_shape=shapes,
        scratch_shapes=list(scratch),
        compiler_params=pltpu.CompilerParams(vmem_limit_bytes=limit * 2**20),
        cost_estimate=pl.CostEstimate(flops=int(micros * SCALE), bytes_accessed=0, transcendentals=0),
    )(*args)


def hold(value, after):
    count = len(after)
    return pl.pallas_call(
        lambda *refs: None,
        name="hold",
        in_specs=[ANY] * (1 + count),
        out_specs=ANY,
        out_shape=jax.ShapeDtypeStruct(value.shape, value.dtype),
        input_output_aliases={0: 0},
        compiler_params=pltpu.CompilerParams(vmem_limit_bytes=2**20),
        cost_estimate=pl.CostEstimate(flops=0, bytes_accessed=0, transcendentals=0),
    )(value, *after)


def slot_of(masks, int_ref, j):
    half = len(masks[0])
    mask = jnp.where(int_ref[0] == 0, masks[0][j], masks[1][j])
    return int_ref[0] * half + ((int_ref[1] & (half - 1)) ^ mask)


def to_column(row):
    n = row.shape[1]
    same = lax.broadcasted_iota(jnp.int32, (n, n), 0) == lax.broadcasted_iota(jnp.int32, (n, n), 1)
    return jnp.sum(jnp.where(same, jnp.broadcast_to(row, (n, n)), 0.0), axis=1, keepdims=True)


def side_by_side(columns, tall):
    lane = lax.broadcasted_iota(jnp.int32, (tall, 128), 1)
    small = jnp.zeros((tall, 128), F32)
    for n, col in enumerate(columns):
        small = jnp.where(lane == n, jnp.broadcast_to(col, (tall, 128)), small)
    return small


def fold(ref, base, block):
    deep = block.shape[0] // 4
    for k in range(4):
        ref[base : base + deep, 128 * k : 128 * (k + 1)] = block[deep * k : deep * (k + 1)]


def unfold(ref, base, deep):
    return jnp.concatenate(
        [ref[base : base + deep, 128 * k : 128 * (k + 1)] for k in range(4)], axis=0
    )


def pack_kernel(w1_ref, w2_ref, b1_ref, b2_ref, pay_ref, w1, w2, b1, b2, sems):
    copies = [
        pltpu.make_async_copy(src, dst, sems.at[n])
        for n, (src, dst) in enumerate(((w1_ref, w1), (w2_ref, w2), (b1_ref, b1), (b2_ref, b2)))
    ]
    for copy in copies:
        copy.start()
    for copy in copies[1:]:
        copy.wait()
    second = w2[0].astype(F32).T.astype(BF16)
    pay_ref[0, 256:320, :256] = second[:64]
    pay_ref[0, 256:320, 256:] = second[64:]
    row = jnp.concatenate([b1[...].astype(F32), b2[...].astype(F32), jnp.zeros((1, 128), F32)], axis=1)
    pay_ref[0, 320:, :] = jnp.broadcast_to(row, (BIAS_ROWS, 512)).astype(BF16)
    copies[0].wait()
    pay_ref[0, :256, :] = w1[0].astype(F32).T.astype(BF16)


def pack(w1, w2, b1, b2):
    arrays = (w1, w2, b1, b2)
    return pl.pallas_call(
        pack_kernel,
        name="pack",
        in_specs=[pl.BlockSpec(memory_space=pltpu.HBM)] * 4,
        out_specs=VMEM,
        out_shape=jax.ShapeDtypeStruct((1, PAY_ROWS, 512), BF16),
        scratch_shapes=[pltpu.VMEM(a.shape, a.dtype) for a in arrays] + [pltpu.SemaphoreType.DMA((4,))],
        compiler_params=pltpu.CompilerParams(vmem_limit_bytes=8 * 2**20),
        cost_estimate=pl.CostEstimate(flops=0, bytes_accessed=0, transcendentals=0),
    )(*[pltpu.with_memory_space_constraint(a, pltpu.HBM) for a in arrays])


def biases(pay):
    flipped = pay[320:, :].astype(F32).T
    return flipped[:256, 0:1], flipped[256:384, 0:1]


def second_weight(pay):
    return jnp.concatenate([pay[256:320, :256], pay[256:320, 256:]], axis=0)


def gate_kernel(masks, groups, int_ref, label_ref, there_ref, gw_ref, gb_ref, mine_ref, other_ref, *refs):
    prob_ref, low_ref, weight_ref, x_out, label_out, scratch, sems = refs
    rows = mine_ref.shape[0]
    experts = 2 * len(masks[0])
    copies = [
        pltpu.make_async_copy(src, x_out.at[pl.ds(n * rows, rows), :], sems.at[n])
        for n, src in enumerate((mine_ref, other_ref))
    ]
    for copy in copies:
        copy.start()
    for side in range(2):
        at = slice(side * rows, (side + 1) * rows)
        label_out[:, at] = (label_ref, there_ref)[side][...].astype(F32)
        copies[side].wait()
        for t in range(2):
            part = dot(gw_ref[t], x_out[at, :], NT) + to_column(gb_ref[t : t + 1, :].astype(F32))
            top = jnp.max(part, axis=0, keepdims=True)
            e = jnp.exp(part - top)
            scratch[t * experts : (t + 1) * experts, at] = e / jnp.sum(e, axis=0, keepdims=True)
        shard = int_ref[0] if side == 0 else 1 - int_ref[0]
        index = int_ref[1] * rows + lax.broadcasted_iota(jnp.int32, (1, rows), 1)
        start = jnp.int32(0)
        weight = jnp.zeros((1, rows), F32)
        for g in range(groups):
            length = int_ref[3 + groups + g]
            size = jnp.where(int_ref[3 + g] == shard, length, 0)
            inside = (index >= start) & (index < start + size)
            recip = 1.0 / jnp.full((1, rows), length, jnp.int32).astype(F32)
            weight = weight + jnp.where(inside, recip, 0.0)
            start = start + size
        weight_ref[:, at] = weight
    for j in range(experts // 2):
        slot = slot_of(masks, int_ref, j)
        for t in range(2):
            row = scratch[pl.ds(t * experts + slot, 1), :]
            prob_ref[j, t : t + 1, :] = row
            low_ref[j, t : t + 1, :] = row.astype(BF16).astype(F32)


def forward_kernel(bundles, first, block, chunk, x_ref, low_ref, *refs):
    count = len(bundles)
    pays, refs = refs[:count], refs[count:]
    if not first:
        mix_in, *refs = refs
    kept, mix_ref = [refs[4 * n : 4 * n + 4] for n in range(count)], refs[4 * count]
    depth = pays[0].shape[0]
    weights = {}
    for k in range(depth):
        for n, pay_ref in enumerate(pays):
            pay = pay_ref[k]
            weights[k, n] = (pay[:256], second_weight(pay), *biases(pay))
    work = [(c, k, n) for c in range(0, block, chunk) for k in range(depth) for n in range(count)]

    def step(i, _):
        base = pl.multiple_of(i * block, block)
        totals = [None, None]

        def layer_one(c, k, n):
            return dot(weights[k, n][0], x_ref[pl.ds(base + c, chunk), :], NT)

        def after_one(pre, c, k, n):
            value, slope = gelu_pair(pre + weights[k, n][2])
            hidden = value.astype(BF16)
            kept[n][0][k, :, pl.ds(base + c, chunk)] = hidden
            kept[n][1][k, :, pl.ds(base + c, chunk)] = slope.astype(kept[n][1].dtype)
            return hidden

        def after_two(pre, c, k, n):
            at = pl.ds(base + c, chunk)
            value, slope = gelu_pair(pre + weights[k, n][3])
            out = value.astype(BF16)
            kept[n][2][k, :, at] = out
            kept[n][3][k, :, at] = slope.astype(kept[n][3].dtype)
            out = out.astype(F32)
            for t in range(2):
                term = low_ref[bundles[n] * depth + k, t : t + 1, at] * out
                if k == 0 and n == 0:
                    totals[t] = term if first else mix_in[t, :, at] + term
                else:
                    totals[t] = totals[t] + term
                if k == depth - 1 and n == count - 1:
                    mix_ref[t, :, at] = totals[t].astype(mix_ref.dtype)

        ones, twos = {0: layer_one(*work[0])}, {}
        for i in range(len(work) + 1):
            if i + 1 < len(work):
                ones[i + 1] = layer_one(*work[i + 1])
            if i < len(work):
                hidden = after_one(ones.pop(i), *work[i])
            if i >= 1:
                after_two(twos.pop(i - 1), *work[i - 1])
            if i < len(work):
                twos[i] = dot(weights[work[i][1:]][1], hidden, NN)
        return 0

    lax.fori_loop(0, x_ref.shape[0] // block, step, 0)


def tower_kernel(
    chunk, mix_ref, come_ref, label_ref, weight_ref, tob_ref, tw_ref, tb_ref, tl_ref,
    pred_ref, dmix_ref, centre_ref, shared_ref, first, sums,
):
    rows = pred_ref.shape[1]
    first[...] = jnp.zeros_like(first)
    sums[...] = jnp.zeros_like(sums)
    tb = [to_column(tb_ref[t : t + 1, :].astype(F32)) for t in range(2)]
    tl = [to_column(tl_ref[t : t + 1, :].astype(F32)) for t in range(2)]

    def step(side, i, _):
        at = pl.ds(pl.multiple_of(side * rows + i * chunk, chunk), chunk)
        there = pl.ds(pl.multiple_of((1 - side) * rows + i * chunk, chunk), chunk)
        cols = []
        for t in range(2):
            mixed = mix_ref[t, :, at].astype(F32) + come_ref[t, :, there].astype(F32)
            low = mixed.astype(BF16)
            act, slope = gelu_pair(dot(tw_ref[t], low, NN) + tb[t])
            score = jnp.sum(act * tl[t], axis=0, keepdims=True) + tob_ref[0:1, t : t + 1].astype(F32)
            pred = 1.0 / (1.0 + jnp.exp(-score))
            d_score = weight_ref[:, at] * (pred - label_ref[t : t + 1, at])
            d_low = (d_score * tl[t] * slope).astype(BF16)
            d_mixed = dot(tw_ref[t], d_low, TN)
            dmix_ref[t, :, at] = d_mixed
            centre_ref[t : t + 1, at] = jnp.sum(d_mixed * mixed, axis=0, keepdims=True)
            if side == 0:
                pred_ref[t : t + 1, at] = pred
                first[t] += dot(d_low, low, NT)
                cols.append(jnp.sum(act * d_score, axis=1, keepdims=True))
                cols.append(jnp.sum(d_low.astype(F32), axis=1, keepdims=True))
                total = jnp.sum(d_score, axis=1, keepdims=True)
                cols.append(jnp.broadcast_to(total, (64, 1)))
        if side == 0:
            sums[...] += side_by_side([cols[3 * t + n] for n in range(3) for t in range(2)], 64)
        return 0

    lax.fori_loop(0, rows // chunk, functools.partial(step, 0), 0)
    lax.fori_loop(0, rows // chunk, functools.partial(step, 1), 0)
    for t in range(2):
        fold(shared_ref, 16 * t, first[t])
    fold(shared_ref, 32, sums[...])


def shared_rows(experts):
    return -(-(48 + 2 * experts + experts // 2) // 16) * 16


def gate_back_kernel(masks, chunk, spot_ref, x_ref, dmix_ref, centre_ref, prob_ref, tower_ref, *refs):
    outs = refs[:8]
    dgate_ref, keep_ref, give_ref, gates, shared_ref = refs[8:]
    depth = outs[0].shape[0]
    experts = 2 * len(masks[0])
    gates[...] = jnp.zeros_like(gates)

    def step(i, _):
        at = pl.ds(pl.multiple_of(i * chunk, chunk), chunk)
        for j in range(8 * depth):
            out = outs[j // depth][j % depth, :, at].astype(F32)
            slot = slot_of(masks, spot_ref, j)
            for t in range(2):
                d_prob = jnp.sum(dmix_ref[t, :, at] * out, axis=0, keepdims=True)
                d_gate = prob_ref[j, t : t + 1, at] * (d_prob - centre_ref[t : t + 1, at])
                gates[pl.ds(t * experts + slot, 1), at] = d_gate
        return 0

    lax.fori_loop(0, x_ref.shape[0] // chunk, step, 0)
    low = gates[...].astype(BF16)
    dgate_ref[...] = low
    shared_ref[...] = jnp.zeros_like(shared_ref)
    shared_ref[:48, :] = tower_ref[...]
    shared_ref[48 : 48 + 2 * experts, :] = dot(low, x_ref[...], NN)
    bias = jnp.sum(low.astype(F32), axis=1, keepdims=True)
    fold(shared_ref, 48 + 2 * experts, side_by_side([bias], 2 * experts))
    deep = keep_ref.shape[0]
    keep_ref[...] = shared_ref[pl.ds(pl.multiple_of(spot_ref[0] * deep, 8), deep), :]
    give_ref[...] = shared_ref[pl.ds(pl.multiple_of((1 - spot_ref[0]) * deep, 8), deep), :]


def backward_kernel(bundles, add, block, x_ref, pay_a, pay_b, low_ref, dmix_ref, *refs):
    kept, refs = (refs[:3], refs[3:6]), refs[6:]
    if add:
        come, refs = refs[:2], refs[2:]
    grads, dones, d_two, sums = refs[:2], refs[2:4], refs[4], refs[5]
    depth = pay_a.shape[0]
    for k in range(depth):
        weights = [second_weight(pay[k]) for pay in (pay_a, pay_b)]
        sums[...] = jnp.zeros_like(sums)

        def step(i, _, k=k, weights=weights):
            at = pl.ds(pl.multiple_of(i * block, block), block)
            for n in range(2):
                _, g1_ref, g2_ref = kept[n]
                j = bundles[n] * depth + k
                d_out = low_ref[j, 0:1, at] * dmix_ref[0, :, at] + low_ref[j, 1:2, at] * dmix_ref[1, :, at]
                two = d_out.astype(BF16).astype(F32) * g2_ref[k, :, at].astype(F32)
                two_low = two.astype(BF16)
                d_two[n, :, at] = two_low
                one = dot(weights[n], two_low, TN) * g1_ref[k, :, at].astype(F32)
                dones[n][k, :, at] = one.astype(BF16)
                add_one, add_two = one[:, :128], two[:, :128]
                for m in range(128, block, 128):
                    add_one = add_one + one[:, m : m + 128]
                    add_two = add_two + two[:, m : m + 128]
                sums[n, :256] += add_one
                sums[n, 256:] += add_two
            return 0

        lax.fori_loop(0, x_ref.shape[0] // block, step, 0)
        for n in range(2):
            h_ref = kept[n][0]
            first = dot(dones[n][k], x_ref[...], NN)
            second = dot(d_two[n], h_ref[k], NT)
            second = jnp.concatenate([second[:64], second[64:]], axis=1)
            row = jnp.concatenate(
                [
                    jnp.sum(sums[n].T, axis=0, keepdims=True),
                    jnp.zeros((1, 128), F32),
                ],
                axis=1,
            )
            high = row.astype(BF16).astype(F32)
            index = lax.broadcasted_iota(jnp.int32, (BIAS_ROWS, 512), 0)
            both = jnp.where(index == 0, high, jnp.where(index == 1, row - high, 0.0))
            if add:
                first = first + come[n][k, :256, :].astype(F32)
                second = second + come[n][k, 256:320, :].astype(F32)
                both = both + come[n][k, 320:, :].astype(F32)
            grads[n][k, :256, :] = first.astype(grads[n].dtype)
            grads[n][k, 256:320, :] = second.astype(grads[n].dtype)
            grads[n][k, 320:, :] = both.astype(grads[n].dtype)


def input_kernel(side, chunk, dgate_ref, gw_ref, *refs):
    experts = gw_ref.shape[1]
    ones, pays, out_ref = refs[:8], refs[8:16], refs[16]
    rows = out_ref.shape[0]

    def step(i, _):
        at = pl.ds(pl.multiple_of(side * rows + i * chunk, chunk), chunk)
        total = dot(dgate_ref[:experts, at], gw_ref[0], TN) + dot(dgate_ref[experts:, at], gw_ref[1], TN)
        for one, pay in zip(ones, pays):
            for k in range(one.shape[0]):
                total = total + dot(one[k, :, at], pay[k, :256, :], TN)
        out_ref[pl.ds(pl.multiple_of(i * chunk, chunk), chunk), :] = total.astype(out_ref.dtype)
        return 0

    lax.fori_loop(0, rows // chunk, step, 0)


def add_kernel(count, *refs):
    total = refs[0][...].astype(F32)
    for ref in refs[1:count]:
        total = total + ref[...].astype(F32)
    for ref in refs[count:]:
        ref[...] = total.astype(ref.dtype)


def input_sum_kernel(own_ref, come_ref, out_ref, done_ref):
    out_ref[...] = own_ref[...] + come_ref[...].astype(F32)
    done_ref[...] = jnp.zeros_like(done_ref)


def finish_kernel(owner_ref, mine_ref, come_ref, w1_ref, b1_ref, w2_ref, b2_ref):
    owner = owner_ref[2] == 1
    mine_ref, come_ref = mine_ref.at[0], come_ref.at[0]
    w1_ref[0] = jnp.where(owner, mine_ref[:256, :], come_ref[:256, :]).T
    second = jnp.where(owner, mine_ref[256:320, :], come_ref[256:320, :])
    w2_ref[0] = jnp.concatenate([second[:, :256], second[:, 256:]], axis=0).T
    bias = jnp.where(owner, mine_ref[320:328, :], come_ref[320:328, :])
    bias = bias[0:1] + bias[1:2]
    b1_ref[...] = bias[:, :256]
    b2_ref[...] = bias[:, 256:384]


def close_kernel(
    experts, spot_ref, keep_ref, give_ref,
    gate_ref, gate_bias_ref, first_ref, tb_ref, tl_ref, tob_ref, done_ref, shared_ref,
):

    base = 48 + 2 * experts
    deep = keep_ref.shape[0]
    shared_ref[pl.ds(pl.multiple_of(spot_ref[0] * deep, 8), deep), :] = keep_ref[...]
    shared_ref[pl.ds(pl.multiple_of((1 - spot_ref[0]) * deep, 8), deep), :] = give_ref[...]
    for t in range(2):
        gate_ref[t] = shared_ref[48 + t * experts : 48 + (t + 1) * experts, :]
        first_ref[t] = unfold(shared_ref, 16 * t, 16)
    small = unfold(shared_ref, 32, 16).T
    tl_ref[...] = small[0:2, :]
    tb_ref[...] = small[2:4, :]
    tob_ref[:, 0:1] = small[4:5, 0:1]
    tob_ref[:, 1:2] = small[5:6, 0:1]
    bias = unfold(shared_ref, base, experts // 2).T
    gate_bias_ref[0:1, :] = bias[0:1, :experts]
    gate_bias_ref[1:2, :] = bias[0:1, experts:]
    done_ref[...] = jnp.zeros_like(done_ref)


def per_device(
    inputs,
    w_first,
    b_first,
    w_second,
    b_second,
    gate_weight,
    gate_bias,
    tower_first_weight,
    tower_first_bias,
    tower_last,
    tower_out_bias,
    labels,
    group_len,
    group_shard,
):
    rows = inputs.shape[0]
    experts = lax.axis_size("expert")
    half = experts // 2
    bits = experts.bit_length() - 1
    depth = half // 8
    pin = True if depth == 1 else None
    chunk = 256 if pin else 512
    core = lax.axis_index("dp")
    place = lax.axis_index("expert")
    owner = core == place // half
    near_bit, mid_bit, end_bit = (2, 2), (1, 0), (0, 1)
    extra = [(b, b) for b in range(bits - 2, 2, -1)]

    def pairs(bit_of_core, want=None, also=0):
        return [
            (c * experts + q, c * experts + (q ^ (1 << bit_of_core[c]) ^ also))
            for c in range(2)
            for q in range(experts)
            if want is None or (c == q // half) == want
        ]

    def send(name, value, bit_of_core, want=None, also=0):
        with jax.named_scope(name):
            return lax.ppermute(value, ("dp", "expert"), pairs(bit_of_core, want, also))

    def swap(name, value):
        with jax.named_scope(name):
            return lax.ppermute(value, "dp", [(0, 1), (1, 0)])

    def deal(value):
        route = []
        for c in range(2):
            for q in range(experts):
                target = c * experts + (q ^ half) if c == q // half else (1 - c) * experts + q
                route.append((c * experts + q, target))
        with jax.named_scope("deal"):
            return lax.ppermute(value, ("dp", "expert"), route)

    def expert_mask(c, j):
        bundle, inner = j // depth, j % depth
        found = sum(1 << extra[e][c] for e in range(len(extra)) if (inner >> e) & 1)
        for n, at in enumerate((near_bit, mid_bit, end_bit)):
            found |= ((bundle >> n) & 1) << at[c]
        return found

    masks = [[expert_mask(c, j) for j in range(half)] for c in range(2)]
    spot = jnp.stack([core, place, owner.astype(jnp.int32)]).astype(jnp.int32)

    def add(values, dtypes, after=()):
        shape = values[0].shape
        outs = [(shape, dtype, True) for dtype in dtypes]
        return call("add", functools.partial(add_kernel, len(values)), values, outs, pin, 0, after=after)

    pay = pack(w_first, w_second, b_first, b_second)
    zero = deal(pay)
    if not extra:
        owners_near = send("owners_near", pay, near_bit, True)
    for at in extra:
        zero = jnp.concatenate([zero, send("pay_extra", zero, at)], axis=0)
    labels_there = swap("labels", labels)
    inputs_there = swap("inputs", inputs)
    gate_rows = jnp.transpose(gate_weight, (0, 2, 1))
    ints = jnp.concatenate([spot, group_shard, group_len])
    outs = [((half, 2, 2 * rows), F32)] * 2 + [((1, 2 * rows), F32), ((2 * rows, 512), BF16), ((2, 2 * rows), F32)]
    kept = pltpu.VMEM if pin else jax.ShapeDtypeStruct
    prob, low, weights, x, both_labels = pl.pallas_call(
        functools.partial(gate_kernel, masks, group_len.shape[0]),
        name="gate",
        in_specs=[SMEM] + [VMEM] * 4 + [ANY] * 2,
        out_specs=[VMEM] * 5,
        out_shape=[kept(shape, dtype) for shape, dtype in outs],
        scratch_shapes=[pltpu.VMEM((2 * experts, 2 * rows), F32), pltpu.SemaphoreType.DMA((2,))],
        compiler_params=pltpu.CompilerParams(vmem_limit_bytes=(8 if pin else 60) * 2**20),
        cost_estimate=pl.CostEstimate(flops=0, bytes_accessed=0, transcendentals=0),
    )(ints, labels, labels_there, gate_rows, gate_bias, inputs, inputs_there)

    pays = [hold(zero, [low])] + [None] * 7
    pays[1] = send("pay_1", pays[0], near_bit, None if extra else False)
    pays[2] = send("pay_2", pays[0], mid_bit)
    pays[4] = send("pay_4", pays[0], end_bit)
    mixed = None
    saved = [None] * 8
    slope_type = F32 if pin else BF16
    for group in GROUPS:
        shape = lambda deep, dtype: ((depth, deep, 2 * rows), dtype, True)
        *kept, mixed = call(
            "forward_" + "".join(str(n) for n in group),
            functools.partial(forward_kernel, group, mixed is None, 4 * chunk, chunk),
            [x, low] + [pays[n] for n in group] + ([] if mixed is None else [mixed]),
            [shape(256, BF16), shape(256, BF16), shape(128, BF16), shape(128, slope_type)] * len(group)
            + [((2, 128, 2 * rows), BF16 if group == GROUPS[-1] else F32, True)],
            pin,
            2.25 * len(group) * depth,
        )
        for n, bundle in enumerate(group):
            saved[bundle] = kept[4 * n : 4 * n + 4]
        if group == GROUPS[0]:
            if extra:
                held = hold(pays[1], [pays[2], pays[4], mixed])
            else:
                pays[2] = hold(pays[2], [pays[4], owners_near, mixed])
                (pays[1],) = add([owners_near, pays[1]], [BF16], [pays[2]])
                held = pays[1]
            pays[3] = send("pay_3", held, mid_bit)
            pays[5] = send("pay_5", held, end_bit)
            pays[6] = send("pay_6", pays[2], end_bit)
        if group == GROUPS[LAST_ASK]:
            pays[7] = send("pay_7", hold(pays[3], [mixed]), end_bit)

    predictions, dmix, centre, tower_sums = call(
        "tower",
        functools.partial(tower_kernel, 512),
        [mixed, swap("mixed", mixed), both_labels, weights, tower_out_bias[None]]
        + [jnp.transpose(tower_first_weight, (0, 2, 1)), tower_first_bias, tower_last],
        [
            ((2, rows), F32, False),
            ((2, 128, 2 * rows), F32, True),
            ((2, 2 * rows), F32, True),
            ((48, 512), F32, True),
        ],
        pin,
        4,
        [pltpu.VMEM((2, 64, 128), F32), pltpu.VMEM((64, 128), F32)],
    )

    def back(a, b, come, dtype, cost, after=()):
        grad = ((depth, PAY_ROWS, 512), dtype, False)
        done = ((depth, 256, 2 * rows), BF16, True)
        return call(
            f"backward_{a}{b}",
            functools.partial(backward_kernel, (a, b), come is not None, BACK_CHUNK),
            [x, pays[a], pays[b], low, dmix]
            + [saved[n][m] for n in (a, b) for m in (0, 1, 3)]
            + list(come or ()),
            [grad, grad, done, done],
            pin,
            cost,
            [pltpu.VMEM((2, 128, 2 * rows), BF16), pltpu.VMEM((2, 384, 128), F32)],
            after=after,
        )

    ones = [None] * 8
    grad_six, grad_seven, ones[6], ones[7] = back(6, 7, None, BF16, 5)
    six, seven = send("grad_six", grad_six, end_bit), send("grad_seven", grad_seven, end_bit)
    grad_four, grad_five, ones[4], ones[5] = back(4, 5, None, BF16, 1, [ones[7]])
    five, four = send("grad_five", grad_five, end_bit), send("grad_four", grad_four, end_bit)
    deep = shared_rows(experts) // 2
    dgate, keep, give = call(
        "gate_back",
        functools.partial(gate_back_kernel, masks, 512),
        [ints, x, dmix, centre, prob, tower_sums] + [kept[2] for kept in saved],
        [((2 * experts, 2 * rows), BF16, True)] + [((deep, 512), F32, True)] * 2,
        pin,
        1,
        [pltpu.VMEM((2 * experts, 2 * rows), F32), pltpu.VMEM((2 * deep, 512), F32)],
        1,
        after=[ones[5]],
    )
    (keep,) = add([keep, swap("give", give)], [F32])
    grad_two, grad_three, ones[2], ones[3] = back(2, 3, (six, seven), BF16, 1, [keep])
    three, two = send("grad_three", grad_three, mid_bit), send("grad_two", grad_two, mid_bit)
    stages = []
    for b in range(2, bits):
        (keep,) = add([keep, send(f"shared_{b}", keep, (b, b))], [F32], [ones[3]])
        stages.append(keep)

    grad_zero, grad_one, ones[0], ones[1] = back(0, 1, (four, five), F32, 1, [ones[3], stages[0]])
    def input_gradient(side, dtype, after=()):
        (out,) = call(
            f"input_{side}",
            functools.partial(input_kernel, side, 512),
            [dgate, gate_rows, *ones, *pays],
            [((rows, 512), dtype, True)],
            pin,
            3.5 * depth,
            after=after,
        )
        return out

    over = input_gradient(1, BF16, [stages[1]])
    own = input_gradient(0, F32)
    top = bits - 1
    (one,) = add([grad_one, three], [BF16], [over])
    if extra:
        (zero,) = add([grad_zero, two, send("near", one, near_bit)], [F32])
        for at in reversed(extra):
            count = zero.shape[0] // 2
            zero = zero[:count] + send("extra", zero[count:].astype(BF16), at).astype(F32)
        low_zero = zero.astype(BF16)
        pieces = []
    else:
        pieces = [send("near", one, near_bit, True), send("cross", one, (top, top), False, 1 << near_bit[0])]
        zero, low_zero = add([grad_zero, two], [F32, BF16])
    pieces = [zero, *pieces, send("far", low_zero, (top, top), False)]
    (keep,) = add([keep, send("shared_1", keep, (1, 1))], [F32], [low_zero, own])
    (keep,) = add([keep, send("shared_0", keep, (0, 0))], [F32])
    give = swap("keep", keep)
    grad_gate, grad_gate_bias, tower_first, tower_bias, last, out_bias, done = call(
        "close",
        functools.partial(close_kernel, experts),
        [ints, keep, give],
        [
            ((2, experts, 512), F32, False),
            ((2, experts), F32, False),
            ((2, 64, 128), F32, False),
            ((2, 64), F32, False),
            ((2, 64), F32, False),
            ((1, 2), F32, False),
            ((8, 128), F32, True),
        ],
        pin,
        1,
        [pltpu.VMEM((2 * deep, 512), F32)],
        1,
    )
    (final,) = add(pieces, [F32], [done, own])

    input_grad, summed = call(
        "input_sum",
        input_sum_kernel,
        [own, swap("over", over)],
        [((rows, 512), F32, False), ((8, 128), F32, True)],
        pin,
        1.5,
        after=[final],
    )
    grad_w_first, grad_b_first, grad_w_second, grad_b_second = call(
        "finish",
        finish_kernel,
        [ints, final, swap("final", final)],
        [
            ((1, 512, 256), F32, False),
            ((1, 256), F32, False),
            ((1, 256, 128), F32, False),
            ((1, 128), F32, False),
        ],
        pin,
        TAIL,
        scalars=1,
        after=[summed],
    )
    return (
        predictions,
        input_grad,
        grad_w_first,
        grad_b_first,
        grad_w_second,
        grad_b_second,
        jnp.transpose(grad_gate, (0, 2, 1)),
        grad_gate_bias,
        jnp.transpose(tower_first, (0, 2, 1)),
        tower_bias,
        last,
        out_bias[0],
    )


def solution(mesh):
    in_specs = (
        P(("dp", "expert"), None),
        P("expert", None, None),
        P("expert", None),
        P("expert", None, None),
        P("expert", None),
        P(),
        P(),
        P(),
        P(),
        P(),
        P(),
        P(None, ("dp", "expert")),
        P(),
        P(),
    )
    out_specs = (
        P(None, ("dp", "expert")),
        P(("dp", "expert"), None),
        P("expert", None, None),
        P("expert", None),
        P("expert", None, None),
        P("expert", None),
        P(),
        P(),
        P(),
        P(),
        P(),
        P(),
    )
    return jax.shard_map(
        per_device, mesh=mesh, in_specs=in_specs, out_specs=out_specs, check_vma=False
    )
```

```python
import functools

import jax
import jax.numpy as jnp
from jax import lax
from jax.experimental import pallas as pl
from jax.experimental.pallas import tpu as pltpu
from jax.sharding import PartitionSpec as P

F32 = jnp.float32
BF16 = jnp.bfloat16
ROOT = 0.7978845608028654
CUBE = 0.044715
NN = (((1,), (0,)), ((), ()))
NT = (((1,), (1,)), ((), ()))
TN = (((0,), (0,)), ((), ()))
TT = (((0,), (1,)), ((), ()))
BIAS_ROWS = 16
SCALE = 3e8
EARLY = 6
BACK_CHUNK = 2048
TAIL = 10
GROUPS = ((0,), (1, 4), (2,), (3, 5), (6, 7))
LAST_ASK = 2
PAY_ROWS = 320 + BIAS_ROWS
VMEM = pl.BlockSpec(memory_space=pltpu.VMEM)
SMEM = pl.BlockSpec(memory_space=pltpu.SMEM)
ANY = pl.BlockSpec(memory_space=pl.ANY)


def dot(a, b, dims):
    return lax.dot_general(a, b, dims, preferred_element_type=F32)


def gelu_pair(v):
    square = v * v
    upper = 0.5 + 0.5 * jnp.tanh(v * (ROOT + (ROOT * CUBE) * square))
    value = v * upper
    slope = upper + value * (1.0 - upper) * (2.0 * ROOT + (6.0 * ROOT * CUBE) * square)
    return value, slope


def call(name, kernel, ins, outs, pin, micros, scratch=(), scalars=0, limit=8, after=(), alias=()):
    limit = limit if pin is not None else 60
    pinned = lambda a: pltpu.with_memory_space_constraint(a, pltpu.VMEM) if pin else a
    args = [a if n < scalars else pinned(a) for n, a in enumerate(ins)] + [pinned(a) for a in alias] + list(after)
    count, skip = len(ins), len(alias) + len(after)
    body = kernel
    if skip:

        def body(*refs):
            return kernel(*refs[:count], *refs[count + skip :])

    kept = pltpu.VMEM if pin else jax.ShapeDtypeStruct
    shapes = [(kept if stay else jax.ShapeDtypeStruct)(shape, dtype) for shape, dtype, stay in outs]
    return pl.pallas_call(
        body,
        name=name,
        in_specs=[SMEM] * scalars + [VMEM] * (count - scalars + len(alias)) + [ANY] * len(after),
        input_output_aliases={count + n: n for n in range(len(alias))},
        out_specs=[VMEM] * len(outs),
        out_shape=shapes,
        scratch_shapes=list(scratch),
        compiler_params=pltpu.CompilerParams(vmem_limit_bytes=limit * 2**20),
        cost_estimate=pl.CostEstimate(flops=int(micros * SCALE), bytes_accessed=0, transcendentals=0),
    )(*args)


def hold(value, after):
    count = len(after)
    return pl.pallas_call(
        lambda *refs: None,
        name="hold",
        in_specs=[ANY] * (1 + count),
        out_specs=ANY,
        out_shape=jax.ShapeDtypeStruct(value.shape, value.dtype),
        input_output_aliases={0: 0},
        compiler_params=pltpu.CompilerParams(vmem_limit_bytes=2**20),
        cost_estimate=pl.CostEstimate(flops=0, bytes_accessed=0, transcendentals=0),
    )(value, *after)


def slot_of(masks, int_ref, j):
    half = len(masks[0])
    mask = jnp.where(int_ref[0] == 0, masks[0][j], masks[1][j])
    return int_ref[0] * half + ((int_ref[1] & (half - 1)) ^ mask)


def to_column(row):
    n = row.shape[1]
    same = lax.broadcasted_iota(jnp.int32, (n, n), 0) == lax.broadcasted_iota(jnp.int32, (n, n), 1)
    return jnp.sum(jnp.where(same, jnp.broadcast_to(row, (n, n)), 0.0), axis=1, keepdims=True)


def side_by_side(columns, tall):
    lane = lax.broadcasted_iota(jnp.int32, (tall, 128), 1)
    small = jnp.zeros((tall, 128), F32)
    for n, col in enumerate(columns):
        small = jnp.where(lane == n, jnp.broadcast_to(col, (tall, 128)), small)
    return small


def fold(ref, base, block):
    deep = block.shape[0] // 4
    for k in range(4):
        ref[base : base + deep, 128 * k : 128 * (k + 1)] = block[deep * k : deep * (k + 1)]


def unfold(ref, base, deep):
    return jnp.concatenate(
        [ref[base : base + deep, 128 * k : 128 * (k + 1)] for k in range(4)], axis=0
    )


def pack_kernel(w1_ref, w2_ref, b1_ref, b2_ref, pay_ref, w1, w2, b1, b2, sems):
    copies = [
        pltpu.make_async_copy(src, dst, sems.at[n])
        for n, (src, dst) in enumerate(((w1_ref, w1), (w2_ref, w2), (b1_ref, b1), (b2_ref, b2)))
    ]
    for copy in copies:
        copy.start()
    for copy in copies[1:]:
        copy.wait()
    second = w2[0].astype(F32).T.astype(BF16)
    pay_ref[0, 256:320, :256] = second[:64]
    pay_ref[0, 256:320, 256:] = second[64:]
    row = jnp.concatenate([b1[...].astype(F32), b2[...].astype(F32), jnp.zeros((1, 128), F32)], axis=1)
    pay_ref[0, 320:, :] = jnp.broadcast_to(row, (BIAS_ROWS, 512)).astype(BF16)
    copies[0].wait()
    pay_ref[0, :256, :] = w1[0].astype(F32).T.astype(BF16)


def pack(w1, w2, b1, b2):
    arrays = (w1, w2, b1, b2)
    return pl.pallas_call(
        pack_kernel,
        name="pack",
        in_specs=[pl.BlockSpec(memory_space=pltpu.HBM)] * 4,
        out_specs=VMEM,
        out_shape=jax.ShapeDtypeStruct((1, PAY_ROWS, 512), BF16),
        scratch_shapes=[pltpu.VMEM(a.shape, a.dtype) for a in arrays] + [pltpu.SemaphoreType.DMA((4,))],
        compiler_params=pltpu.CompilerParams(vmem_limit_bytes=8 * 2**20),
        cost_estimate=pl.CostEstimate(flops=0, bytes_accessed=0, transcendentals=0),
    )(*[pltpu.with_memory_space_constraint(a, pltpu.HBM) for a in arrays])


def biases(pay):
    flipped = pay[320:, :].astype(F32).T
    return flipped[:256, 0:1], flipped[256:384, 0:1]


def second_weight(pay):
    return jnp.concatenate([pay[256:320, :256], pay[256:320, 256:]], axis=0)


def gate_kernel(masks, groups, int_ref, label_ref, there_ref, gw_ref, gb_ref, mine_ref, other_ref, *refs):
    prob_ref, low_ref, weight_ref, x_out, label_out, scratch, sems = refs
    rows = mine_ref.shape[0]
    experts = 2 * len(masks[0])
    copies = [
        pltpu.make_async_copy(src, x_out.at[pl.ds(n * rows, rows), :], sems.at[n])
        for n, src in enumerate((mine_ref, other_ref))
    ]
    for copy in copies:
        copy.start()
    for side in range(2):
        at = slice(side * rows, (side + 1) * rows)
        label_out[:, at] = (label_ref, there_ref)[side][...].astype(F32)
        copies[side].wait()
        for t in range(2):
            part = dot(gw_ref[t], x_out[at, :], NT) + to_column(gb_ref[t : t + 1, :].astype(F32))
            top = jnp.max(part, axis=0, keepdims=True)
            e = jnp.exp(part - top)
            scratch[t * experts : (t + 1) * experts, at] = e / jnp.sum(e, axis=0, keepdims=True)
        shard = int_ref[0] if side == 0 else 1 - int_ref[0]
        index = int_ref[1] * rows + lax.broadcasted_iota(jnp.int32, (1, rows), 1)
        start = jnp.int32(0)
        weight = jnp.zeros((1, rows), F32)
        for g in range(groups):
            length = int_ref[3 + groups + g]
            size = jnp.where(int_ref[3 + g] == shard, length, 0)
            inside = (index >= start) & (index < start + size)
            recip = 1.0 / jnp.full((1, rows), length, jnp.int32).astype(F32)
            weight = weight + jnp.where(inside, recip, 0.0)
            start = start + size
        weight_ref[:, at] = weight
    for j in range(experts // 2):
        slot = slot_of(masks, int_ref, j)
        for t in range(2):
            row = scratch[pl.ds(t * experts + slot, 1), :]
            prob_ref[j, t : t + 1, :] = row
            low_ref[j, t : t + 1, :] = row.astype(BF16).astype(F32)


def forward_kernel(bundles, first, block, chunk, span, x_ref, low_ref, *refs):
    count = len(bundles)
    pays, refs = refs[:count], refs[count:]
    if not first:
        mix_in, *refs = refs
    kept, mix_ref = [refs[4 * n : 4 * n + 4] for n in range(count)], refs[4 * count]
    depth = pays[0].shape[0]
    weights = {}
    for k in range(depth):
        for n, pay_ref in enumerate(pays):
            pay = pay_ref[k]
            weights[k, n] = (pay[:256], second_weight(pay), *biases(pay))
    out_from = 0 if mix_ref.shape[2] == x_ref.shape[0] else span[0]
    work = [(c, k, n) for c in range(0, block, chunk) for k in range(depth) for n in range(count)]

    def step(i, _):
        base = pl.multiple_of(i * block, block)
        totals = [None, None]

        def layer_one(c, k, n):
            return dot(weights[k, n][0], x_ref[pl.ds(base + c, chunk), :], NT)

        def after_one(pre, c, k, n):
            value, slope = gelu_pair(pre + weights[k, n][2])
            hidden = value.astype(BF16)
            kept[n][0][k, :, pl.ds(base + c, chunk)] = hidden
            kept[n][1][k, :, pl.ds(base + c, chunk)] = slope.astype(kept[n][1].dtype)
            return hidden

        def after_two(pre, c, k, n):
            at = pl.ds(base + c, chunk)
            value, slope = gelu_pair(pre + weights[k, n][3])
            out = value.astype(BF16)
            kept[n][2][k, :, at] = out
            kept[n][3][k, :, at] = slope.astype(kept[n][3].dtype)
            out = out.astype(F32)
            for t in range(2):
                term = low_ref[bundles[n] * depth + k, t : t + 1, at] * out
                if k == 0 and n == 0:
                    totals[t] = term if first else mix_in[t, :, at] + term
                else:
                    totals[t] = totals[t] + term
                if k == depth - 1 and n == count - 1:
                    mix_ref[t, :, pl.ds(base + c - out_from, chunk)] = totals[t].astype(mix_ref.dtype)

        ones, twos = {0: layer_one(*work[0])}, {}
        for i in range(len(work) + 1):
            if i + 1 < len(work):
                ones[i + 1] = layer_one(*work[i + 1])
            if i < len(work):
                hidden = after_one(ones.pop(i), *work[i])
            if i >= 1:
                after_two(twos.pop(i - 1), *work[i - 1])
            if i < len(work):
                twos[i] = dot(weights[work[i][1:]][1], hidden, NN)
        return 0

    lax.fori_loop(span[0] // block, span[1] // block, step, 0)


def tower_kernel(
    side, chunk, mix_ref, come_ref, label_ref, weight_ref, tob_ref, tw_ref, tb_ref, tl_ref, dmix_ref, centre_ref, *refs
):
    rows = mix_ref.shape[2]
    if side == 0:
        pred_ref, shared_ref, first, sums = refs
        first[...] = jnp.zeros_like(first)
        sums[...] = jnp.zeros_like(sums)
    tb = [to_column(tb_ref[t : t + 1, :].astype(F32)) for t in range(2)]
    tl = [to_column(tl_ref[t : t + 1, :].astype(F32)) for t in range(2)]

    def step(i, _):
        here = pl.ds(pl.multiple_of(i * chunk, chunk), chunk)
        at = pl.ds(pl.multiple_of(side * rows + i * chunk, chunk), chunk)
        cols = []
        for t in range(2):
            mixed = mix_ref[t, :, here].astype(F32) + come_ref[t, :, here].astype(F32)
            low = mixed.astype(BF16)
            act, slope = gelu_pair(dot(tw_ref[t], low, NN) + tb[t])
            score = jnp.sum(act * tl[t], axis=0, keepdims=True) + tob_ref[0:1, t : t + 1].astype(F32)
            pred = 1.0 / (1.0 + jnp.exp(-score))
            d_score = weight_ref[:, at] * (pred - label_ref[t : t + 1, at])
            d_low = (d_score * tl[t] * slope).astype(BF16)
            d_mixed = dot(tw_ref[t], d_low, TN)
            dmix_ref[t, :, at] = d_mixed
            centre_ref[t : t + 1, at] = jnp.sum(d_mixed * mixed, axis=0, keepdims=True)
            if side == 0:
                pred_ref[t : t + 1, here] = pred
                first[t] += dot(d_low, low, NT)
                cols.append(jnp.sum(act * d_score, axis=1, keepdims=True))
                cols.append(jnp.sum(d_low.astype(F32), axis=1, keepdims=True))
                total = jnp.sum(d_score, axis=1, keepdims=True)
                cols.append(jnp.broadcast_to(total, (64, 1)))
        if side == 0:
            sums[...] += side_by_side([cols[3 * t + n] for n in range(3) for t in range(2)], 64)
        return 0

    lax.fori_loop(0, rows // chunk, step, 0)
    if side == 0:
        for t in range(2):
            fold(shared_ref, 16 * t, first[t])
        fold(shared_ref, 32, sums[...])


def tower_whole_kernel(chunk, mix_ref, come_ref, mix_there, come_there, *refs):
    ins, (dmix_ref, centre_ref, pred_ref, shared_ref, first, sums) = refs[:6], refs[6:]
    tower_kernel(0, chunk, mix_ref, come_ref, *ins, dmix_ref, centre_ref, pred_ref, shared_ref, first, sums)
    tower_kernel(1, chunk, mix_there, come_there, *ins, dmix_ref, centre_ref)


def shared_rows(experts):
    return -(-(48 + 2 * experts + experts // 2) // 16) * 16


def gate_back_kernel(masks, chunk, spot_ref, x_ref, dmix_ref, centre_ref, prob_ref, tower_ref, *refs):
    outs = refs[:8]
    dgate_ref, keep_ref, give_ref, gates, shared_ref = refs[8:]
    depth = outs[0].shape[0]
    experts = 2 * len(masks[0])
    gates[...] = jnp.zeros_like(gates)

    def step(i, _):
        at = pl.ds(pl.multiple_of(i * chunk, chunk), chunk)
        for j in range(8 * depth):
            out = outs[j // depth][j % depth, :, at].astype(F32)
            slot = slot_of(masks, spot_ref, j)
            for t in range(2):
                d_prob = jnp.sum(dmix_ref[t, :, at] * out, axis=0, keepdims=True)
                d_gate = prob_ref[j, t : t + 1, at] * (d_prob - centre_ref[t : t + 1, at])
                gates[pl.ds(t * experts + slot, 1), at] = d_gate
        return 0

    lax.fori_loop(0, x_ref.shape[0] // chunk, step, 0)
    low = gates[...].astype(BF16)
    dgate_ref[...] = low
    shared_ref[...] = jnp.zeros_like(shared_ref)
    shared_ref[:48, :] = tower_ref[...]
    shared_ref[48 : 48 + 2 * experts, :] = dot(low, x_ref[...], NN)
    bias = jnp.sum(low.astype(F32), axis=1, keepdims=True)
    fold(shared_ref, 48 + 2 * experts, side_by_side([bias], 2 * experts))
    deep = keep_ref.shape[0]
    keep_ref[...] = shared_ref[pl.ds(pl.multiple_of(spot_ref[0] * deep, 8), deep), :]
    give_ref[...] = shared_ref[pl.ds(pl.multiple_of((1 - spot_ref[0]) * deep, 8), deep), :]


def backward_kernel(bundles, add, block, x_ref, pay_a, pay_b, low_ref, dmix_ref, *refs):
    kept, refs = (refs[:3], refs[3:6]), refs[6:]
    if add:
        come, refs = refs[:2], refs[2:]
    grads, dones, d_two, sums = refs[:2], refs[2:4], refs[4], refs[5]
    depth = pay_a.shape[0]
    for k in range(depth):
        weights = [second_weight(pay[k]) for pay in (pay_a, pay_b)]
        sums[...] = jnp.zeros_like(sums)

        def step(i, _, k=k, weights=weights):
            at = pl.ds(pl.multiple_of(i * block, block), block)
            for n in range(2):
                _, g1_ref, g2_ref = kept[n]
                j = bundles[n] * depth + k
                d_out = low_ref[j, 0:1, at] * dmix_ref[0, :, at] + low_ref[j, 1:2, at] * dmix_ref[1, :, at]
                two = d_out.astype(BF16).astype(F32) * g2_ref[k, :, at].astype(F32)
                two_low = two.astype(BF16)
                d_two[n, :, at] = two_low
                one = dot(weights[n], two_low, TN) * g1_ref[k, :, at].astype(F32)
                dones[n][k, :, at] = one.astype(BF16)
                add_one, add_two = one[:, :128], two[:, :128]
                for m in range(128, block, 128):
                    add_one = add_one + one[:, m : m + 128]
                    add_two = add_two + two[:, m : m + 128]
                sums[n, :256] += add_one
                sums[n, 256:] += add_two
            return 0

        lax.fori_loop(0, x_ref.shape[0] // block, step, 0)
        for n in range(2):
            h_ref = kept[n][0]
            first = dot(dones[n][k], x_ref[...], NN)
            second = dot(d_two[n], h_ref[k], NT)
            second = jnp.concatenate([second[:64], second[64:]], axis=1)
            row = jnp.concatenate(
                [
                    jnp.sum(sums[n].T, axis=0, keepdims=True),
                    jnp.zeros((1, 128), F32),
                ],
                axis=1,
            )
            high = row.astype(BF16).astype(F32)
            index = lax.broadcasted_iota(jnp.int32, (BIAS_ROWS, 512), 0)
            both = jnp.where(index == 0, high, jnp.where(index == 1, row - high, 0.0))
            if add:
                first = first + come[n][k, :256, :].astype(F32)
                second = second + come[n][k, 256:320, :].astype(F32)
                both = both + come[n][k, 320:, :].astype(F32)
            grads[n][k, :256, :] = first.astype(grads[n].dtype)
            grads[n][k, 256:320, :] = second.astype(grads[n].dtype)
            grads[n][k, 320:, :] = both.astype(grads[n].dtype)


def input_kernel(side, chunk, dgate_ref, gw_ref, *refs):
    experts = gw_ref.shape[1]
    ones, pays, out_ref = refs[:8], refs[8:16], refs[16]
    rows = out_ref.shape[0]

    def step(i, _):
        at = pl.ds(pl.multiple_of(side * rows + i * chunk, chunk), chunk)
        total = dot(dgate_ref[:experts, at], gw_ref[0], TN) + dot(dgate_ref[experts:, at], gw_ref[1], TN)
        for one, pay in zip(ones, pays):
            for k in range(one.shape[0]):
                total = total + dot(one[k, :, at], pay[k, :256, :], TN)
        out_ref[pl.ds(pl.multiple_of(i * chunk, chunk), chunk), :] = total.astype(out_ref.dtype)
        return 0

    lax.fori_loop(0, rows // chunk, step, 0)


def add_kernel(count, *refs):
    total = refs[0][...].astype(F32)
    for ref in refs[1:count]:
        total = total + ref[...].astype(F32)
    for ref in refs[count:]:
        ref[...] = total.astype(ref.dtype)


def input_sum_kernel(own_ref, come_ref, out_ref, done_ref):
    out_ref[...] = own_ref[...] + come_ref[...].astype(F32)
    done_ref[...] = jnp.zeros_like(done_ref)


def finish_kernel(owner_ref, mine_ref, come_ref, w1_ref, b1_ref, w2_ref, b2_ref):
    owner = owner_ref[2] == 1
    mine_ref, come_ref = mine_ref.at[0], come_ref.at[0]
    w1_ref[0] = jnp.where(owner, mine_ref[:256, :], come_ref[:256, :]).T
    second = jnp.where(owner, mine_ref[256:320, :], come_ref[256:320, :])
    w2_ref[0] = jnp.concatenate([second[:, :256], second[:, 256:]], axis=0).T
    bias = jnp.where(owner, mine_ref[320:328, :], come_ref[320:328, :])
    bias = bias[0:1] + bias[1:2]
    b1_ref[...] = bias[:, :256]
    b2_ref[...] = bias[:, 256:384]


def close_kernel(
    experts, spot_ref, keep_ref, give_ref,
    gate_ref, gate_bias_ref, first_ref, tb_ref, tl_ref, tob_ref, done_ref, shared_ref,
):

    base = 48 + 2 * experts
    deep = keep_ref.shape[0]
    shared_ref[pl.ds(pl.multiple_of(spot_ref[0] * deep, 8), deep), :] = keep_ref[...]
    shared_ref[pl.ds(pl.multiple_of((1 - spot_ref[0]) * deep, 8), deep), :] = give_ref[...]
    for t in range(2):
        gate_ref[t] = shared_ref[48 + t * experts : 48 + (t + 1) * experts, :]
        first_ref[t] = unfold(shared_ref, 16 * t, 16)
    small = unfold(shared_ref, 32, 16).T
    tl_ref[...] = small[0:2, :]
    tb_ref[...] = small[2:4, :]
    tob_ref[:, 0:1] = small[4:5, 0:1]
    tob_ref[:, 1:2] = small[5:6, 0:1]
    bias = unfold(shared_ref, base, experts // 2).T
    gate_bias_ref[0:1, :] = bias[0:1, :experts]
    gate_bias_ref[1:2, :] = bias[0:1, experts:]
    done_ref[...] = jnp.zeros_like(done_ref)


def per_device(
    inputs,
    w_first,
    b_first,
    w_second,
    b_second,
    gate_weight,
    gate_bias,
    tower_first_weight,
    tower_first_bias,
    tower_last,
    tower_out_bias,
    labels,
    group_len,
    group_shard,
):
    rows = inputs.shape[0]
    experts = lax.axis_size("expert")
    half = experts // 2
    bits = experts.bit_length() - 1
    depth = half // 8
    pin = True if depth == 1 else None
    chunk = 256 if pin else 512
    core = lax.axis_index("dp")
    place = lax.axis_index("expert")
    owner = core == place // half
    near_bit, mid_bit, end_bit = (2, 2), (1, 0), (0, 1)
    extra = [(b, b) for b in range(bits - 2, 2, -1)]

    def pairs(bit_of_core, want=None, also=0):
        return [
            (c * experts + q, c * experts + (q ^ (1 << bit_of_core[c]) ^ also))
            for c in range(2)
            for q in range(experts)
            if want is None or (c == q // half) == want
        ]

    def send(name, value, bit_of_core, want=None, also=0):
        with jax.named_scope(name):
            return lax.ppermute(value, ("dp", "expert"), pairs(bit_of_core, want, also))

    def swap(name, value):
        with jax.named_scope(name):
            return lax.ppermute(value, "dp", [(0, 1), (1, 0)])

    def deal(value):
        route = []
        for c in range(2):
            for q in range(experts):
                target = c * experts + (q ^ half) if c == q // half else (1 - c) * experts + q
                route.append((c * experts + q, target))
        with jax.named_scope("deal"):
            return lax.ppermute(value, ("dp", "expert"), route)

    def expert_mask(c, j):
        bundle, inner = j // depth, j % depth
        found = sum(1 << extra[e][c] for e in range(len(extra)) if (inner >> e) & 1)
        for n, at in enumerate((near_bit, mid_bit, end_bit)):
            found |= ((bundle >> n) & 1) << at[c]
        return found

    masks = [[expert_mask(c, j) for j in range(half)] for c in range(2)]
    spot = jnp.stack([core, place, owner.astype(jnp.int32)]).astype(jnp.int32)

    def add(values, dtypes, after=()):
        shape = values[0].shape
        outs = [(shape, dtype, True) for dtype in dtypes]
        return call("add", functools.partial(add_kernel, len(values)), values, outs, pin, 0, after=after)

    pay = pack(w_first, w_second, b_first, b_second)
    zero = deal(pay)
    if not extra:
        owners_near = send("owners_near", pay, near_bit, True)
    for at in extra:
        zero = jnp.concatenate([zero, send("pay_extra", zero, at)], axis=0)
    labels_there = swap("labels", labels)
    inputs_there = swap("inputs", inputs)
    gate_rows = jnp.transpose(gate_weight, (0, 2, 1))
    ints = jnp.concatenate([spot, group_shard, group_len])
    outs = [((half, 2, 2 * rows), F32)] * 2 + [((1, 2 * rows), F32), ((2 * rows, 512), BF16), ((2, 2 * rows), F32)]
    kept = pltpu.VMEM if pin else jax.ShapeDtypeStruct
    prob, low, weights, x, both_labels = pl.pallas_call(
        functools.partial(gate_kernel, masks, group_len.shape[0]),
        name="gate",
        in_specs=[SMEM] + [VMEM] * 4 + [ANY] * 2,
        out_specs=[VMEM] * 5,
        out_shape=[kept(shape, dtype) for shape, dtype in outs],
        scratch_shapes=[pltpu.VMEM((2 * experts, 2 * rows), F32), pltpu.SemaphoreType.DMA((2,))],
        compiler_params=pltpu.CompilerParams(vmem_limit_bytes=(8 if pin else 60) * 2**20),
        cost_estimate=pl.CostEstimate(flops=0, bytes_accessed=0, transcendentals=0),
    )(ints, labels, labels_there, gate_rows, gate_bias, inputs, inputs_there)

    pays = [hold(zero, [low])] + [None] * 7
    pays[1] = send("pay_1", pays[0], near_bit, None if extra else False)
    pays[2] = send("pay_2", pays[0], mid_bit)
    pays[4] = send("pay_4", pays[0], end_bit)
    mixed = None
    saved = [None] * 8
    slope_type = F32 if pin else BF16
    for group in GROUPS:
        shape = lambda deep, dtype: ((depth, deep, 2 * rows), dtype, True)
        name = "forward_" + "".join(str(n) for n in group)
        ins = [x, low] + [pays[n] for n in group] + ([] if mixed is None else [mixed])
        kernel = functools.partial(forward_kernel, group, mixed is None, 4 * chunk, chunk)
        outs = [shape(256, BF16), shape(256, BF16), shape(128, BF16), shape(128, slope_type)] * len(group)
        cost = 2.25 * len(group) * depth
        if group != GROUPS[-1]:
            outs.append(((2, 128, 2 * rows), F32, True))
            *kept, mixed = call(name, functools.partial(kernel, (0, 2 * rows)), ins, outs, pin, cost)
        elif extra:
            outs.append(((2, 128, 2 * rows), BF16, True))
            *kept, mixed = call(name, functools.partial(kernel, (0, 2 * rows)), ins, outs, pin, cost)
            mixed_own, mixed_other = mixed[:, :, :rows], mixed[:, :, rows:]
        else:
            outs.append(((2, 128, rows), BF16, True))
            *kept, mixed_other = call(
                name + "_other", functools.partial(kernel, (rows, 2 * rows)), ins, outs, pin, cost / 2
            )
            *kept, mixed_own = call(
                name + "_own", functools.partial(kernel, (0, rows)), ins, outs, pin, cost / 2, alias=kept
            )
        for n, bundle in enumerate(group):
            saved[bundle] = kept[4 * n : 4 * n + 4]
        if group == GROUPS[0]:
            if extra:
                held = hold(pays[1], [pays[2], pays[4], mixed])
            else:
                pays[2] = hold(pays[2], [pays[4], owners_near, mixed])
                (pays[1],) = add([owners_near, pays[1]], [BF16], [pays[2]])
                held = pays[1]
            pays[3] = send("pay_3", held, mid_bit)
            pays[5] = send("pay_5", held, end_bit)
            pays[6] = send("pay_6", pays[2], end_bit)
        if group == GROUPS[LAST_ASK]:
            pays[7] = send("pay_7", hold(pays[3], [mixed]), end_bit)

    tower_ins = [both_labels, weights, tower_out_bias[None], jnp.transpose(tower_first_weight, (0, 2, 1))]
    tower_ins += [tower_first_bias, tower_last]
    tower_outs = [((2, 128, 2 * rows), F32, True), ((2, 2 * rows), F32, True)]
    own_outs = tower_outs + [((2, rows), F32, False), ((48, 512), F32, True)]
    scratch = [pltpu.VMEM((2, 64, 128), F32), pltpu.VMEM((64, 128), F32)]
    come_own, come_other = swap("mixed_other", mixed_other), swap("mixed_own", mixed_own)
    if extra:
        ins = [mixed_own, come_own, mixed_other, come_other, *tower_ins]
        kernel = functools.partial(tower_whole_kernel, 512)
        dmix, centre, predictions, tower_sums = call("tower", kernel, ins, own_outs, pin, 4, scratch)
    else:
        ins = [mixed_own, come_own, *tower_ins]
        kernel = functools.partial(tower_kernel, 0, 512)
        *begun, predictions, tower_sums = call("tower_own", kernel, ins, own_outs, pin, 2, scratch)
        ins = [mixed_other, come_other, *tower_ins]
        kernel = functools.partial(tower_kernel, 1, 512)
        dmix, centre = call("tower_other", kernel, ins, tower_outs, pin, 2, alias=begun)

    def back(a, b, come, dtype, cost, after=()):
        grad = ((depth, PAY_ROWS, 512), dtype, False)
        done = ((depth, 256, 2 * rows), BF16, True)
        return call(
            f"backward_{a}{b}",
            functools.partial(backward_kernel, (a, b), come is not None, BACK_CHUNK),
            [x, pays[a], pays[b], low, dmix]
            + [saved[n][m] for n in (a, b) for m in (0, 1, 3)]
            + list(come or ()),
            [grad, grad, done, done],
            pin,
            cost,
            [pltpu.VMEM((2, 128, 2 * rows), BF16), pltpu.VMEM((2, 384, 128), F32)],
            after=after,
        )

    ones = [None] * 8
    grad_six, grad_seven, ones[6], ones[7] = back(6, 7, None, BF16, 5)
    six, seven = send("grad_six", grad_six, end_bit), send("grad_seven", grad_seven, end_bit)
    grad_four, grad_five, ones[4], ones[5] = back(4, 5, None, BF16, 1, [ones[7]])
    five, four = send("grad_five", grad_five, end_bit), send("grad_four", grad_four, end_bit)
    deep = shared_rows(experts) // 2
    dgate, keep, give = call(
        "gate_back",
        functools.partial(gate_back_kernel, masks, 512),
        [ints, x, dmix, centre, prob, tower_sums] + [kept[2] for kept in saved],
        [((2 * experts, 2 * rows), BF16, True)] + [((deep, 512), F32, True)] * 2,
        pin,
        1,
        [pltpu.VMEM((2 * experts, 2 * rows), F32), pltpu.VMEM((2 * deep, 512), F32)],
        1,
        after=[ones[5]],
    )
    (keep,) = add([keep, swap("give", give)], [F32])
    grad_two, grad_three, ones[2], ones[3] = back(2, 3, (six, seven), BF16, 1, [keep])
    three, two = send("grad_three", grad_three, mid_bit), send("grad_two", grad_two, mid_bit)
    stages = []
    for b in range(2, bits):
        (keep,) = add([keep, send(f"shared_{b}", keep, (b, b))], [F32], [ones[3]])
        stages.append(keep)

    grad_zero, grad_one, ones[0], ones[1] = back(0, 1, (four, five), F32, 1, [ones[3], stages[0]])
    def input_gradient(side, dtype, after=()):
        (out,) = call(
            f"input_{side}",
            functools.partial(input_kernel, side, 512),
            [dgate, gate_rows, *ones, *pays],
            [((rows, 512), dtype, True)],
            pin,
            3.5 * depth,
            after=after,
        )
        return out

    over = input_gradient(1, BF16, [stages[1]])
    own = input_gradient(0, F32)
    top = bits - 1
    (one,) = add([grad_one, three], [BF16], [over])
    if extra:
        (zero,) = add([grad_zero, two, send("near", one, near_bit)], [F32])
        for at in reversed(extra):
            count = zero.shape[0] // 2
            zero = zero[:count] + send("extra", zero[count:].astype(BF16), at).astype(F32)
        low_zero = zero.astype(BF16)
        pieces = []
    else:
        pieces = [send("near", one, near_bit, True), send("cross", one, (top, top), False, 1 << near_bit[0])]
        zero, low_zero = add([grad_zero, two], [F32, BF16])
    pieces = [zero, *pieces, send("far", low_zero, (top, top), False)]
    (keep,) = add([keep, send("shared_1", keep, (1, 1))], [F32], [low_zero, own])
    (keep,) = add([keep, send("shared_0", keep, (0, 0))], [F32])
    give = swap("keep", keep)
    grad_gate, grad_gate_bias, tower_first, tower_bias, last, out_bias, done = call(
        "close",
        functools.partial(close_kernel, experts),
        [ints, keep, give],
        [
            ((2, experts, 512), F32, False),
            ((2, experts), F32, False),
            ((2, 64, 128), F32, False),
            ((2, 64), F32, False),
            ((2, 64), F32, False),
            ((1, 2), F32, False),
            ((8, 128), F32, True),
        ],
        pin,
        1,
        [pltpu.VMEM((2 * deep, 512), F32)],
        1,
    )
    (final,) = add(pieces, [F32], [done, own])

    input_grad, summed = call(
        "input_sum",
        input_sum_kernel,
        [own, swap("over", over)],
        [((rows, 512), F32, False), ((8, 128), F32, True)],
        pin,
        1.5,
        after=[final],
    )
    grad_w_first, grad_b_first, grad_w_second, grad_b_second = call(
        "finish",
        finish_kernel,
        [ints, final, swap("final", final)],
        [
            ((1, 512, 256), F32, False),
            ((1, 256), F32, False),
            ((1, 256, 128), F32, False),
            ((1, 128), F32, False),
        ],
        pin,
        TAIL,
        scalars=1,
        after=[summed],
    )
    return (
        predictions,
        input_grad,
        grad_w_first,
        grad_b_first,
        grad_w_second,
        grad_b_second,
        jnp.transpose(grad_gate, (0, 2, 1)),
        grad_gate_bias,
        jnp.transpose(tower_first, (0, 2, 1)),
        tower_bias,
        last,
        out_bias[0],
    )


def solution(mesh):
    in_specs = (
        P(("dp", "expert"), None),
        P("expert", None, None),
        P("expert", None),
        P("expert", None, None),
        P("expert", None),
        P(),
        P(),
        P(),
        P(),
        P(),
        P(),
        P(None, ("dp", "expert")),
        P(),
        P(),
    )
    out_specs = (
        P(None, ("dp", "expert")),
        P(("dp", "expert"), None),
        P("expert", None, None),
        P("expert", None),
        P("expert", None, None),
        P("expert", None),
        P(),
        P(),
        P(),
        P(),
        P(),
        P(),
    )
    return jax.shard_map(
        per_device, mesh=mesh, in_specs=in_specs, out_specs=out_specs, check_vma=False
    )
```

```python
import functools

import jax
import jax.numpy as jnp
from jax import lax
from jax.experimental import pallas as pl
from jax.experimental.pallas import tpu as pltpu
from jax.sharding import PartitionSpec as P

F32 = jnp.float32
BF16 = jnp.bfloat16
ROOT = 0.7978845608028654
CUBE = 0.044715
NN = (((1,), (0,)), ((), ()))
NT = (((1,), (1,)), ((), ()))
TN = (((0,), (0,)), ((), ()))
TT = (((0,), (1,)), ((), ()))
BIAS_ROWS = 16
SCALE = 3e8
EARLY = 6
BACK_CHUNK = 2048
TAIL = 10
GROUPS = ((0,), (1, 4), (2,), (3, 5), (6, 7))
LAST_ASK = 2
PAY_ROWS = 320 + BIAS_ROWS
VMEM = pl.BlockSpec(memory_space=pltpu.VMEM)
SMEM = pl.BlockSpec(memory_space=pltpu.SMEM)
ANY = pl.BlockSpec(memory_space=pl.ANY)


def dot(a, b, dims):
    return lax.dot_general(a, b, dims, preferred_element_type=F32)


def gelu_pair(v):
    square = v * v
    upper = 0.5 + 0.5 * jnp.tanh(v * (ROOT + (ROOT * CUBE) * square))
    value = v * upper
    slope = upper + value * (1.0 - upper) * (2.0 * ROOT + (6.0 * ROOT * CUBE) * square)
    return value, slope


def call(name, kernel, ins, outs, pin, micros, scratch=(), scalars=0, limit=8, after=(), alias=()):
    limit = limit if pin is not None else 60
    pinned = lambda a: pltpu.with_memory_space_constraint(a, pltpu.VMEM) if pin else a
    args = [a if n < scalars else pinned(a) for n, a in enumerate(ins)] + [pinned(a) for a in alias] + list(after)
    count, skip = len(ins), len(alias) + len(after)
    body = kernel
    if skip:

        def body(*refs):
            return kernel(*refs[:count], *refs[count + skip :])

    kept = pltpu.VMEM if pin else jax.ShapeDtypeStruct
    shapes = [(kept if stay else jax.ShapeDtypeStruct)(shape, dtype) for shape, dtype, stay in outs]
    return pl.pallas_call(
        body,
        name=name,
        in_specs=[SMEM] * scalars + [VMEM] * (count - scalars + len(alias)) + [ANY] * len(after),
        input_output_aliases={count + n: n for n in range(len(alias))},
        out_specs=[VMEM] * len(outs),
        out_shape=shapes,
        scratch_shapes=list(scratch),
        compiler_params=pltpu.CompilerParams(vmem_limit_bytes=limit * 2**20),
        cost_estimate=pl.CostEstimate(flops=int(micros * SCALE), bytes_accessed=0, transcendentals=0),
    )(*args)


def hold(value, after):
    count = len(after)
    return pl.pallas_call(
        lambda *refs: None,
        name="hold",
        in_specs=[ANY] * (1 + count),
        out_specs=ANY,
        out_shape=jax.ShapeDtypeStruct(value.shape, value.dtype),
        input_output_aliases={0: 0},
        compiler_params=pltpu.CompilerParams(vmem_limit_bytes=2**20),
        cost_estimate=pl.CostEstimate(flops=0, bytes_accessed=0, transcendentals=0),
    )(value, *after)


def slot_of(masks, int_ref, j):
    half = len(masks[0])
    mask = jnp.where(int_ref[0] == 0, masks[0][j], masks[1][j])
    return int_ref[0] * half + ((int_ref[1] & (half - 1)) ^ mask)


def to_column(row):
    n = row.shape[1]
    same = lax.broadcasted_iota(jnp.int32, (n, n), 0) == lax.broadcasted_iota(jnp.int32, (n, n), 1)
    return jnp.sum(jnp.where(same, jnp.broadcast_to(row, (n, n)), 0.0), axis=1, keepdims=True)


def side_by_side(columns, tall):
    lane = lax.broadcasted_iota(jnp.int32, (tall, 128), 1)
    small = jnp.zeros((tall, 128), F32)
    for n, col in enumerate(columns):
        small = jnp.where(lane == n, jnp.broadcast_to(col, (tall, 128)), small)
    return small


def fold(ref, base, block):
    deep = block.shape[0] // 4
    for k in range(4):
        ref[base : base + deep, 128 * k : 128 * (k + 1)] = block[deep * k : deep * (k + 1)]


def unfold(ref, base, deep):
    return jnp.concatenate(
        [ref[base : base + deep, 128 * k : 128 * (k + 1)] for k in range(4)], axis=0
    )


def pack_kernel(w1_ref, w2_ref, b1_ref, b2_ref, pay_ref, w1, w2, b1, b2, sems):
    copies = [
        pltpu.make_async_copy(src, dst, sems.at[n])
        for n, (src, dst) in enumerate(((w1_ref, w1), (w2_ref, w2), (b1_ref, b1), (b2_ref, b2)))
    ]
    for copy in copies:
        copy.start()
    for copy in copies[1:]:
        copy.wait()
    second = w2[0].astype(F32).T.astype(BF16)
    pay_ref[0, 256:320, :256] = second[:64]
    pay_ref[0, 256:320, 256:] = second[64:]
    row = jnp.concatenate([b1[...].astype(F32), b2[...].astype(F32), jnp.zeros((1, 128), F32)], axis=1)
    pay_ref[0, 320:, :] = jnp.broadcast_to(row, (BIAS_ROWS, 512)).astype(BF16)
    copies[0].wait()
    pay_ref[0, :256, :] = w1[0].astype(F32).T.astype(BF16)


def pack(w1, w2, b1, b2):
    arrays = (w1, w2, b1, b2)
    return pl.pallas_call(
        pack_kernel,
        name="pack",
        in_specs=[pl.BlockSpec(memory_space=pltpu.HBM)] * 4,
        out_specs=VMEM,
        out_shape=jax.ShapeDtypeStruct((1, PAY_ROWS, 512), BF16),
        scratch_shapes=[pltpu.VMEM(a.shape, a.dtype) for a in arrays] + [pltpu.SemaphoreType.DMA((4,))],
        compiler_params=pltpu.CompilerParams(vmem_limit_bytes=8 * 2**20),
        cost_estimate=pl.CostEstimate(flops=0, bytes_accessed=0, transcendentals=0),
    )(*[pltpu.with_memory_space_constraint(a, pltpu.HBM) for a in arrays])


def biases(pay):
    flipped = pay[320:, :].astype(F32).T
    return flipped[:256, 0:1], flipped[256:384, 0:1]


def second_weight(pay):
    return jnp.concatenate([pay[256:320, :256], pay[256:320, 256:]], axis=0)


def gate_kernel(masks, groups, int_ref, label_ref, there_ref, gw_ref, gb_ref, mine_ref, other_ref, *refs):
    prob_ref, low_ref, weight_ref, x_out, label_out, scratch, sems = refs
    rows = mine_ref.shape[0]
    experts = 2 * len(masks[0])
    copies = [
        pltpu.make_async_copy(src, x_out.at[pl.ds(n * rows, rows), :], sems.at[n])
        for n, src in enumerate((mine_ref, other_ref))
    ]
    for copy in copies:
        copy.start()
    for side in range(2):
        at = slice(side * rows, (side + 1) * rows)
        label_out[:, at] = (label_ref, there_ref)[side][...].astype(F32)
        copies[side].wait()
        for t in range(2):
            part = dot(gw_ref[t], x_out[at, :], NT) + to_column(gb_ref[t : t + 1, :].astype(F32))
            top = jnp.max(part, axis=0, keepdims=True)
            e = jnp.exp(part - top)
            scratch[t * experts : (t + 1) * experts, at] = e / jnp.sum(e, axis=0, keepdims=True)
        shard = int_ref[0] if side == 0 else 1 - int_ref[0]
        index = int_ref[1] * rows + lax.broadcasted_iota(jnp.int32, (1, rows), 1)
        start = jnp.int32(0)
        weight = jnp.zeros((1, rows), F32)
        for g in range(groups):
            length = int_ref[3 + groups + g]
            size = jnp.where(int_ref[3 + g] == shard, length, 0)
            inside = (index >= start) & (index < start + size)
            recip = 1.0 / jnp.full((1, rows), length, jnp.int32).astype(F32)
            weight = weight + jnp.where(inside, recip, 0.0)
            start = start + size
        weight_ref[:, at] = weight
    for j in range(experts // 2):
        slot = slot_of(masks, int_ref, j)
        for t in range(2):
            row = scratch[pl.ds(t * experts + slot, 1), :]
            prob_ref[j, t : t + 1, :] = row
            low_ref[j, t : t + 1, :] = row.astype(BF16).astype(F32)


def forward_kernel(bundles, first, block, chunk, span, x_ref, low_ref, *refs):
    count = len(bundles)
    pays, refs = refs[:count], refs[count:]
    if not first:
        mix_in, *refs = refs
    kept, mix_ref = [refs[4 * n : 4 * n + 4] for n in range(count)], refs[4 * count]
    depth = pays[0].shape[0]
    weights = {}
    for k in range(depth):
        for n, pay_ref in enumerate(pays):
            pay = pay_ref[k]
            weights[k, n] = (pay[:256], second_weight(pay), *biases(pay))
    out_from = 0 if mix_ref.shape[2] == x_ref.shape[0] else span[0]
    work = [(c, k, n) for c in range(0, block, chunk) for k in range(depth) for n in range(count)]

    def step(i, _):
        base = pl.multiple_of(i * block, block)
        totals = [None, None]

        def layer_one(c, k, n):
            return dot(weights[k, n][0], x_ref[pl.ds(base + c, chunk), :], NT)

        def after_one(pre, c, k, n):
            value, slope = gelu_pair(pre + weights[k, n][2])
            hidden = value.astype(BF16)
            kept[n][0][k, :, pl.ds(base + c, chunk)] = hidden
            kept[n][1][k, :, pl.ds(base + c, chunk)] = slope.astype(kept[n][1].dtype)
            return hidden

        def after_two(pre, c, k, n):
            at = pl.ds(base + c, chunk)
            value, slope = gelu_pair(pre + weights[k, n][3])
            out = value.astype(BF16)
            kept[n][2][k, :, at] = out
            kept[n][3][k, :, at] = slope.astype(kept[n][3].dtype)
            out = out.astype(F32)
            for t in range(2):
                term = low_ref[bundles[n] * depth + k, t : t + 1, at] * out
                if k == 0 and n == 0:
                    totals[t] = term if first else mix_in[t, :, at] + term
                else:
                    totals[t] = totals[t] + term
                if k == depth - 1 and n == count - 1:
                    mix_ref[t, :, pl.ds(base + c - out_from, chunk)] = totals[t].astype(mix_ref.dtype)

        ones, twos = {0: layer_one(*work[0])}, {}
        for i in range(len(work) + 1):
            if i + 1 < len(work):
                ones[i + 1] = layer_one(*work[i + 1])
            if i < len(work):
                hidden = after_one(ones.pop(i), *work[i])
            if i >= 1:
                after_two(twos.pop(i - 1), *work[i - 1])
            if i < len(work):
                twos[i] = dot(weights[work[i][1:]][1], hidden, NN)
        return 0

    lax.fori_loop(span[0] // block, span[1] // block, step, 0)


def tower_kernel(
    side, chunk, mix_ref, come_ref, label_ref, weight_ref, tob_ref, tw_ref, tb_ref, tl_ref, dmix_ref, centre_ref, *refs
):
    rows = mix_ref.shape[2]
    if side == 0:
        pred_ref, shared_ref, first, sums = refs
        first[...] = jnp.zeros_like(first)
        sums[...] = jnp.zeros_like(sums)
    tb = [to_column(tb_ref[t : t + 1, :].astype(F32)) for t in range(2)]
    tl = [to_column(tl_ref[t : t + 1, :].astype(F32)) for t in range(2)]

    def step(i, _):
        here = pl.ds(pl.multiple_of(i * chunk, chunk), chunk)
        at = pl.ds(pl.multiple_of(side * rows + i * chunk, chunk), chunk)
        cols = []
        for t in range(2):
            mixed = mix_ref[t, :, here].astype(F32) + come_ref[t, :, here].astype(F32)
            low = mixed.astype(BF16)
            act, slope = gelu_pair(dot(tw_ref[t], low, NN) + tb[t])
            score = jnp.sum(act * tl[t], axis=0, keepdims=True) + tob_ref[0:1, t : t + 1].astype(F32)
            pred = 1.0 / (1.0 + jnp.exp(-score))
            d_score = weight_ref[:, at] * (pred - label_ref[t : t + 1, at])
            d_low = (d_score * tl[t] * slope).astype(BF16)
            d_mixed = dot(tw_ref[t], d_low, TN)
            dmix_ref[t, :, at] = d_mixed
            centre_ref[t : t + 1, at] = jnp.sum(d_mixed * mixed, axis=0, keepdims=True)
            if side == 0:
                pred_ref[t : t + 1, here] = pred
                first[t] += dot(d_low, low, NT)
                cols.append(jnp.sum(act * d_score, axis=1, keepdims=True))
                cols.append(jnp.sum(d_low.astype(F32), axis=1, keepdims=True))
                total = jnp.sum(d_score, axis=1, keepdims=True)
                cols.append(jnp.broadcast_to(total, (64, 1)))
        if side == 0:
            sums[...] += side_by_side([cols[3 * t + n] for n in range(3) for t in range(2)], 64)
        return 0

    lax.fori_loop(0, rows // chunk, step, 0)
    if side == 0:
        for t in range(2):
            fold(shared_ref, 16 * t, first[t])
        fold(shared_ref, 32, sums[...])


def tower_whole_kernel(chunk, mix_ref, come_ref, mix_there, come_there, *refs):
    ins, (dmix_ref, centre_ref, pred_ref, shared_ref, first, sums) = refs[:6], refs[6:]
    tower_kernel(0, chunk, mix_ref, come_ref, *ins, dmix_ref, centre_ref, pred_ref, shared_ref, first, sums)
    tower_kernel(1, chunk, mix_there, come_there, *ins, dmix_ref, centre_ref)


def shared_rows(experts):
    return -(-(48 + 2 * experts + experts // 2) // 16) * 16


def gate_back_kernel(masks, chunk, spot_ref, x_ref, dmix_ref, centre_ref, prob_ref, tower_ref, *refs):
    outs = refs[:8]
    dgate_ref, keep_ref, give_ref, gates, shared_ref = refs[8:]
    depth = outs[0].shape[0]
    experts = 2 * len(masks[0])
    gates[...] = jnp.zeros_like(gates)

    def step(i, _):
        at = pl.ds(pl.multiple_of(i * chunk, chunk), chunk)
        for j in range(8 * depth):
            out = outs[j // depth][j % depth, :, at].astype(F32)
            slot = slot_of(masks, spot_ref, j)
            for t in range(2):
                d_prob = jnp.sum(dmix_ref[t, :, at] * out, axis=0, keepdims=True)
                d_gate = prob_ref[j, t : t + 1, at] * (d_prob - centre_ref[t : t + 1, at])
                gates[pl.ds(t * experts + slot, 1), at] = d_gate
        return 0

    lax.fori_loop(0, x_ref.shape[0] // chunk, step, 0)
    low = gates[...].astype(BF16)
    dgate_ref[...] = low
    shared_ref[...] = jnp.zeros_like(shared_ref)
    shared_ref[:48, :] = tower_ref[...]
    shared_ref[48 : 48 + 2 * experts, :] = dot(low, x_ref[...], NN)
    bias = jnp.sum(low.astype(F32), axis=1, keepdims=True)
    fold(shared_ref, 48 + 2 * experts, side_by_side([bias], 2 * experts))
    deep = keep_ref.shape[0]
    keep_ref[...] = shared_ref[pl.ds(pl.multiple_of(spot_ref[0] * deep, 8), deep), :]
    give_ref[...] = shared_ref[pl.ds(pl.multiple_of((1 - spot_ref[0]) * deep, 8), deep), :]


def backward_kernel(bundles, add, block, x_ref, pay_a, pay_b, low_ref, dmix_ref, *refs):
    kept, refs = (refs[:3], refs[3:6]), refs[6:]
    if add:
        come, refs = refs[:2], refs[2:]
    grads, dones, d_two, sums = refs[:2], refs[2:4], refs[4], refs[5]
    depth = pay_a.shape[0]
    for k in range(depth):
        weights = [second_weight(pay[k]) for pay in (pay_a, pay_b)]
        sums[...] = jnp.zeros_like(sums)

        def step(i, _, k=k, weights=weights):
            at = pl.ds(pl.multiple_of(i * block, block), block)
            for n in range(2):
                _, g1_ref, g2_ref = kept[n]
                j = bundles[n] * depth + k
                d_out = low_ref[j, 0:1, at] * dmix_ref[0, :, at] + low_ref[j, 1:2, at] * dmix_ref[1, :, at]
                two = d_out.astype(BF16).astype(F32) * g2_ref[k, :, at].astype(F32)
                two_low = two.astype(BF16)
                d_two[n, :, at] = two_low
                one = dot(weights[n], two_low, TN) * g1_ref[k, :, at].astype(F32)
                dones[n][k, :, at] = one.astype(BF16)
                add_one, add_two = one[:, :128], two[:, :128]
                for m in range(128, block, 128):
                    add_one = add_one + one[:, m : m + 128]
                    add_two = add_two + two[:, m : m + 128]
                sums[n, :256] += add_one
                sums[n, 256:] += add_two
            return 0

        lax.fori_loop(0, x_ref.shape[0] // block, step, 0)
        for n in range(2):
            h_ref = kept[n][0]
            first = dot(dones[n][k], x_ref[...], NN)
            second = dot(d_two[n], h_ref[k], NT)
            second = jnp.concatenate([second[:64], second[64:]], axis=1)
            row = jnp.concatenate(
                [
                    jnp.sum(sums[n].T, axis=0, keepdims=True),
                    jnp.zeros((1, 128), F32),
                ],
                axis=1,
            )
            high = row.astype(BF16).astype(F32)
            index = lax.broadcasted_iota(jnp.int32, (BIAS_ROWS, 512), 0)
            both = jnp.where(index == 0, high, jnp.where(index == 1, row - high, 0.0))
            if add:
                first = first + come[n][k, :256, :].astype(F32)
                second = second + come[n][k, 256:320, :].astype(F32)
                both = both + come[n][k, 320:, :].astype(F32)
            grads[n][k, :256, :] = first.astype(grads[n].dtype)
            grads[n][k, 256:320, :] = second.astype(grads[n].dtype)
            grads[n][k, 320:, :] = both.astype(grads[n].dtype)


def input_kernel(side, chunk, dgate_ref, gw_ref, *refs):
    experts = gw_ref.shape[1]
    ones, pays, out_ref = refs[:8], refs[8:16], refs[16]
    rows = out_ref.shape[0]

    def step(i, _):
        at = pl.ds(pl.multiple_of(side * rows + i * chunk, chunk), chunk)
        total = dot(dgate_ref[:experts, at], gw_ref[0], TN) + dot(dgate_ref[experts:, at], gw_ref[1], TN)
        for one, pay in zip(ones, pays):
            for k in range(one.shape[0]):
                total = total + dot(one[k, :, at], pay[k, :256, :], TN)
        out_ref[pl.ds(pl.multiple_of(i * chunk, chunk), chunk), :] = total.astype(out_ref.dtype)
        return 0

    lax.fori_loop(0, rows // chunk, step, 0)


def add_kernel(count, *refs):
    total = refs[0][...].astype(F32)
    for ref in refs[1:count]:
        total = total + ref[...].astype(F32)
    for ref in refs[count:]:
        ref[...] = total.astype(ref.dtype)


def input_sum_kernel(own_ref, come_ref, out_ref, done_ref):
    out_ref[...] = own_ref[...] + come_ref[...].astype(F32)
    done_ref[...] = jnp.zeros_like(done_ref)


def finish_kernel(owner_ref, mine_ref, come_ref, w1_ref, b1_ref, w2_ref, b2_ref):
    owner = owner_ref[2] == 1
    mine_ref, come_ref = mine_ref.at[0], come_ref.at[0]
    w1_ref[0] = jnp.where(owner, mine_ref[:256, :], come_ref[:256, :]).T
    second = jnp.where(owner, mine_ref[256:320, :], come_ref[256:320, :])
    w2_ref[0] = jnp.concatenate([second[:, :256], second[:, 256:]], axis=0).T
    bias = jnp.where(owner, mine_ref[320:328, :], come_ref[320:328, :])
    bias = bias[0:1] + bias[1:2]
    b1_ref[...] = bias[:, :256]
    b2_ref[...] = bias[:, 256:384]


def close_kernel(
    experts, spot_ref, keep_ref, give_ref,
    gate_ref, gate_bias_ref, first_ref, tb_ref, tl_ref, tob_ref, done_ref, shared_ref,
):

    base = 48 + 2 * experts
    deep = keep_ref.shape[0]
    shared_ref[pl.ds(pl.multiple_of(spot_ref[0] * deep, 8), deep), :] = keep_ref[...]
    shared_ref[pl.ds(pl.multiple_of((1 - spot_ref[0]) * deep, 8), deep), :] = give_ref[...]
    for t in range(2):
        gate_ref[t] = shared_ref[48 + t * experts : 48 + (t + 1) * experts, :]
        first_ref[t] = unfold(shared_ref, 16 * t, 16)
    small = unfold(shared_ref, 32, 16).T
    tl_ref[...] = small[0:2, :]
    tb_ref[...] = small[2:4, :]
    tob_ref[:, 0:1] = small[4:5, 0:1]
    tob_ref[:, 1:2] = small[5:6, 0:1]
    bias = unfold(shared_ref, base, experts // 2).T
    gate_bias_ref[0:1, :] = bias[0:1, :experts]
    gate_bias_ref[1:2, :] = bias[0:1, experts:]
    done_ref[...] = jnp.zeros_like(done_ref)


def per_device(
    inputs,
    w_first,
    b_first,
    w_second,
    b_second,
    gate_weight,
    gate_bias,
    tower_first_weight,
    tower_first_bias,
    tower_last,
    tower_out_bias,
    labels,
    group_len,
    group_shard,
):
    rows = inputs.shape[0]
    experts = lax.axis_size("expert")
    half = experts // 2
    bits = experts.bit_length() - 1
    depth = half // 8
    pin = True if depth == 1 else None
    chunk = 256 if pin else 512
    core = lax.axis_index("dp")
    place = lax.axis_index("expert")
    owner = core == place // half
    near_bit, mid_bit, end_bit = (2, 2), (1, 0), (0, 1)
    extra = [(b, b) for b in range(bits - 2, 2, -1)]

    def pairs(bit_of_core, want=None, also=0):
        return [
            (c * experts + q, c * experts + (q ^ (1 << bit_of_core[c]) ^ also))
            for c in range(2)
            for q in range(experts)
            if want is None or (c == q // half) == want
        ]

    def send(name, value, bit_of_core, want=None, also=0):
        with jax.named_scope(name):
            return lax.ppermute(value, ("dp", "expert"), pairs(bit_of_core, want, also))

    def swap(name, value):
        with jax.named_scope(name):
            return lax.ppermute(value, "dp", [(0, 1), (1, 0)])

    def deal(value):
        route = []
        for c in range(2):
            for q in range(experts):
                target = c * experts + (q ^ half) if c == q // half else (1 - c) * experts + q
                route.append((c * experts + q, target))
        with jax.named_scope("deal"):
            return lax.ppermute(value, ("dp", "expert"), route)

    def expert_mask(c, j):
        bundle, inner = j // depth, j % depth
        found = sum(1 << extra[e][c] for e in range(len(extra)) if (inner >> e) & 1)
        for n, at in enumerate((near_bit, mid_bit, end_bit)):
            found |= ((bundle >> n) & 1) << at[c]
        return found

    masks = [[expert_mask(c, j) for j in range(half)] for c in range(2)]
    spot = jnp.stack([core, place, owner.astype(jnp.int32)]).astype(jnp.int32)

    def add(values, dtypes, after=()):
        shape = values[0].shape
        outs = [(shape, dtype, True) for dtype in dtypes]
        return call("add", functools.partial(add_kernel, len(values)), values, outs, pin, 0, after=after)

    pay = pack(w_first, w_second, b_first, b_second)
    zero = deal(pay)
    if not extra:
        owners_near = send("owners_near", pay, near_bit, True)
    for at in extra:
        zero = jnp.concatenate([zero, send("pay_extra", zero, at)], axis=0)
    labels_there = swap("labels", labels)
    inputs_there = swap("inputs", inputs)
    gate_rows = jnp.transpose(gate_weight, (0, 2, 1))
    ints = jnp.concatenate([spot, group_shard, group_len])
    outs = [((half, 2, 2 * rows), F32)] * 2 + [((1, 2 * rows), F32), ((2 * rows, 512), BF16), ((2, 2 * rows), F32)]
    kept = pltpu.VMEM if pin else jax.ShapeDtypeStruct
    prob, low, weights, x, both_labels = pl.pallas_call(
        functools.partial(gate_kernel, masks, group_len.shape[0]),
        name="gate",
        in_specs=[SMEM] + [VMEM] * 4 + [ANY] * 2,
        out_specs=[VMEM] * 5,
        out_shape=[kept(shape, dtype) for shape, dtype in outs],
        scratch_shapes=[pltpu.VMEM((2 * experts, 2 * rows), F32), pltpu.SemaphoreType.DMA((2,))],
        compiler_params=pltpu.CompilerParams(vmem_limit_bytes=(8 if pin else 60) * 2**20),
        cost_estimate=pl.CostEstimate(flops=0, bytes_accessed=0, transcendentals=0),
    )(ints, labels, labels_there, gate_rows, gate_bias, inputs, inputs_there)

    pays = [hold(zero, [low])] + [None] * 7
    pays[1] = send("pay_1", pays[0], near_bit, None if extra else False)
    pays[2] = send("pay_2", pays[0], mid_bit)
    pays[4] = send("pay_4", pays[0], end_bit)
    mixed = None
    saved = [None] * 8
    slope_type = F32 if pin else BF16
    for group in GROUPS:
        shape = lambda deep, dtype: ((depth, deep, 2 * rows), dtype, True)
        name = "forward_" + "".join(str(n) for n in group)
        ins = [x, low] + [pays[n] for n in group] + ([] if mixed is None else [mixed])
        kernel = functools.partial(forward_kernel, group, mixed is None, 4 * chunk, chunk)
        outs = [shape(256, BF16), shape(256, BF16), shape(128, BF16), shape(128, slope_type)] * len(group)
        cost = 2.25 * len(group) * depth
        if group != GROUPS[-1]:
            outs.append(((2, 128, 2 * rows), F32, True))
            *kept, mixed = call(name, functools.partial(kernel, (0, 2 * rows)), ins, outs, pin, cost)
        elif extra:
            outs.append(((2, 128, 2 * rows), BF16, True))
            *kept, mixed = call(name, functools.partial(kernel, (0, 2 * rows)), ins, outs, pin, cost)
            mixed_own, mixed_other = mixed[:, :, :rows], mixed[:, :, rows:]
        else:
            outs.append(((2, 128, rows), BF16, True))
            *kept, mixed_other = call(
                name + "_other", functools.partial(kernel, (rows, 2 * rows)), ins, outs, pin, cost / 2
            )
            *kept, mixed_own = call(
                name + "_own", functools.partial(kernel, (0, rows)), ins, outs, pin, cost / 2, alias=kept
            )
        for n, bundle in enumerate(group):
            saved[bundle] = kept[4 * n : 4 * n + 4]
        if group == GROUPS[0]:
            if extra:
                held = hold(pays[1], [pays[2], pays[4], mixed])
            else:
                pays[2] = hold(pays[2], [pays[4], owners_near, mixed])
                (pays[1],) = add([owners_near, pays[1]], [BF16], [pays[2]])
                held = pays[1]
            pays[3] = send("pay_3", held, mid_bit)
            pays[5] = send("pay_5", held, end_bit)
            pays[6] = send("pay_6", pays[2], end_bit)
        if group == GROUPS[LAST_ASK]:
            pays[7] = send("pay_7", hold(pays[3], [mixed]), end_bit)

    tower_ins = [both_labels, weights, tower_out_bias[None], jnp.transpose(tower_first_weight, (0, 2, 1))]
    tower_ins += [tower_first_bias, tower_last]
    tower_outs = [((2, 128, 2 * rows), F32, True), ((2, 2 * rows), F32, True)]
    own_outs = tower_outs + [((2, rows), F32, False), ((48, 512), F32, True)]
    scratch = [pltpu.VMEM((2, 64, 128), F32), pltpu.VMEM((64, 128), F32)]
    come_own, come_other = swap("mixed_other", mixed_other), swap("mixed_own", mixed_own)
    if extra:
        ins = [mixed_own, come_own, mixed_other, come_other, *tower_ins]
        kernel = functools.partial(tower_whole_kernel, 512)
        dmix, centre, predictions, tower_sums = call("tower", kernel, ins, own_outs, pin, 4, scratch)
    else:
        ins = [mixed_own, come_own, *tower_ins]
        kernel = functools.partial(tower_kernel, 0, 512)
        *begun, predictions, tower_sums = call("tower_own", kernel, ins, own_outs, pin, 2, scratch)
        ins = [mixed_other, come_other, *tower_ins]
        kernel = functools.partial(tower_kernel, 1, 512)
        dmix, centre = call("tower_other", kernel, ins, tower_outs, pin, 2, alias=begun)

    def back(a, b, come, dtype, cost, after=()):
        grad = ((depth, PAY_ROWS, 512), dtype, False)
        done = ((depth, 256, 2 * rows), BF16, True)
        return call(
            f"backward_{a}{b}",
            functools.partial(backward_kernel, (a, b), come is not None, BACK_CHUNK),
            [x, pays[a], pays[b], low, dmix]
            + [saved[n][m] for n in (a, b) for m in (0, 1, 3)]
            + list(come or ()),
            [grad, grad, done, done],
            pin,
            cost,
            [pltpu.VMEM((2, 128, 2 * rows), BF16), pltpu.VMEM((2, 384, 128), F32)],
            after=after,
        )

    ones = [None] * 8
    grad_six, grad_seven, ones[6], ones[7] = back(6, 7, None, BF16, 5)
    six, seven = send("grad_six", grad_six, end_bit), send("grad_seven", grad_seven, end_bit)
    grad_four, grad_five, ones[4], ones[5] = back(4, 5, None, BF16, 1, [ones[7]])
    five, four = send("grad_five", grad_five, end_bit), send("grad_four", grad_four, end_bit)
    deep = shared_rows(experts) // 2
    dgate, keep, give = call(
        "gate_back",
        functools.partial(gate_back_kernel, masks, 512),
        [ints, x, dmix, centre, prob, tower_sums] + [kept[2] for kept in saved],
        [((2 * experts, 2 * rows), BF16, True)] + [((deep, 512), F32, True)] * 2,
        pin,
        1,
        [pltpu.VMEM((2 * experts, 2 * rows), F32), pltpu.VMEM((2 * deep, 512), F32)],
        1,
        after=[ones[5]],
    )
    (keep,) = add([keep, swap("give", give)], [F32])
    grad_two, grad_three, ones[2], ones[3] = back(2, 3, (six, seven), BF16, 1, [keep])
    three, two = send("grad_three", grad_three, mid_bit), send("grad_two", grad_two, mid_bit)
    stages = []
    for b in (bits - 1, *range(2, bits - 1)):
        (keep,) = add([keep, send(f"shared_{b}", keep, (b, b))], [F32], [ones[3]])
        stages.append(keep)

    grad_zero, grad_one, ones[0], ones[1] = back(0, 1, (four, five), F32, 1, [ones[3], stages[0]])
    def input_gradient(side, dtype, after=()):
        (out,) = call(
            f"input_{side}",
            functools.partial(input_kernel, side, 512),
            [dgate, gate_rows, *ones, *pays],
            [((rows, 512), dtype, True)],
            pin,
            3.5 * depth,
            after=after,
        )
        return out

    over = input_gradient(1, BF16, [stages[1]])
    own = input_gradient(0, F32)
    top = bits - 1
    (one,) = add([grad_one, three], [BF16], [over])
    if extra:
        (zero,) = add([grad_zero, two, send("near", one, near_bit)], [F32])
        for at in reversed(extra):
            count = zero.shape[0] // 2
            zero = zero[:count] + send("extra", zero[count:].astype(BF16), at).astype(F32)
        low_zero = zero.astype(BF16)
        pieces = []
    else:
        pieces = [send("near", one, near_bit, True), send("cross", one, (top, top), False, 1 << near_bit[0])]
        zero, low_zero = add([grad_zero, two], [F32, BF16])
    pieces = [zero, *pieces, send("far", low_zero, (top, top), False)]
    (keep,) = add([keep, send("shared_1", keep, (1, 1))], [F32], [low_zero, own])
    (keep,) = add([keep, send("shared_0", keep, (0, 0))], [F32])
    give = swap("keep", keep)
    grad_gate, grad_gate_bias, tower_first, tower_bias, last, out_bias, done = call(
        "close",
        functools.partial(close_kernel, experts),
        [ints, keep, give],
        [
            ((2, experts, 512), F32, False),
            ((2, experts), F32, False),
            ((2, 64, 128), F32, False),
            ((2, 64), F32, False),
            ((2, 64), F32, False),
            ((1, 2), F32, False),
            ((8, 128), F32, True),
        ],
        pin,
        1,
        [pltpu.VMEM((2 * deep, 512), F32)],
        1,
    )
    (final,) = add(pieces, [F32], [done, own])

    input_grad, summed = call(
        "input_sum",
        input_sum_kernel,
        [own, swap("over", over)],
        [((rows, 512), F32, False), ((8, 128), F32, True)],
        pin,
        1.5,
        after=[final],
    )
    grad_w_first, grad_b_first, grad_w_second, grad_b_second = call(
        "finish",
        finish_kernel,
        [ints, final, swap("final", final)],
        [
            ((1, 512, 256), F32, False),
            ((1, 256), F32, False),
            ((1, 256, 128), F32, False),
            ((1, 128), F32, False),
        ],
        pin,
        TAIL,
        scalars=1,
        after=[summed],
    )
    return (
        predictions,
        input_grad,
        grad_w_first,
        grad_b_first,
        grad_w_second,
        grad_b_second,
        jnp.transpose(grad_gate, (0, 2, 1)),
        grad_gate_bias,
        jnp.transpose(tower_first, (0, 2, 1)),
        tower_bias,
        last,
        out_bias[0],
    )


def solution(mesh):
    in_specs = (
        P(("dp", "expert"), None),
        P("expert", None, None),
        P("expert", None),
        P("expert", None, None),
        P("expert", None),
        P(),
        P(),
        P(),
        P(),
        P(),
        P(),
        P(None, ("dp", "expert")),
        P(),
        P(),
    )
    out_specs = (
        P(None, ("dp", "expert")),
        P(("dp", "expert"), None),
        P("expert", None, None),
        P("expert", None),
        P("expert", None, None),
        P("expert", None),
        P(),
        P(),
        P(),
        P(),
        P(),
        P(),
    )
    return jax.shard_map(
        per_device, mesh=mesh, in_specs=in_specs, out_specs=out_specs, check_vma=False
    )
```

```python
import functools

import jax
import jax.numpy as jnp
from jax import lax
from jax.experimental import pallas as pl
from jax.experimental.pallas import tpu as pltpu
from jax.sharding import PartitionSpec as P

F32 = jnp.float32
BF16 = jnp.bfloat16
ROOT = 0.7978845608028654
CUBE = 0.044715
NN = (((1,), (0,)), ((), ()))
NT = (((1,), (1,)), ((), ()))
TN = (((0,), (0,)), ((), ()))
TT = (((0,), (1,)), ((), ()))
BIAS_ROWS = 16
SCALE = 3e8
EARLY = 6
BACK_CHUNK = 2048
TAIL = 10
GROUPS = ((0,), (1, 4), (2,), (3, 5), (6, 7))
LAST_ASK = 2
PAY_ROWS = 320 + BIAS_ROWS
VMEM = pl.BlockSpec(memory_space=pltpu.VMEM)
SMEM = pl.BlockSpec(memory_space=pltpu.SMEM)
ANY = pl.BlockSpec(memory_space=pl.ANY)


def dot(a, b, dims):
    return lax.dot_general(a, b, dims, preferred_element_type=F32)


def gelu_pair(v):
    square = v * v
    upper = 0.5 + 0.5 * jnp.tanh(v * (ROOT + (ROOT * CUBE) * square))
    value = v * upper
    slope = upper + value * (1.0 - upper) * (2.0 * ROOT + (6.0 * ROOT * CUBE) * square)
    return value, slope


def call(name, kernel, ins, outs, pin, micros, scratch=(), scalars=0, limit=8, after=(), alias=()):
    limit = limit if pin is not None else 60
    pinned = lambda a: pltpu.with_memory_space_constraint(a, pltpu.VMEM) if pin else a
    args = [a if n < scalars else pinned(a) for n, a in enumerate(ins)] + [pinned(a) for a in alias] + list(after)
    count, skip = len(ins), len(alias) + len(after)
    body = kernel
    if skip:

        def body(*refs):
            return kernel(*refs[:count], *refs[count + skip :])

    kept = pltpu.VMEM if pin else jax.ShapeDtypeStruct
    shapes = [(kept if stay else jax.ShapeDtypeStruct)(shape, dtype) for shape, dtype, stay in outs]
    return pl.pallas_call(
        body,
        name=name,
        in_specs=[SMEM] * scalars + [VMEM] * (count - scalars + len(alias)) + [ANY] * len(after),
        input_output_aliases={count + n: n for n in range(len(alias))},
        out_specs=[VMEM] * len(outs),
        out_shape=shapes,
        scratch_shapes=list(scratch),
        compiler_params=pltpu.CompilerParams(vmem_limit_bytes=limit * 2**20),
        cost_estimate=pl.CostEstimate(flops=int(micros * SCALE), bytes_accessed=0, transcendentals=0),
    )(*args)


def hold(value, after):
    count = len(after)
    return pl.pallas_call(
        lambda *refs: None,
        name="hold",
        in_specs=[ANY] * (1 + count),
        out_specs=ANY,
        out_shape=jax.ShapeDtypeStruct(value.shape, value.dtype),
        input_output_aliases={0: 0},
        compiler_params=pltpu.CompilerParams(vmem_limit_bytes=2**20),
        cost_estimate=pl.CostEstimate(flops=0, bytes_accessed=0, transcendentals=0),
    )(value, *after)


def slot_of(masks, int_ref, j):
    half = len(masks[0])
    mask = jnp.where(int_ref[0] == 0, masks[0][j], masks[1][j])
    return int_ref[0] * half + ((int_ref[1] & (half - 1)) ^ mask)


def to_column(row):
    n = row.shape[1]
    same = lax.broadcasted_iota(jnp.int32, (n, n), 0) == lax.broadcasted_iota(jnp.int32, (n, n), 1)
    return jnp.sum(jnp.where(same, jnp.broadcast_to(row, (n, n)), 0.0), axis=1, keepdims=True)


def side_by_side(columns, tall):
    lane = lax.broadcasted_iota(jnp.int32, (tall, 128), 1)
    small = jnp.zeros((tall, 128), F32)
    for n, col in enumerate(columns):
        small = jnp.where(lane == n, jnp.broadcast_to(col, (tall, 128)), small)
    return small


def fold(ref, base, block):
    deep = block.shape[0] // 4
    for k in range(4):
        ref[base : base + deep, 128 * k : 128 * (k + 1)] = block[deep * k : deep * (k + 1)]


def unfold(ref, base, deep):
    return jnp.concatenate(
        [ref[base : base + deep, 128 * k : 128 * (k + 1)] for k in range(4)], axis=0
    )


def pack_kernel(w1_ref, w2_ref, b1_ref, b2_ref, pay_ref, w1, w2, b1, b2, sems):
    copies = [
        pltpu.make_async_copy(src, dst, sems.at[n])
        for n, (src, dst) in enumerate(((w1_ref, w1), (w2_ref, w2), (b1_ref, b1), (b2_ref, b2)))
    ]
    for copy in copies:
        copy.start()
    for copy in copies[1:]:
        copy.wait()
    second = w2[0].astype(F32).T.astype(BF16)
    pay_ref[0, 256:320, :256] = second[:64]
    pay_ref[0, 256:320, 256:] = second[64:]
    row = jnp.concatenate([b1[...].astype(F32), b2[...].astype(F32), jnp.zeros((1, 128), F32)], axis=1)
    pay_ref[0, 320:, :] = jnp.broadcast_to(row, (BIAS_ROWS, 512)).astype(BF16)
    copies[0].wait()
    pay_ref[0, :256, :] = w1[0].astype(F32).T.astype(BF16)


def pack(w1, w2, b1, b2):
    arrays = (w1, w2, b1, b2)
    return pl.pallas_call(
        pack_kernel,
        name="pack",
        in_specs=[pl.BlockSpec(memory_space=pltpu.HBM)] * 4,
        out_specs=VMEM,
        out_shape=jax.ShapeDtypeStruct((1, PAY_ROWS, 512), BF16),
        scratch_shapes=[pltpu.VMEM(a.shape, a.dtype) for a in arrays] + [pltpu.SemaphoreType.DMA((4,))],
        compiler_params=pltpu.CompilerParams(vmem_limit_bytes=8 * 2**20),
        cost_estimate=pl.CostEstimate(flops=0, bytes_accessed=0, transcendentals=0),
    )(*[pltpu.with_memory_space_constraint(a, pltpu.HBM) for a in arrays])


def biases(pay):
    flipped = pay[320:, :].astype(F32).T
    return flipped[:256, 0:1], flipped[256:384, 0:1]


def second_weight(pay):
    return jnp.concatenate([pay[256:320, :256], pay[256:320, 256:]], axis=0)


def gate_kernel(masks, groups, int_ref, label_ref, there_ref, gw_ref, gb_ref, mine_ref, other_ref, *refs):
    prob_ref, low_ref, weight_ref, x_out, label_out, scratch, sems = refs
    rows = mine_ref.shape[0]
    experts = 2 * len(masks[0])
    copies = [
        pltpu.make_async_copy(src, x_out.at[pl.ds(n * rows, rows), :], sems.at[n])
        for n, src in enumerate((mine_ref, other_ref))
    ]
    for copy in copies:
        copy.start()
    for side in range(2):
        at = slice(side * rows, (side + 1) * rows)
        label_out[:, at] = (label_ref, there_ref)[side][...].astype(F32)
        copies[side].wait()
        for t in range(2):
            part = dot(gw_ref[t], x_out[at, :], NT) + to_column(gb_ref[t : t + 1, :].astype(F32))
            top = jnp.max(part, axis=0, keepdims=True)
            e = jnp.exp(part - top)
            scratch[t * experts : (t + 1) * experts, at] = e / jnp.sum(e, axis=0, keepdims=True)
        shard = int_ref[0] if side == 0 else 1 - int_ref[0]
        index = int_ref[1] * rows + lax.broadcasted_iota(jnp.int32, (1, rows), 1)
        start = jnp.int32(0)
        weight = jnp.zeros((1, rows), F32)
        for g in range(groups):
            length = int_ref[3 + groups + g]
            size = jnp.where(int_ref[3 + g] == shard, length, 0)
            inside = (index >= start) & (index < start + size)
            recip = 1.0 / jnp.full((1, rows), length, jnp.int32).astype(F32)
            weight = weight + jnp.where(inside, recip, 0.0)
            start = start + size
        weight_ref[:, at] = weight
    for j in range(experts // 2):
        slot = slot_of(masks, int_ref, j)
        for t in range(2):
            row = scratch[pl.ds(t * experts + slot, 1), :]
            prob_ref[j, t : t + 1, :] = row
            low_ref[j, t : t + 1, :] = row.astype(BF16).astype(F32)


def forward_kernel(bundles, first, block, chunk, span, x_ref, low_ref, *refs):
    count = len(bundles)
    pays, refs = refs[:count], refs[count:]
    if not first:
        mix_in, *refs = refs
    kept, mix_ref = [refs[4 * n : 4 * n + 4] for n in range(count)], refs[4 * count]
    depth = pays[0].shape[0]
    weights = {}
    for k in range(depth):
        for n, pay_ref in enumerate(pays):
            pay = pay_ref[k]
            weights[k, n] = (pay[:256], second_weight(pay), *biases(pay))
    out_from = 0 if mix_ref.shape[2] == x_ref.shape[0] else span[0]
    work = [(c, k, n) for c in range(0, block, chunk) for k in range(depth) for n in range(count)]

    def step(i, _):
        base = pl.multiple_of(i * block, block)
        totals = [None, None]

        def layer_one(c, k, n):
            return dot(weights[k, n][0], x_ref[pl.ds(base + c, chunk), :], NT)

        def after_one(pre, c, k, n):
            value, slope = gelu_pair(pre + weights[k, n][2])
            hidden = value.astype(BF16)
            kept[n][0][k, :, pl.ds(base + c, chunk)] = hidden
            kept[n][1][k, :, pl.ds(base + c, chunk)] = slope.astype(kept[n][1].dtype)
            return hidden

        def after_two(pre, c, k, n):
            at = pl.ds(base + c, chunk)
            value, slope = gelu_pair(pre + weights[k, n][3])
            out = value.astype(BF16)
            kept[n][2][k, :, at] = out
            kept[n][3][k, :, at] = slope.astype(kept[n][3].dtype)
            out = out.astype(F32)
            for t in range(2):
                term = low_ref[bundles[n] * depth + k, t : t + 1, at] * out
                if k == 0 and n == 0:
                    totals[t] = term if first else mix_in[t, :, at] + term
                else:
                    totals[t] = totals[t] + term
                if k == depth - 1 and n == count - 1:
                    mix_ref[t, :, pl.ds(base + c - out_from, chunk)] = totals[t].astype(mix_ref.dtype)

        ones, twos = {0: layer_one(*work[0])}, {}
        for i in range(len(work) + 1):
            if i + 1 < len(work):
                ones[i + 1] = layer_one(*work[i + 1])
            if i < len(work):
                hidden = after_one(ones.pop(i), *work[i])
            if i >= 1:
                after_two(twos.pop(i - 1), *work[i - 1])
            if i < len(work):
                twos[i] = dot(weights[work[i][1:]][1], hidden, NN)
        return 0

    lax.fori_loop(span[0] // block, span[1] // block, step, 0)


def tower_kernel(
    side, chunk, mix_ref, come_ref, label_ref, weight_ref, tob_ref, tw_ref, tb_ref, tl_ref, dmix_ref, centre_ref, *refs
):
    rows = mix_ref.shape[2]
    if side == 0:
        pred_ref, shared_ref, first, sums = refs
        first[...] = jnp.zeros_like(first)
        sums[...] = jnp.zeros_like(sums)
    tb = [to_column(tb_ref[t : t + 1, :].astype(F32)) for t in range(2)]
    tl = [to_column(tl_ref[t : t + 1, :].astype(F32)) for t in range(2)]

    def step(i, _):
        here = pl.ds(pl.multiple_of(i * chunk, chunk), chunk)
        at = pl.ds(pl.multiple_of(side * rows + i * chunk, chunk), chunk)
        cols = []
        for t in range(2):
            mixed = mix_ref[t, :, here].astype(F32) + come_ref[t, :, here].astype(F32)
            low = mixed.astype(BF16)
            act, slope = gelu_pair(dot(tw_ref[t], low, NN) + tb[t])
            score = jnp.sum(act * tl[t], axis=0, keepdims=True) + tob_ref[0:1, t : t + 1].astype(F32)
            pred = 1.0 / (1.0 + jnp.exp(-score))
            d_score = weight_ref[:, at] * (pred - label_ref[t : t + 1, at])
            d_low = (d_score * tl[t] * slope).astype(BF16)
            d_mixed = dot(tw_ref[t], d_low, TN)
            dmix_ref[t, :, at] = d_mixed
            centre_ref[t : t + 1, at] = jnp.sum(d_mixed * mixed, axis=0, keepdims=True)
            if side == 0:
                pred_ref[t : t + 1, here] = pred
                first[t] += dot(d_low, low, NT)
                cols.append(jnp.sum(act * d_score, axis=1, keepdims=True))
                cols.append(jnp.sum(d_low.astype(F32), axis=1, keepdims=True))
                total = jnp.sum(d_score, axis=1, keepdims=True)
                cols.append(jnp.broadcast_to(total, (64, 1)))
        if side == 0:
            sums[...] += side_by_side([cols[3 * t + n] for n in range(3) for t in range(2)], 64)
        return 0

    lax.fori_loop(0, rows // chunk, step, 0)
    if side == 0:
        for t in range(2):
            fold(shared_ref, 16 * t, first[t])
        fold(shared_ref, 32, sums[...])


def tower_whole_kernel(chunk, mix_ref, come_ref, mix_there, come_there, *refs):
    ins, (dmix_ref, centre_ref, pred_ref, shared_ref, first, sums) = refs[:6], refs[6:]
    tower_kernel(0, chunk, mix_ref, come_ref, *ins, dmix_ref, centre_ref, pred_ref, shared_ref, first, sums)
    tower_kernel(1, chunk, mix_there, come_there, *ins, dmix_ref, centre_ref)


def shared_rows(experts):
    return -(-(48 + 2 * experts + experts // 2) // 16) * 16


def gate_back_kernel(masks, chunk, spot_ref, x_ref, dmix_ref, centre_ref, prob_ref, tower_ref, *refs):
    outs = refs[:8]
    dgate_ref, keep_ref, give_ref, gates, shared_ref = refs[8:]
    depth = outs[0].shape[0]
    experts = 2 * len(masks[0])
    gates[...] = jnp.zeros_like(gates)

    def step(i, _):
        at = pl.ds(pl.multiple_of(i * chunk, chunk), chunk)
        for j in range(8 * depth):
            out = outs[j // depth][j % depth, :, at].astype(F32)
            slot = slot_of(masks, spot_ref, j)
            for t in range(2):
                d_prob = jnp.sum(dmix_ref[t, :, at] * out, axis=0, keepdims=True)
                d_gate = prob_ref[j, t : t + 1, at] * (d_prob - centre_ref[t : t + 1, at])
                gates[pl.ds(t * experts + slot, 1), at] = d_gate
        return 0

    lax.fori_loop(0, x_ref.shape[0] // chunk, step, 0)
    low = gates[...].astype(BF16)
    dgate_ref[...] = low
    shared_ref[...] = jnp.zeros_like(shared_ref)
    shared_ref[:48, :] = tower_ref[...]
    shared_ref[48 : 48 + 2 * experts, :] = dot(low, x_ref[...], NN)
    bias = jnp.sum(low.astype(F32), axis=1, keepdims=True)
    fold(shared_ref, 48 + 2 * experts, side_by_side([bias], 2 * experts))
    deep = keep_ref.shape[0]
    keep_ref[...] = shared_ref[pl.ds(pl.multiple_of(spot_ref[0] * deep, 8), deep), :]
    give_ref[...] = shared_ref[pl.ds(pl.multiple_of((1 - spot_ref[0]) * deep, 8), deep), :]


def backward_kernel(bundles, add, block, x_ref, low_ref, dmix_ref, *refs):
    count = len(bundles)
    pays, refs = refs[:count], refs[count:]
    kept, refs = [refs[3 * n : 3 * n + 3] for n in range(count)], refs[3 * count :]
    if add:
        come, refs = refs[:count], refs[count:]
    grads, dones, d_two, sums = refs[:count], refs[count : 2 * count], refs[-2], refs[-1]
    depth = pays[0].shape[0]
    for k in range(depth):
        weights = [second_weight(pay[k]) for pay in pays]
        sums[...] = jnp.zeros_like(sums)

        def step(i, _, k=k, weights=weights):
            at = pl.ds(pl.multiple_of(i * block, block), block)
            for n in range(count):
                _, g1_ref, g2_ref = kept[n]
                j = bundles[n] * depth + k
                d_out = low_ref[j, 0:1, at] * dmix_ref[0, :, at] + low_ref[j, 1:2, at] * dmix_ref[1, :, at]
                two = d_out.astype(BF16).astype(F32) * g2_ref[k, :, at].astype(F32)
                two_low = two.astype(BF16)
                d_two[n, :, at] = two_low
                one = dot(weights[n], two_low, TN) * g1_ref[k, :, at].astype(F32)
                dones[n][k, :, at] = one.astype(BF16)
                add_one, add_two = one[:, :128], two[:, :128]
                for m in range(128, block, 128):
                    add_one = add_one + one[:, m : m + 128]
                    add_two = add_two + two[:, m : m + 128]
                sums[n, :256] += add_one
                sums[n, 256:] += add_two
            return 0

        lax.fori_loop(0, x_ref.shape[0] // block, step, 0)
        for n in range(count):
            h_ref = kept[n][0]
            first = dot(dones[n][k], x_ref[...], NN)
            second = dot(d_two[n], h_ref[k], NT)
            second = jnp.concatenate([second[:64], second[64:]], axis=1)
            row = jnp.concatenate(
                [
                    jnp.sum(sums[n].T, axis=0, keepdims=True),
                    jnp.zeros((1, 128), F32),
                ],
                axis=1,
            )
            high = row.astype(BF16).astype(F32)
            index = lax.broadcasted_iota(jnp.int32, (BIAS_ROWS, 512), 0)
            both = jnp.where(index == 0, high, jnp.where(index == 1, row - high, 0.0))
            if add:
                first = first + come[n][k, :256, :].astype(F32)
                second = second + come[n][k, 256:320, :].astype(F32)
                both = both + come[n][k, 320:, :].astype(F32)
            grads[n][k, :256, :] = first.astype(grads[n].dtype)
            grads[n][k, 256:320, :] = second.astype(grads[n].dtype)
            grads[n][k, 320:, :] = both.astype(grads[n].dtype)


def input_kernel(side, chunk, dgate_ref, gw_ref, *refs):
    experts = gw_ref.shape[1]
    ones, pays, out_ref = refs[:8], refs[8:16], refs[16]
    rows = out_ref.shape[0]

    def step(i, _):
        at = pl.ds(pl.multiple_of(side * rows + i * chunk, chunk), chunk)
        total = dot(dgate_ref[:experts, at], gw_ref[0], TN) + dot(dgate_ref[experts:, at], gw_ref[1], TN)
        for one, pay in zip(ones, pays):
            for k in range(one.shape[0]):
                total = total + dot(one[k, :, at], pay[k, :256, :], TN)
        out_ref[pl.ds(pl.multiple_of(i * chunk, chunk), chunk), :] = total.astype(out_ref.dtype)
        return 0

    lax.fori_loop(0, rows // chunk, step, 0)


def add_kernel(count, *refs):
    total = refs[0][...].astype(F32)
    for ref in refs[1:count]:
        total = total + ref[...].astype(F32)
    for ref in refs[count:]:
        ref[...] = total.astype(ref.dtype)


def input_sum_kernel(own_ref, come_ref, out_ref, done_ref):
    out_ref[...] = own_ref[...] + come_ref[...].astype(F32)
    done_ref[...] = jnp.zeros_like(done_ref)


def finish_kernel(owner_ref, mine_ref, come_ref, w1_ref, b1_ref, w2_ref, b2_ref):
    owner = owner_ref[2] == 1
    mine_ref, come_ref = mine_ref.at[0], come_ref.at[0]
    w1_ref[0] = jnp.where(owner, mine_ref[:256, :], come_ref[:256, :]).T
    second = jnp.where(owner, mine_ref[256:320, :], come_ref[256:320, :])
    w2_ref[0] = jnp.concatenate([second[:, :256], second[:, 256:]], axis=0).T
    bias = jnp.where(owner, mine_ref[320:328, :], come_ref[320:328, :])
    bias = bias[0:1] + bias[1:2]
    b1_ref[...] = bias[:, :256]
    b2_ref[...] = bias[:, 256:384]


def close_kernel(
    experts, spot_ref, keep_ref, give_ref,
    gate_ref, gate_bias_ref, first_ref, tb_ref, tl_ref, tob_ref, done_ref, shared_ref,
):

    base = 48 + 2 * experts
    deep = keep_ref.shape[0]
    shared_ref[pl.ds(pl.multiple_of(spot_ref[0] * deep, 8), deep), :] = keep_ref[...]
    shared_ref[pl.ds(pl.multiple_of((1 - spot_ref[0]) * deep, 8), deep), :] = give_ref[...]
    for t in range(2):
        gate_ref[t] = shared_ref[48 + t * experts : 48 + (t + 1) * experts, :]
        first_ref[t] = unfold(shared_ref, 16 * t, 16)
    small = unfold(shared_ref, 32, 16).T
    tl_ref[...] = small[0:2, :]
    tb_ref[...] = small[2:4, :]
    tob_ref[:, 0:1] = small[4:5, 0:1]
    tob_ref[:, 1:2] = small[5:6, 0:1]
    bias = unfold(shared_ref, base, experts // 2).T
    gate_bias_ref[0:1, :] = bias[0:1, :experts]
    gate_bias_ref[1:2, :] = bias[0:1, experts:]
    done_ref[...] = jnp.zeros_like(done_ref)


def per_device(
    inputs,
    w_first,
    b_first,
    w_second,
    b_second,
    gate_weight,
    gate_bias,
    tower_first_weight,
    tower_first_bias,
    tower_last,
    tower_out_bias,
    labels,
    group_len,
    group_shard,
):
    rows = inputs.shape[0]
    experts = lax.axis_size("expert")
    half = experts // 2
    bits = experts.bit_length() - 1
    depth = half // 8
    pin = True if depth == 1 else None
    chunk = 256 if pin else 512
    core = lax.axis_index("dp")
    place = lax.axis_index("expert")
    owner = core == place // half
    near_bit, mid_bit, end_bit = (2, 2), (1, 0), (0, 1)
    extra = [(b, b) for b in range(bits - 2, 2, -1)]

    def pairs(bit_of_core, want=None, also=0):
        return [
            (c * experts + q, c * experts + (q ^ (1 << bit_of_core[c]) ^ also))
            for c in range(2)
            for q in range(experts)
            if want is None or (c == q // half) == want
        ]

    def send(name, value, bit_of_core, want=None, also=0):
        with jax.named_scope(name):
            return lax.ppermute(value, ("dp", "expert"), pairs(bit_of_core, want, also))

    def swap(name, value):
        with jax.named_scope(name):
            return lax.ppermute(value, "dp", [(0, 1), (1, 0)])

    def deal(value):
        route = []
        for c in range(2):
            for q in range(experts):
                target = c * experts + (q ^ half) if c == q // half else (1 - c) * experts + q
                route.append((c * experts + q, target))
        with jax.named_scope("deal"):
            return lax.ppermute(value, ("dp", "expert"), route)

    def expert_mask(c, j):
        bundle, inner = j // depth, j % depth
        found = sum(1 << extra[e][c] for e in range(len(extra)) if (inner >> e) & 1)
        for n, at in enumerate((near_bit, mid_bit, end_bit)):
            found |= ((bundle >> n) & 1) << at[c]
        return found

    masks = [[expert_mask(c, j) for j in range(half)] for c in range(2)]
    spot = jnp.stack([core, place, owner.astype(jnp.int32)]).astype(jnp.int32)

    def add(values, dtypes, after=()):
        shape = values[0].shape
        outs = [(shape, dtype, True) for dtype in dtypes]
        return call("add", functools.partial(add_kernel, len(values)), values, outs, pin, 0, after=after)

    pay = pack(w_first, w_second, b_first, b_second)
    zero = deal(pay)
    if not extra:
        owners_near = send("owners_near", pay, near_bit, True)
    for at in extra:
        zero = jnp.concatenate([zero, send("pay_extra", zero, at)], axis=0)
    labels_there = swap("labels", labels)
    inputs_there = swap("inputs", inputs)
    gate_rows = jnp.transpose(gate_weight, (0, 2, 1))
    ints = jnp.concatenate([spot, group_shard, group_len])
    outs = [((half, 2, 2 * rows), F32)] * 2 + [((1, 2 * rows), F32), ((2 * rows, 512), BF16), ((2, 2 * rows), F32)]
    kept = pltpu.VMEM if pin else jax.ShapeDtypeStruct
    prob, low, weights, x, both_labels = pl.pallas_call(
        functools.partial(gate_kernel, masks, group_len.shape[0]),
        name="gate",
        in_specs=[SMEM] + [VMEM] * 4 + [ANY] * 2,
        out_specs=[VMEM] * 5,
        out_shape=[kept(shape, dtype) for shape, dtype in outs],
        scratch_shapes=[pltpu.VMEM((2 * experts, 2 * rows), F32), pltpu.SemaphoreType.DMA((2,))],
        compiler_params=pltpu.CompilerParams(vmem_limit_bytes=(8 if pin else 60) * 2**20),
        cost_estimate=pl.CostEstimate(flops=0, bytes_accessed=0, transcendentals=0),
    )(ints, labels, labels_there, gate_rows, gate_bias, inputs, inputs_there)

    pays = [hold(zero, [low])] + [None] * 7
    pays[1] = send("pay_1", pays[0], near_bit, None if extra else False)
    pays[2] = send("pay_2", pays[0], mid_bit)
    pays[4] = send("pay_4", pays[0], end_bit)
    mixed = None
    saved = [None] * 8
    slope_type = F32 if pin else BF16
    for group in GROUPS:
        shape = lambda deep, dtype: ((depth, deep, 2 * rows), dtype, True)
        name = "forward_" + "".join(str(n) for n in group)
        ins = [x, low] + [pays[n] for n in group] + ([] if mixed is None else [mixed])
        kernel = functools.partial(forward_kernel, group, mixed is None, 4 * chunk, chunk)
        outs = [shape(256, BF16), shape(256, BF16), shape(128, BF16), shape(128, slope_type)] * len(group)
        cost = 2.25 * len(group) * depth
        if group != GROUPS[-1]:
            outs.append(((2, 128, 2 * rows), F32, True))
            *kept, mixed = call(name, functools.partial(kernel, (0, 2 * rows)), ins, outs, pin, cost)
        elif extra:
            outs.append(((2, 128, 2 * rows), BF16, True))
            *kept, mixed = call(name, functools.partial(kernel, (0, 2 * rows)), ins, outs, pin, cost)
            mixed_own, mixed_other = mixed[:, :, :rows], mixed[:, :, rows:]
        else:
            outs.append(((2, 128, rows), BF16, True))
            *kept, mixed_other = call(
                name + "_other", functools.partial(kernel, (rows, 2 * rows)), ins, outs, pin, cost / 2
            )
            *kept, mixed_own = call(
                name + "_own", functools.partial(kernel, (0, rows)), ins, outs, pin, cost / 2, alias=kept
            )
        for n, bundle in enumerate(group):
            saved[bundle] = kept[4 * n : 4 * n + 4]
        if group == GROUPS[0]:
            if extra:
                held = hold(pays[1], [pays[2], pays[4], mixed])
            else:
                pays[2] = hold(pays[2], [pays[4], owners_near, mixed])
                (pays[1],) = add([owners_near, pays[1]], [BF16], [pays[2]])
                held = pays[1]
            pays[3] = send("pay_3", held, mid_bit)
            pays[5] = send("pay_5", held, end_bit)
            pays[6] = send("pay_6", pays[2], end_bit)
        if group == GROUPS[LAST_ASK]:
            pays[7] = send("pay_7", hold(pays[3], [mixed]), end_bit)

    tower_ins = [both_labels, weights, tower_out_bias[None], jnp.transpose(tower_first_weight, (0, 2, 1))]
    tower_ins += [tower_first_bias, tower_last]
    tower_outs = [((2, 128, 2 * rows), F32, True), ((2, 2 * rows), F32, True)]
    own_outs = tower_outs + [((2, rows), F32, False), ((48, 512), F32, True)]
    scratch = [pltpu.VMEM((2, 64, 128), F32), pltpu.VMEM((64, 128), F32)]
    come_own, come_other = swap("mixed_other", mixed_other), swap("mixed_own", mixed_own)
    if extra:
        ins = [mixed_own, come_own, mixed_other, come_other, *tower_ins]
        kernel = functools.partial(tower_whole_kernel, 512)
        dmix, centre, predictions, tower_sums = call("tower", kernel, ins, own_outs, pin, 4, scratch)
    else:
        ins = [mixed_own, come_own, *tower_ins]
        kernel = functools.partial(tower_kernel, 0, 512)
        *begun, predictions, tower_sums = call("tower_own", kernel, ins, own_outs, pin, 2, scratch)
        ins = [mixed_other, come_other, *tower_ins]
        kernel = functools.partial(tower_kernel, 1, 512)
        dmix, centre = call("tower_other", kernel, ins, tower_outs, pin, 2, alias=begun)

    def back(bundles, come, dtype, cost, after=()):
        grad = ((depth, PAY_ROWS, 512), dtype, False)
        done = ((depth, 256, 2 * rows), BF16, True)
        return call(
            "backward_" + "".join(str(n) for n in bundles),
            functools.partial(backward_kernel, bundles, come is not None, BACK_CHUNK),
            [x, low, dmix]
            + [pays[n] for n in bundles]
            + [saved[n][m] for n in bundles for m in (0, 1, 3)]
            + list(come or ()),
            [grad] * len(bundles) + [done] * len(bundles),
            pin,
            cost,
            [pltpu.VMEM((2, 128, 2 * rows), BF16), pltpu.VMEM((2, 384, 128), F32)],
            after=after,
        )

    ones = [None] * 8
    grad_seven, ones[7] = back((7,), None, BF16, 2)
    grad_six, ones[6] = back((6,), None, BF16, 2, [ones[7]])
    six, seven = send("grad_six", grad_six, end_bit), send("grad_seven", grad_seven, end_bit)
    grad_four, grad_five, ones[4], ones[5] = back((4, 5), None, BF16, 1, [ones[6]])
    five, four = send("grad_five", grad_five, end_bit), send("grad_four", grad_four, end_bit)
    deep = shared_rows(experts) // 2
    dgate, keep, give = call(
        "gate_back",
        functools.partial(gate_back_kernel, masks, 512),
        [ints, x, dmix, centre, prob, tower_sums] + [kept[2] for kept in saved],
        [((2 * experts, 2 * rows), BF16, True)] + [((deep, 512), F32, True)] * 2,
        pin,
        1,
        [pltpu.VMEM((2 * experts, 2 * rows), F32), pltpu.VMEM((2 * deep, 512), F32)],
        1,
        after=[ones[5]],
    )
    (keep,) = add([keep, swap("give", give)], [F32])
    grad_two, grad_three, ones[2], ones[3] = back((2, 3), (six, seven), BF16, 1, [keep])
    three, two = send("grad_three", grad_three, mid_bit), send("grad_two", grad_two, mid_bit)
    stages = []
    for b in (bits - 1, *range(2, bits - 1)):
        (keep,) = add([keep, send(f"shared_{b}", keep, (b, b))], [F32], [ones[3]])
        stages.append(keep)

    grad_zero, grad_one, ones[0], ones[1] = back((0, 1), (four, five), F32, 1, [ones[3], stages[0]])
    def input_gradient(side, dtype, after=()):
        (out,) = call(
            f"input_{side}",
            functools.partial(input_kernel, side, 512),
            [dgate, gate_rows, *ones, *pays],
            [((rows, 512), dtype, True)],
            pin,
            3.5 * depth,
            after=after,
        )
        return out

    over = input_gradient(1, BF16, [stages[1]])
    own = input_gradient(0, F32)
    top = bits - 1
    (one,) = add([grad_one, three], [BF16], [over])
    if extra:
        (zero,) = add([grad_zero, two, send("near", one, near_bit)], [F32])
        for at in reversed(extra):
            count = zero.shape[0] // 2
            zero = zero[:count] + send("extra", zero[count:].astype(BF16), at).astype(F32)
        low_zero = zero.astype(BF16)
        pieces = []
    else:
        pieces = [send("near", one, near_bit, True), send("cross", one, (top, top), False, 1 << near_bit[0])]
        zero, low_zero = add([grad_zero, two], [F32, BF16])
    pieces = [zero, *pieces, send("far", low_zero, (top, top), False)]
    (keep,) = add([keep, send("shared_1", keep, (1, 1))], [F32], [low_zero, own])
    (keep,) = add([keep, send("shared_0", keep, (0, 0))], [F32])
    give = swap("keep", keep)
    grad_gate, grad_gate_bias, tower_first, tower_bias, last, out_bias, done = call(
        "close",
        functools.partial(close_kernel, experts),
        [ints, keep, give],
        [
            ((2, experts, 512), F32, False),
            ((2, experts), F32, False),
            ((2, 64, 128), F32, False),
            ((2, 64), F32, False),
            ((2, 64), F32, False),
            ((1, 2), F32, False),
            ((8, 128), F32, True),
        ],
        pin,
        1,
        [pltpu.VMEM((2 * deep, 512), F32)],
        1,
    )
    (final,) = add(pieces, [F32], [done, own])

    input_grad, summed = call(
        "input_sum",
        input_sum_kernel,
        [own, swap("over", over)],
        [((rows, 512), F32, False), ((8, 128), F32, True)],
        pin,
        1.5,
        after=[final],
    )
    grad_w_first, grad_b_first, grad_w_second, grad_b_second = call(
        "finish",
        finish_kernel,
        [ints, final, swap("final", final)],
        [
            ((1, 512, 256), F32, False),
            ((1, 256), F32, False),
            ((1, 256, 128), F32, False),
            ((1, 128), F32, False),
        ],
        pin,
        TAIL,
        scalars=1,
        after=[summed],
    )
    return (
        predictions,
        input_grad,
        grad_w_first,
        grad_b_first,
        grad_w_second,
        grad_b_second,
        jnp.transpose(grad_gate, (0, 2, 1)),
        grad_gate_bias,
        jnp.transpose(tower_first, (0, 2, 1)),
        tower_bias,
        last,
        out_bias[0],
    )


def solution(mesh):
    in_specs = (
        P(("dp", "expert"), None),
        P("expert", None, None),
        P("expert", None),
        P("expert", None, None),
        P("expert", None),
        P(),
        P(),
        P(),
        P(),
        P(),
        P(),
        P(None, ("dp", "expert")),
        P(),
        P(),
    )
    out_specs = (
        P(None, ("dp", "expert")),
        P(("dp", "expert"), None),
        P("expert", None, None),
        P("expert", None),
        P("expert", None, None),
        P("expert", None),
        P(),
        P(),
        P(),
        P(),
        P(),
        P(),
    )
    return jax.shard_map(
        per_device, mesh=mesh, in_specs=in_specs, out_specs=out_specs, check_vma=False
    )
```
